128 devices in a mesh: ta: 8 (over y_lo, x), xyz: 16 (over y_hi, z, core).
Axes of the slice: x: 4, y: 4 (y_hi: 2, y_lo: 2; y = y_hi * 2 + y_lo), z: 4, core: 2. Of those that a mesh axis runs over, the one named last changes fastest.
Arguments:
- source: float32 [2, 4, 3, 32, 64, 128], P(None, None, None, 'ta', 'xyz'), may hold values from -6 to 6
- gauge_links: bfloat16 [4, 2, 3, 3, 32, 64, 128], P(None, None, None, None, 'ta', 'xyz'), may hold values from -2.390625 to 2.390625
- clover_raw: bfloat16 [2, 2, 6, 6, 32, 64, 128], P(None, None, None, None, 'ta', 'xyz'), may hold values from -0.59765625 to 0.59765625
- null_vectors: bfloat16 [16, 2, 4, 3, 32, 64, 128], P(None, None, None, None, 'ta', 'xyz'), may hold values from -0.107910156 to 0.107910156
- coarse_operator: float32 [9, 2, 16, 16384], P(None, None, None, ('ta', 'xyz')), may hold values from -0.19 to 2.71
Outputs:
- solution: float32 [2, 4, 3, 32, 64, 128], P(None, None, None, 'ta', 'xyz')
- coarse_error: float32 [2, 16384], P(None, ('ta', 'xyz'))
The draws below stay inside these ranges and needn't reach their ends.
All inputs are finite; a program needn't handle non-finite values.
Results may differ from the reference program's by a relative error of at most 0.0004.
Values may be sent and summed in bfloat16 or wider, within the bound.
A program may use at most 128 MiB of HBM per device.

```python
import jax
import jax.numpy as jnp
import numpy as np
from jax import lax

LT = 4
LX = 4
LY = 8
LZ = 16
NVEC = 16
MR_STEPS = 2
SAP_CYCLES = 2
GCR_ITERS = 4
NT = 32
NX = 64
AGG_TOTAL = 1024
N_TA = 8
N_XYZ = 16


def draw_coarse_operator(key, part):
    key = jax.random.fold_in(key, 7)
    full_shape = (9, 2, NVEC, AGG_TOTAL * NVEC)
    centre = 2.4
    hopping = 0.1
    centre_spread = 0.1
    hop_spread = 0.06
    noise = jax.random.uniform(key, full_shape, jnp.float32, -1.0, 1.0)
    row_index = lax.broadcasted_iota(jnp.int32, full_shape, 2)
    col_index = lax.broadcasted_iota(jnp.int32, full_shape, 3) % NVEC
    stencil = lax.broadcasted_iota(jnp.int32, full_shape, 0)
    component = lax.broadcasted_iota(jnp.int32, full_shape, 1)
    diagonal = (row_index == col_index) & (component == 0)
    diag_value = jnp.where(stencil == 0, centre, -hopping)
    spread = jnp.where(stencil == 0, centre_spread, hop_spread)
    return spread * noise + jnp.where(diagonal, diag_value, 0.0)


def shard_levels(own_key, extent, pieces, least, top_value):
    loudness = 1.0
    for dim, shards_of in pieces:
        heights = jax.random.uniform(jax.random.fold_in(jax.random.fold_in(own_key, 6), dim), (shards_of,), jnp.float32, least / len(pieces), top_value / len(pieces))
        loudness = loudness * jnp.repeat(jnp.exp(heights), extent[dim] // shards_of).reshape((-1,) + (1,) * (len(extent) - 1 - dim))
    return loudness


def bell_draw(rng, extent, scale, reach, split=(), kind=jnp.bfloat16):
    result = scale * jax.random.normal(rng, extent, jnp.float32)
    if split:
        result = result * shard_levels(rng, extent, split, -0.22, 0.18)
    return jnp.clip(result, -reach, reach).astype(kind)


def setup_inputs(seed: int = 0) -> dict:
    key_list = jax.random.split(jax.random.key(seed), 6)
    return {
        "source": bell_draw(key_list[0], (2, 4, 3, NT, NX, LY * LZ), 1.0, 6.0, ((3, 8), (4, 16)), jnp.float32),
        "gauge_links": bell_draw(key_list[1], (4, 2, 3, 3, NT, NX, LY * LZ), 0.4, 2.390625, ((4, 8), (5, 16))),
        "clover_raw": bell_draw(key_list[2], (2, 2, 6, 6, NT, NX, LY * LZ), 0.1, 0.59765625, ((4, 8), (5, 16))),
        "null_vectors": bell_draw(key_list[3], (NVEC, 2, 4, 3, NT, NX, LY * LZ), 0.018, 0.107910156, ((4, 8), (5, 16))),
        "coarse_operator": draw_coarse_operator(jax.random.fold_in(key_list[5], 71), 0),
    }


mass_shift = 0.2
mean_eps = 1e-06
block_entries = 6144.0
gamma_perm = [[2, 3, 0, 1], [3, 2, 1, 0], [3, 2, 1, 0], [2, 3, 0, 1]]
gamma_real = [[1.0, 1.0, 1.0, 1.0], [0.0, 0.0, 0.0, 0.0], [-1.0, 1.0, 1.0, -1.0], [0.0, 0.0, 0.0, 0.0]]
gamma_imag = [[0.0, 0.0, 0.0, 0.0], [1.0, 1.0, -1.0, -1.0], [0.0, 0.0, 0.0, 0.0], [1.0, -1.0, -1.0, 1.0]]

def gamma_mult(spinor, direction):
    perm_order = gamma_perm[direction]
    real_part = jnp.stack([spinor[0, index] for index in perm_order])
    imag_part = jnp.stack([spinor[1, index] for index in perm_order])
    phase_re = np.array(gamma_real[direction], np.float32).reshape(4, 1, 1, 1, 1)
    phase_im = np.array(gamma_imag[direction], np.float32).reshape(4, 1, 1, 1, 1)
    return jnp.stack([phase_re * real_part - phase_im * imag_part, phase_re * imag_part + phase_im * real_part])

def color_mult(link_field, spinor):
    link_re = link_field[0][None]
    link_im = link_field[1][None]
    spin_re = spinor[0][:, None]
    spin_im = spinor[1][:, None]
    real_part = lax.optimization_barrier(jnp.sum(link_re * spin_re - link_im * spin_im, axis=2))
    imag_part = lax.optimization_barrier(jnp.sum(link_re * spin_im + link_im * spin_re, axis=2))
    return jnp.stack([real_part, imag_part])

def color_mult_dagger(link_field, spinor):
    link_re = jnp.swapaxes(link_field[0], 0, 1)[None]
    link_im = jnp.swapaxes(link_field[1], 0, 1)[None]
    spin_re = spinor[0][:, None]
    spin_im = spinor[1][:, None]
    real_part = lax.optimization_barrier(jnp.sum(link_re * spin_re + link_im * spin_im, axis=2))
    imag_part = lax.optimization_barrier(jnp.sum(link_re * spin_im - link_im * spin_re, axis=2))
    return jnp.stack([real_part, imag_part])

def hermitian(clover_raw):
    raw_values = clover_raw.astype(jnp.float32)
    herm_re = 0.5 * (raw_values[0] + jnp.swapaxes(raw_values[0], 1, 2))
    herm_im = 0.5 * (raw_values[1] - jnp.swapaxes(raw_values[1], 1, 2))
    return (herm_re, herm_im)

def clover_apply(herm_re, herm_im, spinor):
    halves = []
    for chirality in range(2):
        chiral_part = spinor[:, 2 * chirality:2 * chirality + 2]
        part_shape = chiral_part.shape
        chiral_part = chiral_part.reshape((2, 6) + part_shape[3:])
        block_re = herm_re[chirality]
        block_im = herm_im[chirality]
        real_part = lax.optimization_barrier(jnp.sum(block_re * chiral_part[0][None] - block_im * chiral_part[1][None], axis=1))
        imag_part = lax.optimization_barrier(jnp.sum(block_re * chiral_part[1][None] + block_im * chiral_part[0][None], axis=1))
        halves.append(jnp.stack([real_part, imag_part]).reshape(part_shape))
    return jnp.concatenate(halves, axis=1)

def wilson_apply(spinor, ahead_list, behind_list, links_list, back_list, herm_re, herm_im):
    hopping = jnp.zeros_like(spinor)
    for direction in range(4):
        forward_term = color_mult(links_list[direction], ahead_list[direction])
        backward_term = color_mult_dagger(back_list[direction], behind_list[direction])
        hopping = hopping + (forward_term - gamma_mult(forward_term, direction))
        hopping = hopping + (backward_term + gamma_mult(backward_term, direction))
    return (4.0 + mass_shift) * spinor + clover_apply(herm_re, herm_im, spinor) - 0.5 * hopping

def plane_neighbors(spinor, depth, blocked):
    plane_width = spinor.shape[-1]
    position = lax.broadcasted_iota(jnp.int32, (plane_width,), 0)
    z_index = position % depth
    y_index = position // depth
    y_ahead = jnp.roll(spinor, -depth, axis=-1)
    y_behind = jnp.roll(spinor, depth, axis=-1)
    z_ahead = jnp.roll(spinor, -1, axis=-1)
    z_behind = jnp.roll(spinor, 1, axis=-1)
    nothing = jnp.zeros_like(spinor)
    if blocked:
        y_ahead = jnp.where(y_index % 4 == 3, nothing, y_ahead)
        y_behind = jnp.where(y_index % 4 == 0, nothing, y_behind)
        z_ahead = jnp.where(z_index % 4 == 3, nothing, z_ahead)
        z_behind = jnp.where(z_index % 4 == 0, nothing, z_behind)
    else:
        z_ahead = jnp.where(z_index == depth - 1, jnp.roll(spinor, depth - 1, axis=-1), z_ahead)
        z_behind = jnp.where(z_index == 0, jnp.roll(spinor, 1 - depth, axis=-1), z_behind)
    return (y_ahead, y_behind, z_ahead, z_behind)

def block_neighbors(spinor, axis):
    axis_length = spinor.shape[axis]
    position = lax.broadcasted_iota(jnp.int32, (axis_length,) + (1,) * (spinor.ndim - axis - 1), 0) % 4
    nothing = jnp.zeros_like(spinor)
    ahead = jnp.where(position == 3, nothing, jnp.roll(spinor, -1, axis=axis))
    behind = jnp.where(position == 0, nothing, jnp.roll(spinor, 1, axis=axis))
    return (ahead, behind)

def block_sum(values, depth):
    leading = values.shape[:-3]
    t_len, x_len, plane_width = values.shape[-3:]
    row_count = plane_width // depth
    shaped = values.reshape(leading + (t_len // 4, 4, x_len // 4, 4, row_count // 4, 4, depth // 4, 4))
    offset = len(leading)
    return lax.optimization_barrier(jnp.sum(shaped, axis=(offset + 1, offset + 3, offset + 5, offset + 7)))

def block_expand(values):
    leading = values.shape[:-4]
    size_t, size_x, size_y, size_z = values.shape[-4:]
    expanded = values.reshape(leading + (size_t, 1, size_x, 1, size_y, 1, size_z, 1))
    expanded = jnp.broadcast_to(expanded, leading + (size_t, 4, size_x, 4, size_y, 4, size_z, 4))
    return expanded.reshape(leading + (4 * size_t, 4 * size_x, 16 * size_y * size_z))

def block_parity(t_count, x_count, t_start, x_start, rows_y, rows_z):
    shape = (t_count, x_count, rows_y, rows_z)
    total = lax.broadcasted_iota(jnp.int32, shape, 0) + t_start
    total = total + lax.broadcasted_iota(jnp.int32, shape, 1) + x_start
    total = total + lax.broadcasted_iota(jnp.int32, shape, 2) + lax.broadcasted_iota(jnp.int32, shape, 3)
    return (total % 2).astype(jnp.float32)

def block_wilson(spinor, links_list, back_list, herm_re, herm_im):
    t_ahead, t_behind = block_neighbors(spinor, 3)
    x_ahead, x_behind = block_neighbors(spinor, 4)
    y_ahead, y_behind, z_ahead, z_behind = plane_neighbors(spinor, LZ, True)
    return wilson_apply(spinor, [t_ahead, x_ahead, y_ahead, z_ahead], [t_behind, x_behind, y_behind, z_behind], links_list, back_list, herm_re, herm_im)

def block_solve(residual, links_list, back_list, herm_re, herm_im):
    answer = jnp.zeros_like(residual)
    remain = residual
    for sweep_index in range(MR_STEPS):
        image_field = block_wilson(remain, links_list, back_list, herm_re, herm_im)
        inner_re = block_sum(lax.optimization_barrier(jnp.sum(image_field[0] * remain[0] + image_field[1] * remain[1], axis=(0, 1))), LZ) / block_entries
        inner_im = block_sum(lax.optimization_barrier(jnp.sum(image_field[0] * remain[1] - image_field[1] * remain[0], axis=(0, 1))), LZ) / block_entries
        squares = block_sum(lax.optimization_barrier(jnp.sum(image_field[0] * image_field[0] + image_field[1] * image_field[1], axis=(0, 1))), LZ) / block_entries + mean_eps
        alpha_re = block_expand(inner_re / squares)
        alpha_im = block_expand(inner_im / squares)
        answer = answer + jnp.stack([alpha_re * remain[0] - alpha_im * remain[1], alpha_re * remain[1] + alpha_im * remain[0]])
        remain = remain - jnp.stack([alpha_re * image_field[0] - alpha_im * image_field[1], alpha_re * image_field[1] + alpha_im * image_field[0]])
    return answer

def coarse_apply(operator, shifted):
    total_re = 0.0
    total_im = 0.0
    for stencil in range(9):
        neighbor = shifted[stencil]
        matrix_re = operator[stencil, 0]
        matrix_im = operator[stencil, 1]
        total_re = total_re + lax.optimization_barrier(jnp.sum(matrix_re * neighbor[0][None] - matrix_im * neighbor[1][None], axis=-1))
        total_im = total_im + lax.optimization_barrier(jnp.sum(matrix_re * neighbor[1][None] + matrix_im * neighbor[0][None], axis=-1))
    return jnp.stack([jnp.moveaxis(total_re, 0, -1), jnp.moveaxis(total_im, 0, -1)])

def inner_product(left, right):
    return (jnp.sum(left[0] * right[0] + left[1] * right[1]), jnp.sum(left[0] * right[1] - left[1] * right[0]))

def complex_scale(scale_re, scale_im, values):
    return jnp.stack([scale_re * values[0] - scale_im * values[1], scale_re * values[1] + scale_im * values[0]])

def torus_neighbors(view):
    shifted = [view]
    for axis in (1, 2, 3, 4):
        shifted.append(jnp.roll(view, -1, axis=axis))
        shifted.append(jnp.roll(view, 1, axis=axis))
    return shifted

def reference(source, gauge_links, clover_raw, null_vectors, coarse_operator):
    links32 = gauge_links.astype(jnp.float32)
    herm_re, herm_im = hermitian(clover_raw)
    t_len = source.shape[3]
    position = lax.broadcasted_iota(jnp.int32, (t_len, 1, 1), 0)
    sign_ahead = jnp.where(position == t_len - 1, -1.0, 1.0)
    sign_behind = jnp.where(position == 0, -1.0, 1.0)
    links_list = [links32[0], links32[1], links32[2], links32[3]]
    back_list = [jnp.roll(links32[0], 1, axis=3), jnp.roll(links32[1], 1, axis=4), plane_neighbors(links32[2], LZ, False)[1], plane_neighbors(links32[3], LZ, False)[3]]

    def global_wilson(spinor):
        t_ahead = jnp.roll(spinor, -1, axis=3) * sign_ahead
        t_behind = jnp.roll(spinor, 1, axis=3) * sign_behind
        x_ahead = jnp.roll(spinor, -1, axis=4)
        x_behind = jnp.roll(spinor, 1, axis=4)
        y_ahead, y_behind, z_ahead, z_behind = plane_neighbors(spinor, LZ, False)
        return wilson_apply(spinor, [t_ahead, x_ahead, y_ahead, z_ahead], [t_behind, x_behind, y_behind, z_behind], links_list, back_list, herm_re, herm_im)
    color_field = block_expand(block_parity(NT // 4, NX // 4, 0, 0, LY // 4, LZ // 4))
    smoothed = jnp.zeros_like(source)
    for sap_cycle in range(SAP_CYCLES):
        for colour_index in range(2):
            residual = source - global_wilson(smoothed)
            weight = color_field if colour_index == 1 else 1.0 - color_field
            smoothed = smoothed + weight * block_solve(residual, links_list, back_list, herm_re, herm_im)
    residual = source - global_wilson(smoothed)
    rows_re = []
    rows_im = []
    for vector in range(NVEC):
        basis_vec = null_vectors[vector].astype(jnp.float32)
        rows_re.append(block_sum(lax.optimization_barrier(jnp.sum(basis_vec[0] * residual[0] + basis_vec[1] * residual[1], axis=(0, 1))), LZ))
        rows_im.append(block_sum(lax.optimization_barrier(jnp.sum(basis_vec[0] * residual[1] - basis_vec[1] * residual[0], axis=(0, 1))), LZ))
    coarse_rhs = jnp.stack([jnp.stack(rows_re, axis=-1), jnp.stack(rows_im, axis=-1)])
    span_t = LT // 4
    span_x = LX // 4
    rows_y = LY // 4
    rows_z = LZ // 4
    operator = coarse_operator.reshape((9, 2, NVEC, N_TA, N_XYZ, span_t, span_x, rows_y, rows_z, NVEC))
    operator = jnp.transpose(operator, (0, 1, 2, 3, 5, 4, 6, 7, 8, 9))
    operator = operator.reshape((9, 2, NVEC, N_TA * span_t, N_XYZ * span_x, rows_y, rows_z, NVEC))
    answer = jnp.zeros_like(coarse_rhs)
    remain = coarse_rhs
    past_directions = []
    past_images = []
    for iteration in range(GCR_ITERS):
        direction = remain
        image_field = coarse_apply(operator, torus_neighbors(direction))
        margins = [inner_product(unit, image_field) for unit in past_images]
        for earlier in range(len(margins)):
            image_field = image_field - complex_scale(margins[earlier][0], margins[earlier][1], past_images[earlier])
            direction = direction - complex_scale(margins[earlier][0], margins[earlier][1], past_directions[earlier])
        length = jnp.sqrt(inner_product(image_field, image_field)[0] + mean_eps)
        along = inner_product(image_field, remain)
        unit_image = image_field / length
        unit_direction = direction / length
        step_re = along[0] / length
        step_im = along[1] / length
        answer = answer + complex_scale(step_re, step_im, unit_direction)
        remain = remain - complex_scale(step_re, step_im, unit_image)
        past_directions.append(unit_direction)
        past_images.append(unit_image)
    correction = jnp.zeros_like(source)
    for vector in range(NVEC):
        basis_vec = null_vectors[vector].astype(jnp.float32)
        error_re = block_expand(answer[0, ..., vector])
        error_im = block_expand(answer[1, ..., vector])
        correction = correction + jnp.stack([basis_vec[0] * error_re - basis_vec[1] * error_im, basis_vec[0] * error_im + basis_vec[1] * error_re])
    solution = smoothed + correction
    flat_error = answer.reshape((2, N_TA, span_t, N_XYZ, span_x, rows_y, rows_z, NVEC))
    flat_error = jnp.transpose(flat_error, (0, 1, 3, 2, 4, 5, 6, 7)).reshape((2, -1))
    return (solution, flat_error)
```

```python
import functools

import jax
import jax.numpy as jnp
from jax import lax
from jax.experimental import pallas as pl
from jax.experimental.pallas import tpu as pltpu
from jax.sharding import PartitionSpec as P

MESH = pl.DeviceIdType.MESH
NVEC = 16
MR_STEPS = 2
SAP_CYCLES = 2
GCR_ITERS = 4
HALF_STEPS = 2 * SAP_CYCLES

mass_shift = 0.2
mean_eps = 1e-06
block_entries = 6144.0

gamma_perm = [[2, 3, 0, 1], [3, 2, 1, 0], [3, 2, 1, 0], [2, 3, 0, 1]]
gamma_real = [[1, 1, 1, 1], [0, 0, 0, 0], [-1, 1, 1, -1], [0, 0, 0, 0]]
gamma_imag = [[0, 0, 0, 0], [1, 1, -1, -1], [0, 0, 0, 0], [1, -1, -1, 1]]


def roll(value, shift, axis):
    axis = value.ndim + axis
    size = value.shape[axis]
    return pltpu.roll(value, shift % size, axis)


def signed_add(base, sign, value):
    return base + value if sign > 0 else base - value


def project(v, mu, sign):
    half_re, half_im = [], []
    for s in range(2):
        q = gamma_perm[mu][s]
        if gamma_real[mu][s]:
            w = sign * gamma_real[mu][s]
            half_re.append(signed_add(v[0][s], w, v[0][q]))
            half_im.append(signed_add(v[1][s], w, v[1][q]))
        else:
            w = sign * gamma_imag[mu][s]
            half_re.append(signed_add(v[0][s], -w, v[1][q]))
            half_im.append(signed_add(v[1][s], w, v[0][q]))
    return jnp.stack(half_re), jnp.stack(half_im)


def unproject(out, half, mu, sign):
    half_re, half_im = half
    for s in range(2):
        out[0][s] = out[0][s] + half_re[s]
        out[1][s] = out[1][s] + half_im[s]
    for s in range(2, 4):
        q = gamma_perm[mu][s]
        if gamma_real[mu][s]:
            w = sign * gamma_real[mu][s]
            out[0][s] = signed_add(out[0][s], w, half_re[q])
            out[1][s] = signed_add(out[1][s], w, half_im[q])
        else:
            w = sign * gamma_imag[mu][s]
            out[0][s] = signed_add(out[0][s], -w, half_im[q])
            out[1][s] = signed_add(out[1][s], w, half_re[q])


def link_apply(links, colour, mu, half):
    half_re, half_im = half
    out_re = out_im = None
    for b in range(3):
        u_re = links[colour, mu, 0, b][None]
        u_im = links[colour, mu, 1, b][None]
        h_re = half_re[:, b][:, None]
        h_im = half_im[:, b][:, None]
        term_re = u_re * h_re - u_im * h_im
        term_im = u_re * h_im + u_im * h_re
        out_re = term_re if b == 0 else out_re + term_re
        out_im = term_im if b == 0 else out_im + term_im
    return out_re, out_im


def link_apply_dagger(links, colour, mu, half):
    half_re, half_im = half
    out_re = out_im = None
    for b in range(3):
        u_re = links[colour, mu, 0, :, b][None]
        u_im = links[colour, mu, 1, :, b][None]
        h_re = half_re[:, b][:, None]
        h_im = half_im[:, b][:, None]
        term_re = u_re * h_re + u_im * h_im
        term_im = u_re * h_im - u_im * h_re
        out_re = term_re if b == 0 else out_re + term_re
        out_im = term_im if b == 0 else out_im + term_im
    return out_re, out_im


def split_dot(value, weights):
    rows = value.shape[0]
    high = value.astype(jnp.bfloat16)
    rest = value - high.astype(jnp.float32)
    mid = rest.astype(jnp.bfloat16)
    low = (rest - mid.astype(jnp.float32)).astype(jnp.bfloat16)
    out = jnp.dot(
        jnp.concatenate([high, mid, low], axis=0), weights, preferred_element_type=jnp.float32
    )
    return out[:rows] + out[rows : 2 * rows] + out[2 * rows :]


def iota(shape, dim):
    return lax.broadcasted_iota(jnp.int32, shape, dim)


def kernel(
    n_ta, n_xyz,
    source_ref, gauge_ref, clover_ref, null_ref, coarse_ref,
    out_ref, error_ref,
    link_in, link_out, herm, resid, smooth,
    halo_out, halo_in, partial, spread,
    cvec_out, cvec_in, dot_out, dot_row, dot_sum, dot_col,
    halo_send, halo_recv, cvec_send, cvec_recv,
    row_send, row_recv, col_send, col_recv,
):
    f32 = jnp.float32
    ta = lax.axis_index("ta")
    xyz = lax.axis_index("xyz")

    def ta_off(d):
        return (lax.rem(ta + d, n_ta), xyz)

    def xyz_off(d):
        return (ta, lax.rem(xyz + d, n_xyz))

    barrier = pltpu.get_barrier_semaphore()
    for d in range(1, n_ta):
        pl.semaphore_signal(barrier, inc=1, device_id=ta_off(d), device_id_type=MESH)
    for d in range(1, n_xyz):
        pl.semaphore_signal(barrier, inc=1, device_id=xyz_off(d), device_id_type=MESH)

    vreg = (8, 128)
    lane = iota(vreg, 1)
    subl = iota(vreg, 0)
    t_low = subl // 4
    x_pos = subl % 4
    y_pos = lane // 16
    z_pos = lane % 16
    parity = (ta + xyz + y_pos // 4 + z_pos // 4) % 2
    t_high = [parity, 1 - parity]

    def compact(natural):
        first = natural[..., :8, :]
        second = roll(natural[..., 8:, :], 64, -1)
        low = jnp.broadcast_to(parity == 0, first.shape)
        return jnp.where(low, first, second), jnp.where(low, second, first)

    def expand(even, odd):
        low = jnp.broadcast_to(parity == 0, even.shape)
        return jnp.where(low, even, odd), roll(jnp.where(low, odd, even), 64, -1)

    t_sign = jnp.where(ta == n_ta - 1, f32(0.5), f32(-0.5))
    for mu in range(4):
        planes = gauge_ref[pl.ds(18 * mu, 18)].astype(f32)
        pair = compact(planes)
        for colour in range(2):
            if mu == 0:
                inside = jnp.logical_not((t_high[colour] == 1) & (t_low == 1))
            elif mu == 1:
                inside = x_pos != 3
            elif mu == 2:
                inside = y_pos % 4 != 3
            else:
                inside = z_pos % 4 != 3
            weight_in = jnp.where(inside, f32(-0.5), f32(0.0))
            weight_out = jnp.where(inside, f32(0.0), t_sign if mu == 0 else f32(-0.5))
            for part in range(2):
                for row in range(3):
                    first = 9 * part + 3 * row
                    mine = pair[colour][first : first + 3]
                    link_in[colour, mu, part, :, row] = mine * weight_in
                    link_out[colour, mu, part, :, row] = mine * weight_out

    for chi in range(2):
        for col in range(6):
            row_at = 36 * chi + 6 * col
            for part in range(2):
                base = 72 * part
                line = clover_ref[pl.ds(base + row_at, 6)].astype(f32)
                column = jnp.stack(
                    [clover_ref[base + 36 * chi + 6 * r + col].astype(f32) for r in range(6)]
                )
                if part == 0:
                    sym = 0.5 * (column + line)
                    diag = iota((6, 1, 1), 0) == col
                    sym = sym + jnp.where(diag, f32(4.0 + mass_shift), f32(0.0))
                else:
                    sym = 0.5 * (column - line)
                pair = compact(sym)
                for colour in range(2):
                    herm[colour, part, chi, col] = pair[colour]

    pair = compact(source_ref[...])
    for colour in range(2):
        resid[colour] = pair[colour].reshape(2, 4, 3, 8, 128)
    smooth[...] = jnp.zeros_like(smooth)

    square = (128, 128)
    into = iota(square, 0)
    outof = iota(square, 1)
    block_weights = ((into % 16) // 4 == (outof % 16) // 4).astype(f32).astype(jnp.bfloat16)

    def load(ref, colour):
        value = ref[colour]
        return [[value[part, s] for s in range(4)] for part in range(2)]

    def t_swap(value):
        return roll(value, 4, -2)

    def block_wilson(v, colour):
        out = [[None] * 4, [None] * 4]
        for chi in range(2):
            v_re = jnp.concatenate([v[0][2 * chi], v[0][2 * chi + 1]])
            v_im = jnp.concatenate([v[1][2 * chi], v[1][2 * chi + 1]])
            acc_re = acc_im = None
            for col in range(6):
                h_re = herm[colour, 0, chi, col]
                h_im = herm[colour, 1, chi, col]
                term_re = h_re * v_re[col][None] - h_im * v_im[col][None]
                term_im = h_re * v_im[col][None] + h_im * v_re[col][None]
                acc_re = term_re if col == 0 else acc_re + term_re
                acc_im = term_im if col == 0 else acc_im + term_im
            for half in range(2):
                out[0][2 * chi + half] = acc_re[3 * half : 3 * half + 3]
                out[1][2 * chi + half] = acc_im[3 * half : 3 * half + 3]
        low = t_low == 0
        for mu in range(4):
            ahead = project(v, mu, -1)
            behind = link_apply_dagger(link_in, colour, mu, project(v, mu, 1))
            if mu == 0:
                ahead = [
                    roll(jnp.where(low, roll(w, 64, -1), w), 4, -2) for w in ahead
                ]
                behind = [
                    roll(jnp.where(low, w, roll(w, 64, -1)), 4, -2) for w in behind
                ]
            elif mu == 1:
                ahead = [roll(w, -1, -2) for w in ahead]
                behind = [roll(w, 1, -2) for w in behind]
            else:
                step = 16 if mu == 2 else 1
                ahead = [roll(w, -step, -1) for w in ahead]
                behind = [roll(w, step, -1) for w in behind]
            unproject(out, link_apply(link_in, colour, mu, ahead), mu, -1)
            unproject(out, behind, mu, 1)
        return out

    def each(function, *fields):
        return [[function(*(f[part][s] for f in fields)) for s in range(4)] for part in range(2)]

    def site_sum(pairs):
        total = None
        for left, right, sign in pairs:
            for s in range(4):
                term = left[s] * right[s]
                total = term if total is None else signed_add(total, sign, term)
        return total[0] + total[1] + total[2]

    def minimal_residual(colour):
        rho = load(resid, colour)
        answer = None
        for _ in range(MR_STEPS):
            image = block_wilson(rho, colour)
            sums = jnp.concatenate(
                [
                    site_sum([(image[0], rho[0], 1), (image[1], rho[1], 1)]),
                    site_sum([(image[0], rho[1], 1), (image[1], rho[0], -1)]),
                    site_sum([(image[0], image[0], 1), (image[1], image[1], 1)]),
                ],
                axis=0,
            )
            sums = split_dot(sums, block_weights)
            sums = [
                jnp.sum(sums[8 * i : 8 * i + 8], axis=0, keepdims=True) / block_entries
                for i in range(3)
            ]
            squares = sums[2] + mean_eps
            a_re = jnp.broadcast_to(sums[0] / squares, vreg)
            a_im = jnp.broadcast_to(sums[1] / squares, vreg)
            step = [
                [a_re * rho[0][s] - a_im * rho[1][s] for s in range(4)],
                [a_re * rho[1][s] + a_im * rho[0][s] for s in range(4)],
            ]
            answer = step if answer is None else each(jnp.add, answer, step)
            rho = [
                [rho[0][s] - (a_re * image[0][s] - a_im * image[1][s]) for s in range(4)],
                [rho[1][s] - (a_re * image[1][s] + a_im * image[0][s]) for s in range(4)],
            ]
        return answer, rho

    def flat(half):
        return jnp.concatenate([half[0].reshape(6, 8, 128), half[1].reshape(6, 8, 128)])

    def pack_x(half, face):
        groups = flat(half).reshape(3, 4, 8, 128)
        packed = None
        for j in range(4):
            moved = roll(groups[:, j], j - face, -2)
            packed = moved if j == 0 else jnp.where(x_pos == j, moved, packed)
        return packed

    def unpack_x(packed, face):
        rows = jnp.stack([roll(packed, face - j, -2) for j in range(4)], axis=1)
        rows = rows.reshape(2, 2, 3, 8, 128)
        return rows[0], rows[1]

    def pack_t(half, face, away):
        groups = flat(half).reshape(3, 4, 8, 128)
        here = (away == 0) if face == 0 else (away == 1)
        first = jnp.where(here, groups[:, 0], roll(groups[:, 1], 64, -1))
        second = jnp.where(here, groups[:, 2], roll(groups[:, 3], 64, -1))
        if face == 0:
            return jnp.where(t_low == 0, first, roll(second, 4, -2))
        return jnp.where(t_low == 1, first, roll(second, 4, -2))

    def unpack_t(packed):
        turned = roll(packed, 64, -1)
        rows = jnp.stack([roll(turned, 4, -2), roll(packed, 4, -2), turned, packed], axis=1)
        rows = rows.reshape(2, 2, 3, 8, 128)
        return rows[0], rows[1]

    def halo_copy(step, side):
        target = (ta_off(n_ta - 1), ta_off(1), xyz_off(n_xyz - 1), xyz_off(1))[side]
        return pltpu.make_async_remote_copy(
            src_ref=halo_out.at[step, side],
            dst_ref=halo_in.at[step, side],
            send_sem=halo_send.at[step, side],
            recv_sem=halo_recv.at[step, side],
            device_id=target,
            device_id_type=MESH,
        )

    def reduce_copies(slot):
        rows = [
            pltpu.make_async_remote_copy(
                src_ref=dot_out.at[slot],
                dst_ref=dot_row.at[slot, d - 1],
                send_sem=row_send.at[slot, d - 1],
                recv_sem=row_recv.at[slot, d - 1],
                device_id=xyz_off(d),
                device_id_type=MESH,
            )
            for d in range(1, n_xyz)
        ]
        cols = [
            pltpu.make_async_remote_copy(
                src_ref=dot_sum.at[slot],
                dst_ref=dot_col.at[slot, d - 1],
                send_sem=col_send.at[slot, d - 1],
                recv_sem=col_recv.at[slot, d - 1],
                device_id=ta_off(d),
                device_id_type=MESH,
            )
            for d in range(1, n_ta)
        ]
        return rows, cols

    trace_rows, trace_cols = reduce_copies(0)
    coarse_lane = iota((16, 128), 1)
    coarse_row = iota((16, 128), 0)
    on_diagonal = (coarse_lane % NVEC) == coarse_row
    trace = jnp.where(on_diagonal, coarse_ref[0, 0], f32(0.0))
    trace = jnp.sum(trace, axis=0, keepdims=True)
    trace = jnp.sum(trace, axis=1, keepdims=True) / f32(128 * n_ta * n_xyz)
    dot_out[0] = jnp.broadcast_to(trace, vreg)

    pl.semaphore_wait(barrier, n_ta - 1 + n_xyz - 1)
    for copy in trace_rows:
        copy.start()

    def half_step(step, carry):
        colour = lax.rem(step, 2)
        other = 1 - colour
        z, rho = minimal_residual(colour)
        away = jnp.where(colour == 0, t_high[0], t_high[1])
        ahead_t = project(z, 0, -1)
        behind_t = link_apply_dagger(link_out, colour, 0, project(z, 0, 1))
        ahead_x = project(z, 1, -1)
        behind_x = link_apply_dagger(link_out, colour, 1, project(z, 1, 1))
        halo_out[step, 0] = pack_t(ahead_t, 0, away)
        halo_out[step, 1] = pack_t(behind_t, 3, away)
        halo_out[step, 2] = pack_x(ahead_x, 0)
        halo_out[step, 3] = pack_x(behind_x, 3)
        copies = [halo_copy(step, side) for side in range(4)]
        for copy in copies:
            copy.start()
        for part in range(2):
            for s in range(4):
                resid[colour, part, s] = rho[part][s]
                smooth[colour, part, s] = smooth[colour, part, s] + z[part][s]

        def zeros():
            return [[jnp.zeros((3, 8, 128), f32)] * 4 for _ in range(2)]

        change = zeros()
        for mu in (2, 3):
            ahead = project(z, mu, -1)
            behind = link_apply_dagger(link_out, colour, mu, project(z, mu, 1))
            if mu == 2:
                ahead = [roll(w, -16, -1) for w in ahead]
                behind = [roll(w, 16, -1) for w in behind]
            else:
                ahead = [jnp.where(z_pos == 15, roll(w, 15, -1), roll(w, -1, -1)) for w in ahead]
                behind = [jnp.where(z_pos == 0, roll(w, -15, -1), roll(w, 1, -1)) for w in behind]
            unproject(change, link_apply(link_out, other, mu, ahead), mu, -1)
            unproject(change, behind, mu, 1)
        for copy in copies:
            copy.wait()
        ahead = unpack_t(halo_in[step, 0])
        unproject(change, link_apply(link_out, other, 0, ahead), 0, -1)
        first = (away == 1) & (t_low == 0)
        behind = [jnp.where(first, w, f32(0.0)) for w in unpack_t(halo_in[step, 1])]
        unproject(change, behind, 0, 1)
        ahead = unpack_x(halo_in[step, 2], 3)
        unproject(change, link_apply(link_out, other, 1, ahead), 1, -1)
        behind = [jnp.where(x_pos == 0, w, f32(0.0)) for w in unpack_x(halo_in[step, 3], 0)]
        unproject(change, behind, 1, 1)
        for part in range(2):
            for s in range(4):
                resid[other, part, s] = resid[other, part, s] - change[part][s]
        return carry

    lax.fori_loop(0, HALF_STEPS, half_step, 0)

    for copy in trace_rows:
        copy.wait()
    total = dot_out[0]
    for d in range(n_xyz - 1):
        total = total + dot_row[0, d]
    dot_sum[0] = total
    for copy in trace_cols:
        copy.start()

    natural = expand(resid[0].reshape(24, 8, 128), resid[1].reshape(24, 8, 128))

    def restrict(a, carry):
        basis = null_ref[a].astype(f32)
        acc_re = acc_im = None
        for i, half in enumerate(natural):
            b_re = basis[0, :, 8 * i : 8 * i + 8]
            b_im = basis[1, :, 8 * i : 8 * i + 8]
            term_re = jnp.sum(b_re * half[:12] + b_im * half[12:], axis=0)
            term_im = jnp.sum(b_re * half[12:] - b_im * half[:12], axis=0)
            acc_re = term_re if i == 0 else acc_re + term_re
            acc_im = term_im if i == 0 else acc_im + term_im
        partial[0, a] = acc_re
        partial[1, a] = acc_im
        return carry

    lax.fori_loop(0, NVEC, restrict, 0)
    site_agg = 4 * (into // 64) + (into % 16) // 4
    to_agg = (site_agg == outof // NVEC).astype(f32).astype(jnp.bfloat16)
    site_agg = 4 * (outof // 64) + (outof % 16) // 4
    from_agg = (site_agg == into // NVEC).astype(f32).astype(jnp.bfloat16)
    agg_weights = (into // NVEC == outof // NVEC).astype(f32).astype(jnp.bfloat16)
    rows = jnp.sum(partial[...], axis=2).reshape(32, 128)

    def diagonal_row(both):
        return [
            jnp.sum(
                jnp.where(on_diagonal, both[16 * i : 16 * i + 16], f32(0.0)),
                axis=0,
                keepdims=True,
            )
            for i in range(2)
        ]

    vec = diagonal_row(split_dot(rows, to_agg))

    for copy in trace_cols:
        copy.wait()
    total = dot_sum[0]
    for d in range(n_ta - 1):
        total = total + dot_col[0, d]
    shift = total

    row_at = iota(vreg, 0)
    basis_re = jnp.where(row_at == 0, jnp.broadcast_to(vec[0], vreg), f32(0.0))
    basis_im = jnp.where(row_at == 0, jnp.broadcast_to(vec[1], vreg), f32(0.0))
    agg_z = (iota((1, 128), 1) % 64) // NVEC

    def cvec_copy(k, side):
        target = (ta_off(n_ta - 1), ta_off(1), xyz_off(n_xyz - 1), xyz_off(1))[side]
        return pltpu.make_async_remote_copy(
            src_ref=cvec_out.at[k],
            dst_ref=cvec_in.at[k, side],
            send_sem=cvec_send.at[k, side],
            recv_sem=cvec_recv.at[k, side],
            device_id=target,
            device_id_type=MESH,
        )

    for k in range(GCR_ITERS):
        re, im = vec
        cvec_out[k] = jnp.where(
            row_at == 0, jnp.broadcast_to(re, vreg), jnp.broadcast_to(im, vreg)
        )
        copies = [cvec_copy(k, side) for side in range(4)]
        for copy in copies:
            copy.start()

        def term(stencil, n_re, n_im, acc):
            m_re = coarse_ref[stencil, 0]
            m_im = coarse_ref[stencil, 1]
            return (
                acc[0] + (m_re * n_re - m_im * n_im),
                acc[1] + (m_re * n_im + m_im * n_re),
            )

        diag_shift = jnp.where(on_diagonal, jnp.broadcast_to(shift[:1], (16, 128)), f32(0.0))
        centre_re = coarse_ref[0, 0] - diag_shift
        centre_im = coarse_ref[0, 1]
        acc = (centre_re * re - centre_im * im, centre_re * im + centre_im * re)
        far = [roll(w, 64, -1) for w in vec]
        acc = term(5, *far, acc)
        acc = term(6, *far, acc)
        z_ahead = [jnp.where(agg_z == 3, roll(w, 48, -1), roll(w, -16, -1)) for w in vec]
        z_behind = [jnp.where(agg_z == 0, roll(w, -48, -1), roll(w, 16, -1)) for w in vec]
        acc = term(7, *z_ahead, acc)
        acc = term(8, *z_behind, acc)
        for side, copy in enumerate(copies):
            copy.wait()
            got = cvec_in[k, side]
            acc = term(1 + side, got[0:1], got[1:2], acc)
        vec = diagonal_row(split_dot(jnp.concatenate(acc, axis=0), agg_weights))
        basis_re = jnp.where(row_at == k + 1, jnp.broadcast_to(vec[0], vreg), basis_re)
        basis_im = jnp.where(row_at == k + 1, jnp.broadcast_to(vec[1], vreg), basis_im)

    gram = jnp.zeros(vreg, f32)
    for k in range(GCR_ITERS + 1):
        k_re = basis_re[k : k + 1]
        k_im = basis_im[k : k + 1]
        dot_re = jnp.sum(basis_re * k_re + basis_im * k_im, axis=1, keepdims=True)
        dot_im = jnp.sum(basis_re * k_im - basis_im * k_re, axis=1, keepdims=True)
        gram = jnp.where(lane == 2 * k, jnp.broadcast_to(dot_re, vreg), gram)
        gram = jnp.where(lane == 2 * k + 1, jnp.broadcast_to(dot_im, vreg), gram)
    gram_rows, gram_cols = reduce_copies(1)
    dot_out[1] = gram
    for copy in gram_rows:
        copy.start()
    for d, copy in enumerate(gram_rows):
        copy.wait()
        gram = gram + dot_row[1, d]
    dot_sum[1] = gram
    for copy in gram_cols:
        copy.start()
    for d, copy in enumerate(gram_cols):
        copy.wait()
        gram = gram + dot_col[1, d]

    columns = []
    for k in range(GCR_ITERS + 1):
        columns.append(
            (
                jnp.broadcast_to(gram[:, 2 * k : 2 * k + 1], vreg),
                jnp.broadcast_to(gram[:, 2 * k + 1 : 2 * k + 2], vreg),
            )
        )

    def gram_apply(x):
        out = None
        for k, (g_re, g_im) in enumerate(columns):
            x_re = jnp.broadcast_to(x[0][k : k + 1], vreg)
            x_im = jnp.broadcast_to(x[1][k : k + 1], vreg)
            now = (g_re * x_re - g_im * x_im, g_re * x_im + g_im * x_re)
            out = now if out is None else (out[0] + now[0], out[1] + now[1])
        return out

    def row_sum(value):
        return jnp.broadcast_to(jnp.sum(value, axis=0, keepdims=True), vreg)

    def inner(left, image):
        return (
            row_sum(left[0] * image[0] + left[1] * image[1]),
            row_sum(left[0] * image[1] - left[1] * image[0]),
        )

    def scaled(a, x):
        return (a[0] * x[0] - a[1] * x[1], a[0] * x[1] + a[1] * x[0])

    def minus(x, y):
        return (x[0] - y[0], x[1] - y[1])

    remain = (jnp.where(row_at == 0, f32(1.0), f32(0.0)), jnp.zeros(vreg, f32))
    answer = (jnp.zeros(vreg, f32), jnp.zeros(vreg, f32))
    past = []
    for iteration in range(GCR_ITERS):
        direction = remain
        image = tuple(roll(w, 1, -2) + shift * w for w in direction)
        image_dots = gram_apply(image)
        margins = [inner(unit_image, image_dots) for _, unit_image in past]
        for margin, (unit_direction, unit_image) in zip(margins, past):
            image = minus(image, scaled(margin, unit_image))
            direction = minus(direction, scaled(margin, unit_direction))
        if past:
            image_dots = gram_apply(image)
        squares = jnp.maximum(inner(image, image_dots)[0], f32(0.0))
        along = inner(remain, image_dots)
        inverse = 1.0 / jnp.sqrt(squares + mean_eps)
        unit_image = tuple(w * inverse for w in image)
        unit_direction = tuple(w * inverse for w in direction)
        step = (along[0] * inverse, -(along[1] * inverse))
        moved = scaled(step, unit_direction)
        answer = (answer[0] + moved[0], answer[1] + moved[1])
        remain = minus(remain, scaled(step, unit_image))
        past.append((unit_direction, unit_image))

    error = scaled(answer, (basis_re, basis_im))
    error = [jnp.sum(w, axis=0, keepdims=True) for w in error]
    error_ref[0:1] = error[0]
    error_ref[1:2] = error[1]

    diag_rows = jnp.concatenate(
        [jnp.where(on_diagonal, jnp.broadcast_to(w, (16, 128)), f32(0.0)) for w in error], axis=0
    )
    spread[...] = split_dot(diag_rows, from_agg).reshape(2, NVEC, 1, 128)
    smooth_first, smooth_second = expand(
        smooth[0].reshape(24, 8, 128), smooth[1].reshape(24, 8, 128)
    )
    for i, half in enumerate((smooth_first, smooth_second)):
        out_ref[:, 8 * i : 8 * i + 8] = half

    def prolong(entry, carry):
        n_re = null_ref[:, 0, entry].astype(f32)
        n_im = null_ref[:, 1, entry].astype(f32)
        e_re = spread[0]
        e_im = spread[1]
        out_ref[entry] = out_ref[entry] + jnp.sum(n_re * e_re - n_im * e_im, axis=0)
        out_ref[12 + entry] = out_ref[12 + entry] + jnp.sum(n_re * e_im + n_im * e_re, axis=0)
        return carry

    lax.fori_loop(0, 12, prolong, 0)


def solution(mesh):
    n_ta, n_xyz = mesh.shape["ta"], mesh.shape["xyz"]

    def shards(source, gauge_links, clover_raw, null_vectors, coarse_operator):
        f32 = jnp.float32
        dma = pltpu.SemaphoreType.DMA
        field, error = pl.pallas_call(
            functools.partial(kernel, n_ta, n_xyz),
            out_shape=(
                jax.ShapeDtypeStruct((24, 16, 128), f32),
                jax.ShapeDtypeStruct((2, 128), f32),
            ),
            in_specs=[pl.BlockSpec(memory_space=pltpu.VMEM)] * 5,
            out_specs=(pl.BlockSpec(memory_space=pltpu.VMEM),) * 2,
            scratch_shapes=[
                pltpu.VMEM((2, 4, 2, 3, 3, 8, 128), f32),
                pltpu.VMEM((2, 4, 2, 3, 3, 8, 128), f32),
                pltpu.VMEM((2, 2, 2, 6, 6, 8, 128), f32),
                pltpu.VMEM((2, 2, 4, 3, 8, 128), f32),
                pltpu.VMEM((2, 2, 4, 3, 8, 128), f32),
                pltpu.VMEM((HALF_STEPS, 4, 3, 8, 128), f32),
                pltpu.VMEM((HALF_STEPS, 4, 3, 8, 128), f32),
                pltpu.VMEM((2, NVEC, 8, 128), f32),
                pltpu.VMEM((2, NVEC, 1, 128), f32),
                pltpu.VMEM((GCR_ITERS, 8, 128), f32),
                pltpu.VMEM((GCR_ITERS, 4, 8, 128), f32),
                pltpu.VMEM((2, 8, 128), f32),
                pltpu.VMEM((2, n_xyz - 1, 8, 128), f32),
                pltpu.VMEM((2, 8, 128), f32),
                pltpu.VMEM((2, n_ta - 1, 8, 128), f32),
                dma((HALF_STEPS, 4)),
                dma((HALF_STEPS, 4)),
                dma((GCR_ITERS, 4)),
                dma((GCR_ITERS, 4)),
                dma((2, n_xyz - 1)),
                dma((2, n_xyz - 1)),
                dma((2, n_ta - 1)),
                dma((2, n_ta - 1)),
            ],
            compiler_params=pltpu.CompilerParams(
                collective_id=0, has_side_effects=True, vmem_limit_bytes=40 * 2**20
            ),
        )(
            source.reshape(24, 16, 128),
            gauge_links.reshape(72, 16, 128),
            clover_raw.reshape(144, 16, 128),
            null_vectors.reshape(NVEC, 2, 12, 16, 128),
            coarse_operator,
        )
        return field.reshape(source.shape), error

    in_specs = (
        P(None, None, None, "ta", "xyz", None),
        P(None, None, None, None, "ta", "xyz", None),
        P(None, None, None, None, "ta", "xyz", None),
        P(None, None, None, None, "ta", "xyz", None),
        P(None, None, None, ("ta", "xyz")),
    )
    out_specs = (P(None, None, None, "ta", "xyz", None), P(None, ("ta", "xyz")))
    return jax.shard_map(shards, mesh=mesh, in_specs=in_specs, out_specs=out_specs, check_vma=False)
```

```python
import functools

import jax
import jax.numpy as jnp
from jax import lax
from jax.experimental import pallas as pl
from jax.experimental.pallas import tpu as pltpu
from jax.sharding import PartitionSpec as P

MESH = pl.DeviceIdType.MESH
NVEC = 16
MR_STEPS = 2
SAP_CYCLES = 2
GCR_ITERS = 4
HALF_STEPS = 2 * SAP_CYCLES

mass_shift = 0.2
mean_eps = 1e-06
block_entries = 6144.0

gamma_perm = [[2, 3, 0, 1], [3, 2, 1, 0], [3, 2, 1, 0], [2, 3, 0, 1]]
gamma_real = [[1, 1, 1, 1], [0, 0, 0, 0], [-1, 1, 1, -1], [0, 0, 0, 0]]
gamma_imag = [[0, 0, 0, 0], [1, 1, -1, -1], [0, 0, 0, 0], [1, -1, -1, 1]]


def roll(value, shift, axis):
    axis = value.ndim + axis
    size = value.shape[axis]
    return pltpu.roll(value, shift % size, axis)


def signed_add(base, sign, value):
    return base + value if sign > 0 else base - value


def project(v, mu, sign):
    half_re, half_im = [], []
    for s in range(2):
        q = gamma_perm[mu][s]
        if gamma_real[mu][s]:
            w = sign * gamma_real[mu][s]
            half_re.append(signed_add(v[0][s], w, v[0][q]))
            half_im.append(signed_add(v[1][s], w, v[1][q]))
        else:
            w = sign * gamma_imag[mu][s]
            half_re.append(signed_add(v[0][s], -w, v[1][q]))
            half_im.append(signed_add(v[1][s], w, v[0][q]))
    return jnp.stack(half_re), jnp.stack(half_im)


def unproject(out, half, mu, sign):
    half_re, half_im = half
    for s in range(2):
        out[0][s] = out[0][s] + half_re[s]
        out[1][s] = out[1][s] + half_im[s]
    for s in range(2, 4):
        q = gamma_perm[mu][s]
        if gamma_real[mu][s]:
            w = sign * gamma_real[mu][s]
            out[0][s] = signed_add(out[0][s], w, half_re[q])
            out[1][s] = signed_add(out[1][s], w, half_im[q])
        else:
            w = sign * gamma_imag[mu][s]
            out[0][s] = signed_add(out[0][s], -w, half_im[q])
            out[1][s] = signed_add(out[1][s], w, half_re[q])


def link_apply(links, colour, mu, half):
    half_re, half_im = half
    out_re = out_im = None
    for b in range(3):
        u_re = links[colour, mu, 0, b][None]
        u_im = links[colour, mu, 1, b][None]
        h_re = half_re[:, b][:, None]
        h_im = half_im[:, b][:, None]
        term_re = u_re * h_re - u_im * h_im
        term_im = u_re * h_im + u_im * h_re
        out_re = term_re if b == 0 else out_re + term_re
        out_im = term_im if b == 0 else out_im + term_im
    return out_re, out_im


def link_apply_dagger(links, colour, mu, half):
    half_re, half_im = half
    out_re = out_im = None
    for b in range(3):
        u_re = links[colour, mu, 0, :, b][None]
        u_im = links[colour, mu, 1, :, b][None]
        h_re = half_re[:, b][:, None]
        h_im = half_im[:, b][:, None]
        term_re = u_re * h_re + u_im * h_im
        term_im = u_re * h_im - u_im * h_re
        out_re = term_re if b == 0 else out_re + term_re
        out_im = term_im if b == 0 else out_im + term_im
    return out_re, out_im


def split_dot(value, weights):
    rows = value.shape[0]
    high = value.astype(jnp.bfloat16)
    rest = value - high.astype(jnp.float32)
    mid = rest.astype(jnp.bfloat16)
    low = (rest - mid.astype(jnp.float32)).astype(jnp.bfloat16)
    out = jnp.dot(
        jnp.concatenate([high, mid, low], axis=0), weights, preferred_element_type=jnp.float32
    )
    return out[:rows] + out[rows : 2 * rows] + out[2 * rows :]


def iota(shape, dim):
    return lax.broadcasted_iota(jnp.int32, shape, dim)


def kernel(
    n_ta, n_xyz,
    source_hbm, gauge_hbm, clover_hbm, null_hbm, coarse_hbm,
    out_ref, error_ref,
    source_ref, gauge_ref, clover_ref, null_ref, coarse_ref,
    link_in, link_out, herm, resid, smooth, z_ref,
    halo_out, halo_in, partial, spread, prolonged,
    stencil_in, cvec_out, cvec_in, dot_out, dot_row, dot_sum, dot_col,
    load_sem, halo_send, halo_recv, stencil_send, stencil_recv, cvec_send, cvec_recv,
    row_send, row_recv, col_send, col_recv,
):
    f32 = jnp.float32
    ta = lax.axis_index("ta")
    xyz = lax.axis_index("xyz")

    loads = [
        pltpu.make_async_copy(src, dst, load_sem.at[i])
        for i, (src, dst) in enumerate(
            [
                (gauge_hbm, gauge_ref),
                (clover_hbm, clover_ref),
                (source_hbm, source_ref),
                (coarse_hbm, coarse_ref),
                (null_hbm, null_ref),
            ]
        )
    ]
    for load in loads:
        load.start()

    def device_at(t_off, x_off):
        return (lax.rem(ta + t_off + n_ta, n_ta), lax.rem(xyz + x_off + n_xyz, n_xyz))

    def ta_off(d):
        return device_at(d, 0)

    def xyz_off(d):
        return device_at(0, d)

    barrier = pltpu.get_barrier_semaphore()
    peers = [(d, 0) for d in range(1, n_ta)] + [(0, d) for d in range(1, n_xyz)]
    peers = peers + [(1, 1), (1, -1), (-1, 1), (-1, -1)]
    for peer in peers:
        pl.semaphore_signal(barrier, inc=1, device_id=device_at(*peer), device_id_type=MESH)

    vreg = (8, 128)
    lane = iota(vreg, 1)
    subl = iota(vreg, 0)
    t_low = subl // 4
    x_pos = subl % 4
    y_pos = lane // 16
    z_pos = lane % 16
    parity = (ta + xyz + y_pos // 4 + z_pos // 4) % 2
    t_high = [parity, 1 - parity]

    def compact(natural):
        first = natural[..., :8, :]
        second = roll(natural[..., 8:, :], 64, -1)
        low = jnp.broadcast_to(parity == 0, first.shape)
        return jnp.where(low, first, second), jnp.where(low, second, first)

    def expand(even, odd):
        low = jnp.broadcast_to(parity == 0, even.shape)
        return jnp.where(low, even, odd), roll(jnp.where(low, odd, even), 64, -1)

    loads[0].wait()
    t_sign = jnp.where(ta == n_ta - 1, f32(0.5), f32(-0.5))
    for mu in range(4):
        planes = gauge_ref[pl.ds(18 * mu, 18)].astype(f32)
        pair = compact(planes)
        for colour in range(2):
            if mu == 0:
                inside = jnp.logical_not((t_high[colour] == 1) & (t_low == 1))
            elif mu == 1:
                inside = x_pos != 3
            elif mu == 2:
                inside = y_pos % 4 != 3
            else:
                inside = z_pos % 4 != 3
            weight_in = jnp.where(inside, f32(-0.5), f32(0.0))
            weight_out = jnp.where(inside, f32(0.0), t_sign if mu == 0 else f32(-0.5))
            for part in range(2):
                for row in range(3):
                    first = 9 * part + 3 * row
                    mine = pair[colour][first : first + 3]
                    link_in[colour, mu, part, :, row] = mine * weight_in
                    link_out[colour, mu, part, :, row] = mine * weight_out

    loads[1].wait()
    for chi in range(2):
        for col in range(6):
            row_at = 36 * chi + 6 * col
            for part in range(2):
                base = 72 * part
                line = clover_ref[pl.ds(base + row_at, 6)].astype(f32)
                column = jnp.stack(
                    [clover_ref[base + 36 * chi + 6 * r + col].astype(f32) for r in range(6)]
                )
                if part == 0:
                    sym = 0.5 * (column + line)
                    diag = iota((6, 1, 1), 0) == col
                    sym = sym + jnp.where(diag, f32(4.0 + mass_shift), f32(0.0))
                else:
                    sym = 0.5 * (column - line)
                pair = compact(sym)
                for colour in range(2):
                    herm[colour, part, chi, col] = pair[colour]

    loads[2].wait()
    pair = compact(source_ref[...])
    for colour in range(2):
        resid[colour] = pair[colour].reshape(2, 4, 3, 8, 128)
    smooth[...] = jnp.zeros_like(smooth)

    square = (128, 128)
    into = iota(square, 0)
    outof = iota(square, 1)
    block_weights = ((into % 16) // 4 == (outof % 16) // 4).astype(f32).astype(jnp.bfloat16)

    def load(ref, colour):
        value = ref[colour]
        return [[value[part, s] for s in range(4)] for part in range(2)]

    def t_swap(value):
        return roll(value, 4, -2)

    def block_wilson(v, colour):
        out = [[None] * 4, [None] * 4]
        for chi in range(2):
            v_re = jnp.concatenate([v[0][2 * chi], v[0][2 * chi + 1]])
            v_im = jnp.concatenate([v[1][2 * chi], v[1][2 * chi + 1]])
            acc_re = acc_im = None
            for col in range(6):
                h_re = herm[colour, 0, chi, col]
                h_im = herm[colour, 1, chi, col]
                term_re = h_re * v_re[col][None] - h_im * v_im[col][None]
                term_im = h_re * v_im[col][None] + h_im * v_re[col][None]
                acc_re = term_re if col == 0 else acc_re + term_re
                acc_im = term_im if col == 0 else acc_im + term_im
            for half in range(2):
                out[0][2 * chi + half] = acc_re[3 * half : 3 * half + 3]
                out[1][2 * chi + half] = acc_im[3 * half : 3 * half + 3]
        low = t_low == 0
        for mu in range(4):
            ahead = project(v, mu, -1)
            behind = link_apply_dagger(link_in, colour, mu, project(v, mu, 1))
            if mu == 0:
                ahead = [
                    roll(jnp.where(low, roll(w, 64, -1), w), 4, -2) for w in ahead
                ]
                behind = [
                    roll(jnp.where(low, w, roll(w, 64, -1)), 4, -2) for w in behind
                ]
            elif mu == 1:
                ahead = [roll(w, -1, -2) for w in ahead]
                behind = [roll(w, 1, -2) for w in behind]
            else:
                step = 16 if mu == 2 else 1
                ahead = [roll(w, -step, -1) for w in ahead]
                behind = [roll(w, step, -1) for w in behind]
            unproject(out, link_apply(link_in, colour, mu, ahead), mu, -1)
            unproject(out, behind, mu, 1)
        return out

    def each(function, *fields):
        return [[function(*(f[part][s] for f in fields)) for s in range(4)] for part in range(2)]

    def site_sum(pairs):
        total = None
        for left, right, sign in pairs:
            for s in range(4):
                term = left[s] * right[s]
                total = term if total is None else signed_add(total, sign, term)
        return total[0] + total[1] + total[2]

    def minimal_residual(colour):
        rho = load(resid, colour)
        answer = None
        for _ in range(MR_STEPS):
            image = block_wilson(rho, colour)
            sums = jnp.concatenate(
                [
                    site_sum([(image[0], rho[0], 1), (image[1], rho[1], 1)]),
                    site_sum([(image[0], rho[1], 1), (image[1], rho[0], -1)]),
                    site_sum([(image[0], image[0], 1), (image[1], image[1], 1)]),
                ],
                axis=0,
            )
            sums = split_dot(sums, block_weights)
            sums = [
                jnp.sum(sums[8 * i : 8 * i + 8], axis=0, keepdims=True) / block_entries
                for i in range(3)
            ]
            squares = sums[2] + mean_eps
            a_re = jnp.broadcast_to(sums[0] / squares, vreg)
            a_im = jnp.broadcast_to(sums[1] / squares, vreg)
            step = [
                [a_re * rho[0][s] - a_im * rho[1][s] for s in range(4)],
                [a_re * rho[1][s] + a_im * rho[0][s] for s in range(4)],
            ]
            answer = step if answer is None else each(jnp.add, answer, step)
            rho = [
                [rho[0][s] - (a_re * image[0][s] - a_im * image[1][s]) for s in range(4)],
                [rho[1][s] - (a_re * image[1][s] + a_im * image[0][s]) for s in range(4)],
            ]
        return answer, rho

    def flat(half):
        return jnp.concatenate([half[0].reshape(6, 8, 128), half[1].reshape(6, 8, 128)])

    def pack_x(half, face):
        groups = flat(half).reshape(3, 4, 8, 128)
        packed = None
        for j in range(4):
            moved = roll(groups[:, j], j - face, -2)
            packed = moved if j == 0 else jnp.where(x_pos == j, moved, packed)
        return packed

    def unpack_x(packed, face):
        rows = jnp.stack([roll(packed, face - j, -2) for j in range(4)], axis=1)
        rows = rows.reshape(2, 2, 3, 8, 128)
        return rows[0], rows[1]

    def pack_t(half, face, away):
        groups = flat(half).reshape(3, 4, 8, 128)
        here = (away == 0) if face == 0 else (away == 1)
        first = jnp.where(here, groups[:, 0], roll(groups[:, 1], 64, -1))
        second = jnp.where(here, groups[:, 2], roll(groups[:, 3], 64, -1))
        if face == 0:
            return jnp.where(t_low == 0, first, roll(second, 4, -2))
        return jnp.where(t_low == 1, first, roll(second, 4, -2))

    def unpack_t(packed):
        turned = roll(packed, 64, -1)
        rows = jnp.stack([roll(turned, 4, -2), roll(packed, 4, -2), turned, packed], axis=1)
        rows = rows.reshape(2, 2, 3, 8, 128)
        return rows[0], rows[1]

    def halo_copy(step, side):
        target = (ta_off(n_ta - 1), ta_off(1), xyz_off(n_xyz - 1), xyz_off(1))[side]
        return pltpu.make_async_remote_copy(
            src_ref=halo_out.at[step, side],
            dst_ref=halo_in.at[step, side],
            send_sem=halo_send.at[step, side],
            recv_sem=halo_recv.at[step, side],
            device_id=target,
            device_id_type=MESH,
        )

    def reduce_copies(slot):
        rows = [
            pltpu.make_async_remote_copy(
                src_ref=dot_out.at[slot],
                dst_ref=dot_row.at[slot, d - 1],
                send_sem=row_send.at[slot, d - 1],
                recv_sem=row_recv.at[slot, d - 1],
                device_id=xyz_off(d),
                device_id_type=MESH,
            )
            for d in range(1, n_xyz)
        ]
        cols = [
            pltpu.make_async_remote_copy(
                src_ref=dot_sum.at[slot],
                dst_ref=dot_col.at[slot, d - 1],
                send_sem=col_send.at[slot, d - 1],
                recv_sem=col_recv.at[slot, d - 1],
                device_id=ta_off(d),
                device_id_type=MESH,
            )
            for d in range(1, n_ta)
        ]
        return rows, cols

    loads[3].wait()
    trace_rows, trace_cols = reduce_copies(0)
    coarse_lane = iota((16, 128), 1)
    coarse_row = iota((16, 128), 0)
    on_diagonal = (coarse_lane % NVEC) == coarse_row
    trace = jnp.where(on_diagonal, coarse_ref[0, 0], f32(0.0))
    trace = jnp.sum(trace, axis=0, keepdims=True)
    trace = jnp.sum(trace, axis=1, keepdims=True) / f32(128 * n_ta * n_xyz)
    dot_out[0] = jnp.broadcast_to(trace, vreg)

    def stencil_copy(side):
        t_off, x_off = areas[1 + side]
        return pltpu.make_async_remote_copy(
            src_ref=coarse_ref,
            dst_ref=stencil_in.at[side],
            send_sem=stencil_send.at[side],
            recv_sem=stencil_recv.at[side],
            device_id=device_at(-t_off, -x_off),
            device_id_type=MESH,
        )

    def solve(colour):
        z, rho = minimal_residual(colour)
        for part in range(2):
            for s in range(4):
                z_ref[part, s] = z[part][s]
                resid[colour, part, s] = rho[part][s]
                smooth[colour, part, s] = smooth[colour, part, s] + z[part][s]

    def exchange(step, meanwhile):
        colour = lax.rem(step, 2)
        other = 1 - colour
        z = [[z_ref[part, s] for s in range(4)] for part in range(2)]
        away = jnp.where(colour == 0, t_high[0], t_high[1])
        halo_out[step, 1] = pack_t(link_apply_dagger(link_out, colour, 0, project(z, 0, 1)), 3, away)
        halo_out[step, 3] = pack_x(link_apply_dagger(link_out, colour, 1, project(z, 1, 1)), 3)
        halo_out[step, 0] = pack_t(project(z, 0, -1), 0, away)
        halo_out[step, 2] = pack_x(project(z, 1, -1), 0)
        copies = [halo_copy(step, side) for side in range(4)]
        for copy in copies[::-1]:
            copy.start()
        meanwhile(step)
        change = [[jnp.zeros((3, 8, 128), f32)] * 4 for _ in range(2)]
        for mu in (2, 3):
            ahead = project(z, mu, -1)
            behind = link_apply_dagger(link_out, colour, mu, project(z, mu, 1))
            if mu == 2:
                ahead = [roll(w, -16, -1) for w in ahead]
                behind = [roll(w, 16, -1) for w in behind]
            else:
                ahead = [jnp.where(z_pos == 15, roll(w, 15, -1), roll(w, -1, -1)) for w in ahead]
                behind = [jnp.where(z_pos == 0, roll(w, -15, -1), roll(w, 1, -1)) for w in behind]
            unproject(change, link_apply(link_out, other, mu, ahead), mu, -1)
            unproject(change, behind, mu, 1)
        for copy in copies:
            copy.wait()
        ahead = unpack_t(halo_in[step, 0])
        unproject(change, link_apply(link_out, other, 0, ahead), 0, -1)
        first = (away == 1) & (t_low == 0)
        behind = [jnp.where(first, w, f32(0.0)) for w in unpack_t(halo_in[step, 1])]
        unproject(change, behind, 0, 1)
        ahead = unpack_x(halo_in[step, 2], 3)
        unproject(change, link_apply(link_out, other, 1, ahead), 1, -1)
        behind = [jnp.where(x_pos == 0, w, f32(0.0)) for w in unpack_x(halo_in[step, 3], 0)]
        unproject(change, behind, 1, 1)
        for part in range(2):
            for s in range(4):
                resid[other, part, s] = resid[other, part, s] - change[part][s]

    def background(step):
        @pl.when(step == 0)
        def _():
            for copy in stencil_copies + trace_rows:
                copy.start()

        @pl.when(step == 1)
        def _():
            for copy in trace_rows:
                copy.wait()
            total = dot_out[0]
            for d in range(n_xyz - 1):
                total = total + dot_row[0, d]
            dot_sum[0] = total
            for copy in trace_cols:
                copy.start()

    def half_step(step, carry):
        exchange(step, background)
        solve(1 - lax.rem(step, 2))
        return carry

    areas = [(0, 0), (1, 0), (-1, 0), (0, 1), (0, -1)]
    stencil_copies = [stencil_copy(side) for side in range(4)]
    solve(0)
    pl.semaphore_wait(barrier, len(peers))
    lax.fori_loop(0, HALF_STEPS - 1, half_step, 0)
    exchange(HALF_STEPS - 1, lambda step: None)

    loads[4].wait()
    natural = expand(resid[0].reshape(24, 8, 128), resid[1].reshape(24, 8, 128))

    def restrict(a, carry):
        basis = null_ref[a].astype(f32)
        acc_re = acc_im = None
        for i, half in enumerate(natural):
            b_re = basis[0, :, 8 * i : 8 * i + 8]
            b_im = basis[1, :, 8 * i : 8 * i + 8]
            term_re = jnp.sum(b_re * half[:12] + b_im * half[12:], axis=0)
            term_im = jnp.sum(b_re * half[12:] - b_im * half[:12], axis=0)
            acc_re = term_re if i == 0 else acc_re + term_re
            acc_im = term_im if i == 0 else acc_im + term_im
        partial[0, a] = acc_re
        partial[1, a] = acc_im
        return carry

    lax.fori_loop(0, NVEC, restrict, 0)
    site_agg = 4 * (into // 64) + (into % 16) // 4
    to_agg = (site_agg == outof // NVEC).astype(f32).astype(jnp.bfloat16)
    site_agg = 4 * (outof // 64) + (outof % 16) // 4
    from_agg = (site_agg == into // NVEC).astype(f32).astype(jnp.bfloat16)
    agg_weights = (into // NVEC == outof // NVEC).astype(f32).astype(jnp.bfloat16)
    rows = jnp.sum(partial[...], axis=2).reshape(32, 128)

    def diagonal_row(both):
        return [
            jnp.sum(
                jnp.where(on_diagonal, both[16 * i : 16 * i + 16], f32(0.0)),
                axis=0,
                keepdims=True,
            )
            for i in range(2)
        ]

    vec = diagonal_row(split_dot(rows, to_agg))

    for copy in trace_cols:
        copy.wait()
    total = dot_sum[0]
    for d in range(n_ta - 1):
        total = total + dot_col[0, d]
    shift = total

    row_at = iota(vreg, 0)
    agg_z = (lane % 64) // NVEC
    diag_shift = jnp.where(on_diagonal, jnp.broadcast_to(shift[:1], (16, 128)), f32(0.0))

    def tile(row_re, row_im):
        return jnp.where(
            row_at == 0, jnp.broadcast_to(row_re, vreg), jnp.broadcast_to(row_im, vreg)
        )

    near = [(0, -1), (0, 1), (1, 0), (-1, 0)]
    far = [(0, 2), (0, -2), (1, 1), (1, -1), (-1, 1), (-1, -1), (2, 0), (-2, 0)]
    around = far + near

    def cvec_copy(k, slot):
        t_off, x_off = around[slot]
        return pltpu.make_async_remote_copy(
            src_ref=cvec_out.at[k],
            dst_ref=cvec_in.at[k, slot],
            send_sem=cvec_send.at[k, slot],
            recv_sem=cvec_recv.at[k, slot],
            device_id=device_at(-t_off, -x_off),
            device_id_type=MESH,
        )

    def stencil_of(area, k):
        if area == 0:
            return coarse_ref[k, 0], coarse_ref[k, 1]
        return stencil_in[area - 1, k, 0], stencil_in[area - 1, k, 1]

    def add_term(acc, matrix, vec):
        m_re, m_im = matrix
        v_re, v_im = vec[0:1], vec[1:2]
        now = (m_re * v_re - m_im * v_im, m_re * v_im + m_im * v_re)
        return now if acc is None else (acc[0] + now[0], acc[1] + now[1])

    def local_terms(area, vec):
        m_re, m_im = stencil_of(area, 0)
        acc = add_term(None, (m_re - diag_shift, m_im), vec)
        over = roll(vec, 64, -1)
        p_re, p_im = stencil_of(area, 5)
        q_re, q_im = stencil_of(area, 6)
        acc = add_term(acc, (p_re + q_re, p_im + q_im), over)
        ahead = jnp.where(agg_z == 3, roll(vec, 48, -1), roll(vec, -16, -1))
        behind = jnp.where(agg_z == 0, roll(vec, -48, -1), roll(vec, 16, -1))
        acc = add_term(acc, stencil_of(area, 7), ahead)
        return add_term(acc, stencil_of(area, 8), behind)

    def finish(accs):
        rows = jnp.concatenate([w for acc in accs for w in acc], axis=0)
        rows = split_dot(rows, agg_weights)
        return [tile(*diagonal_row(rows[32 * i : 32 * i + 32])) for i in range(len(accs))]

    vecs = [tile(*vec)]
    for pair_at in range(GCR_ITERS // 2):
        own = vecs[-1]
        cvec_out[pair_at] = own
        copies = [cvec_copy(pair_at, slot) for slot in range(len(around))]
        for copy in copies:
            copy.start()
        accs = [local_terms(0, own)]
        if pair_at == 0:
            for copy in stencil_copies:
                copy.wait()
        for copy in copies:
            copy.wait()
        have = {(0, 0): own}
        for slot, place in enumerate(around):
            have[place] = cvec_in[pair_at, slot]
        for area in range(1, 5):
            accs.append(local_terms(area, have[areas[area]]))
        for area, (t_off, x_off) in enumerate(areas):
            for side in range(4):
                t_step, x_step = areas[1 + side]
                there = have[(t_off + t_step, x_off + x_step)]
                accs[area] = add_term(accs[area], stencil_of(area, 1 + side), there)
        nexts = finish(accs)
        acc = local_terms(0, nexts[0])
        for side in range(4):
            acc = add_term(acc, stencil_of(0, 1 + side), nexts[1 + side])
        vecs = vecs + [nexts[0]] + finish([acc])

    basis_re = basis_im = jnp.zeros(vreg, f32)
    for k, vec in enumerate(vecs):
        basis_re = jnp.where(row_at == k, jnp.broadcast_to(vec[0:1], vreg), basis_re)
        basis_im = jnp.where(row_at == k, jnp.broadcast_to(vec[1:2], vreg), basis_im)

    gram = jnp.zeros(vreg, f32)
    for k in range(GCR_ITERS + 1):
        k_re = basis_re[k : k + 1]
        k_im = basis_im[k : k + 1]
        dot_re = jnp.sum(basis_re * k_re + basis_im * k_im, axis=1, keepdims=True)
        dot_im = jnp.sum(basis_re * k_im - basis_im * k_re, axis=1, keepdims=True)
        gram = jnp.where(lane == 2 * k, jnp.broadcast_to(dot_re, vreg), gram)
        gram = jnp.where(lane == 2 * k + 1, jnp.broadcast_to(dot_im, vreg), gram)
    gram_rows, gram_cols = reduce_copies(1)
    dot_out[1] = gram
    for copy in gram_rows:
        copy.start()

    diag_rows = jnp.concatenate(
        [
            jnp.where(on_diagonal, jnp.broadcast_to(vec[part : part + 1], (16, 128)), f32(0.0))
            for vec in vecs[:GCR_ITERS]
            for part in range(2)
        ],
        axis=0,
    )
    spread[...] = split_dot(diag_rows, from_agg).reshape(GCR_ITERS, 2, NVEC, 1, 128)

    def prolong(entry, carry):
        n_re = null_ref[:, 0, entry].astype(f32)
        n_im = null_ref[:, 1, entry].astype(f32)
        for k in range(GCR_ITERS):
            e_re = spread[k, 0]
            e_im = spread[k, 1]
            prolonged[k, entry] = jnp.sum(n_re * e_re - n_im * e_im, axis=0)
            prolonged[k, 12 + entry] = jnp.sum(n_re * e_im + n_im * e_re, axis=0)
        return carry

    lax.fori_loop(0, 12, prolong, 0)
    halves = expand(smooth[0].reshape(24, 8, 128), smooth[1].reshape(24, 8, 128))
    for i, half in enumerate(halves):
        out_ref[:, 8 * i : 8 * i + 8] = half

    for d, copy in enumerate(gram_rows):
        copy.wait()
        gram = gram + dot_row[1, d]
    dot_sum[1] = gram
    for copy in gram_cols:
        copy.start()
    for d, copy in enumerate(gram_cols):
        copy.wait()
        gram = gram + dot_col[1, d]

    columns = []
    for k in range(GCR_ITERS + 1):
        columns.append(
            (
                jnp.broadcast_to(gram[:, 2 * k : 2 * k + 1], vreg),
                jnp.broadcast_to(gram[:, 2 * k + 1 : 2 * k + 2], vreg),
            )
        )

    def gram_apply(x):
        out = None
        for k, (g_re, g_im) in enumerate(columns):
            x_re = jnp.broadcast_to(x[0][k : k + 1], vreg)
            x_im = jnp.broadcast_to(x[1][k : k + 1], vreg)
            now = (g_re * x_re - g_im * x_im, g_re * x_im + g_im * x_re)
            out = now if out is None else (out[0] + now[0], out[1] + now[1])
        return out

    def row_sum(value):
        return jnp.broadcast_to(jnp.sum(value, axis=0, keepdims=True), vreg)

    def inner(left, image):
        return (
            row_sum(left[0] * image[0] + left[1] * image[1]),
            row_sum(left[0] * image[1] - left[1] * image[0]),
        )

    def scaled(a, x):
        return (a[0] * x[0] - a[1] * x[1], a[0] * x[1] + a[1] * x[0])

    def minus(x, y):
        return (x[0] - y[0], x[1] - y[1])

    remain = (jnp.where(row_at == 0, f32(1.0), f32(0.0)), jnp.zeros(vreg, f32))
    answer = (jnp.zeros(vreg, f32), jnp.zeros(vreg, f32))
    past = []
    for iteration in range(GCR_ITERS):
        direction = remain
        image = tuple(roll(w, 1, -2) + shift * w for w in direction)
        image_dots = gram_apply(image)
        margins = [inner(unit_image, image_dots) for _, unit_image in past]
        for margin, (unit_direction, unit_image) in zip(margins, past):
            image = minus(image, scaled(margin, unit_image))
            direction = minus(direction, scaled(margin, unit_direction))
        if past:
            image_dots = gram_apply(image)
        squares = jnp.maximum(inner(image, image_dots)[0], f32(0.0))
        along = inner(remain, image_dots)
        inverse = 1.0 / jnp.sqrt(squares + mean_eps)
        unit_image = tuple(w * inverse for w in image)
        unit_direction = tuple(w * inverse for w in direction)
        step = (along[0] * inverse, -(along[1] * inverse))
        moved = scaled(step, unit_direction)
        answer = (answer[0] + moved[0], answer[1] + moved[1])
        remain = minus(remain, scaled(step, unit_image))
        past.append((unit_direction, unit_image))

    error = scaled(answer, (basis_re, basis_im))
    error = [jnp.sum(w, axis=0, keepdims=True) for w in error]
    error_ref[0:1] = error[0]
    error_ref[1:2] = error[1]

    for k in range(GCR_ITERS):
        c_re = answer[0][k : k + 1]
        c_im = answer[1][k : k + 1]
        w_re = prolonged[k, :12]
        w_im = prolonged[k, 12:]
        now_re = c_re * w_re - c_im * w_im
        now_im = c_re * w_im + c_im * w_re
        sum_re = now_re if k == 0 else sum_re + now_re
        sum_im = now_im if k == 0 else sum_im + now_im
    out_ref[:12] = out_ref[:12] + sum_re
    out_ref[12:] = out_ref[12:] + sum_im


def solution(mesh):
    n_ta, n_xyz = mesh.shape["ta"], mesh.shape["xyz"]

    def shards(source, gauge_links, clover_raw, null_vectors, coarse_operator):
        f32 = jnp.float32
        dma = pltpu.SemaphoreType.DMA
        field, error = pl.pallas_call(
            functools.partial(kernel, n_ta, n_xyz),
            out_shape=(
                jax.ShapeDtypeStruct((24, 16, 128), f32),
                jax.ShapeDtypeStruct((2, 128), f32),
            ),
            in_specs=[pl.BlockSpec(memory_space=pltpu.HBM)] * 5,
            out_specs=(pl.BlockSpec(memory_space=pltpu.VMEM),) * 2,
            scratch_shapes=[
                pltpu.VMEM((24, 16, 128), f32),
                pltpu.VMEM((72, 16, 128), jnp.bfloat16),
                pltpu.VMEM((144, 16, 128), jnp.bfloat16),
                pltpu.VMEM((NVEC, 2, 12, 16, 128), jnp.bfloat16),
                pltpu.VMEM((9, 2, NVEC, 128), f32),
                pltpu.VMEM((2, 4, 2, 3, 3, 8, 128), f32),
                pltpu.VMEM((2, 4, 2, 3, 3, 8, 128), f32),
                pltpu.VMEM((2, 2, 2, 6, 6, 8, 128), f32),
                pltpu.VMEM((2, 2, 4, 3, 8, 128), f32),
                pltpu.VMEM((2, 2, 4, 3, 8, 128), f32),
                pltpu.VMEM((2, 4, 3, 8, 128), f32),
                pltpu.VMEM((HALF_STEPS, 4, 3, 8, 128), f32),
                pltpu.VMEM((HALF_STEPS, 4, 3, 8, 128), f32),
                pltpu.VMEM((2, NVEC, 8, 128), f32),
                pltpu.VMEM((GCR_ITERS, 2, NVEC, 1, 128), f32),
                pltpu.VMEM((GCR_ITERS, 24, 16, 128), f32),
                pltpu.VMEM((4, 9, 2, NVEC, 128), f32),
                pltpu.VMEM((GCR_ITERS // 2, 8, 128), f32),
                pltpu.VMEM((GCR_ITERS // 2, 12, 8, 128), f32),
                pltpu.VMEM((2, 8, 128), f32),
                pltpu.VMEM((2, n_xyz - 1, 8, 128), f32),
                pltpu.VMEM((2, 8, 128), f32),
                pltpu.VMEM((2, n_ta - 1, 8, 128), f32),
                dma((5,)),
                dma((HALF_STEPS, 4)),
                dma((HALF_STEPS, 4)),
                dma((4,)),
                dma((4,)),
                dma((GCR_ITERS // 2, 12)),
                dma((GCR_ITERS // 2, 12)),
                dma((2, n_xyz - 1)),
                dma((2, n_xyz - 1)),
                dma((2, n_ta - 1)),
                dma((2, n_ta - 1)),
            ],
            compiler_params=pltpu.CompilerParams(
                collective_id=0, has_side_effects=True, vmem_limit_bytes=60 * 2**20
            ),
        )(
            source.reshape(24, 16, 128),
            gauge_links.reshape(72, 16, 128),
            clover_raw.reshape(144, 16, 128),
            null_vectors.reshape(NVEC, 2, 12, 16, 128),
            coarse_operator,
        )
        return field.reshape(source.shape), error

    in_specs = (
        P(None, None, None, "ta", "xyz", None),
        P(None, None, None, None, "ta", "xyz", None),
        P(None, None, None, None, "ta", "xyz", None),
        P(None, None, None, None, "ta", "xyz", None),
        P(None, None, None, ("ta", "xyz")),
    )
    out_specs = (P(None, None, None, "ta", "xyz", None), P(None, ("ta", "xyz")))
    return jax.shard_map(shards, mesh=mesh, in_specs=in_specs, out_specs=out_specs, check_vma=False)
```

```python
import functools

import jax
import jax.numpy as jnp
from jax import lax
from jax.experimental import pallas as pl
from jax.experimental.pallas import tpu as pltpu
from jax.sharding import PartitionSpec as P

MESH = pl.DeviceIdType.MESH
NVEC = 16
MR_STEPS = 2
SAP_CYCLES = 2
GCR_ITERS = 4
HALF_STEPS = 2 * SAP_CYCLES

mass_shift = 0.2
mean_eps = 1e-06
block_entries = 6144.0

gamma_perm = [[2, 3, 0, 1], [3, 2, 1, 0], [3, 2, 1, 0], [2, 3, 0, 1]]
gamma_real = [[1, 1, 1, 1], [0, 0, 0, 0], [-1, 1, 1, -1], [0, 0, 0, 0]]
gamma_imag = [[0, 0, 0, 0], [1, 1, -1, -1], [0, 0, 0, 0], [1, -1, -1, 1]]


def roll(value, shift, axis):
    axis = value.ndim + axis
    size = value.shape[axis]
    return pltpu.roll(value, shift % size, axis)


def signed_add(base, sign, value):
    return base + value if sign > 0 else base - value


def project(v, mu, sign):
    half_re, half_im = [], []
    for s in range(2):
        q = gamma_perm[mu][s]
        if gamma_real[mu][s]:
            w = sign * gamma_real[mu][s]
            half_re.append(signed_add(v[0][s], w, v[0][q]))
            half_im.append(signed_add(v[1][s], w, v[1][q]))
        else:
            w = sign * gamma_imag[mu][s]
            half_re.append(signed_add(v[0][s], -w, v[1][q]))
            half_im.append(signed_add(v[1][s], w, v[0][q]))
    return jnp.stack(half_re), jnp.stack(half_im)


def unproject(out, half, mu, sign):
    half_re, half_im = half
    for s in range(2):
        out[0][s] = out[0][s] + half_re[s]
        out[1][s] = out[1][s] + half_im[s]
    for s in range(2, 4):
        q = gamma_perm[mu][s]
        if gamma_real[mu][s]:
            w = sign * gamma_real[mu][s]
            out[0][s] = signed_add(out[0][s], w, half_re[q])
            out[1][s] = signed_add(out[1][s], w, half_im[q])
        else:
            w = sign * gamma_imag[mu][s]
            out[0][s] = signed_add(out[0][s], -w, half_im[q])
            out[1][s] = signed_add(out[1][s], w, half_re[q])


def link_apply(links, colour, mu, half):
    half_re, half_im = half
    out_re = out_im = None
    for b in range(3):
        u_re = links[colour, mu, 0, b][None]
        u_im = links[colour, mu, 1, b][None]
        h_re = half_re[:, b][:, None]
        h_im = half_im[:, b][:, None]
        term_re = u_re * h_re - u_im * h_im
        term_im = u_re * h_im + u_im * h_re
        out_re = term_re if b == 0 else out_re + term_re
        out_im = term_im if b == 0 else out_im + term_im
    return out_re, out_im


def link_apply_dagger(links, colour, mu, half):
    half_re, half_im = half
    out_re = out_im = None
    for b in range(3):
        u_re = links[colour, mu, 0, :, b][None]
        u_im = links[colour, mu, 1, :, b][None]
        h_re = half_re[:, b][:, None]
        h_im = half_im[:, b][:, None]
        term_re = u_re * h_re + u_im * h_im
        term_im = u_re * h_im - u_im * h_re
        out_re = term_re if b == 0 else out_re + term_re
        out_im = term_im if b == 0 else out_im + term_im
    return out_re, out_im


def split_dot(value, weights):
    rows = value.shape[0]
    high = value.astype(jnp.bfloat16)
    rest = value - high.astype(jnp.float32)
    mid = rest.astype(jnp.bfloat16)
    low = (rest - mid.astype(jnp.float32)).astype(jnp.bfloat16)
    out = jnp.dot(
        jnp.concatenate([high, mid, low], axis=0), weights, preferred_element_type=jnp.float32
    )
    return out[:rows] + out[rows : 2 * rows] + out[2 * rows :]


def iota(shape, dim):
    return lax.broadcasted_iota(jnp.int32, shape, dim)


def kernel(
    n_ta, n_xyz,
    source_hbm, gauge_hbm, clover_hbm, null_hbm, coarse_hbm,
    out_ref, error_ref,
    source_ref, gauge_ref, clover_ref, null_ref, coarse_ref,
    link_in, link_out, herm, resid, smooth, z_ref,
    halo_out, halo_in, partial, spread, prolonged,
    stencil_in, cvec_out, cvec_in, dot_out, dot_in,
    load_sem, halo_send, halo_recv, stencil_send, stencil_recv, cvec_send, cvec_recv,
    dot_send, dot_recv,
):
    f32 = jnp.float32
    ta = lax.axis_index("ta")
    xyz = lax.axis_index("xyz")

    loads = [
        pltpu.make_async_copy(src, dst, load_sem.at[i])
        for i, (src, dst) in enumerate(
            [
                (gauge_hbm, gauge_ref),
                (clover_hbm, clover_ref),
                (source_hbm, source_ref),
                (coarse_hbm, coarse_ref),
                (null_hbm, null_ref),
            ]
        )
    ]
    for load in loads[:-1]:
        load.start()

    def device_at(t_off, x_off):
        return (lax.rem(ta + t_off + n_ta, n_ta), lax.rem(xyz + x_off + n_xyz, n_xyz))

    def depth_peer(d):
        low = lax.rem(xyz, n_low)
        return (ta, xyz - low + lax.rem(low + d, n_low))

    def plane_peer(d):
        return (lax.rem(ta + d, n_ta), lax.rem(xyz + n_low * (d // n_ta), n_xyz))

    n_low = n_xyz // 2
    groups = [
        [depth_peer(d) for d in range(1, n_low)],
        [plane_peer(d) for d in range(1, 2 * n_ta)],
    ]
    close = [(0, 1), (0, -1), (0, 2), (0, -2), (1, 1), (1, -1), (-1, 1), (-1, -1)]
    peers = groups[0] + groups[1] + [device_at(*place) for place in close]
    barrier = pltpu.get_barrier_semaphore()
    for peer in peers:
        pl.semaphore_signal(barrier, inc=1, device_id=peer, device_id_type=MESH)

    vreg = (8, 128)
    lane = iota(vreg, 1)
    subl = iota(vreg, 0)
    t_low = subl // 4
    x_pos = subl % 4
    y_pos = lane // 16
    z_pos = lane % 16
    parity = (ta + xyz + y_pos // 4 + z_pos // 4) % 2
    t_high = [parity, 1 - parity]

    def compact(natural):
        first = natural[..., :8, :]
        second = roll(natural[..., 8:, :], 64, -1)
        low = jnp.broadcast_to(parity == 0, first.shape)
        return jnp.where(low, first, second), jnp.where(low, second, first)

    def expand(even, odd):
        low = jnp.broadcast_to(parity == 0, even.shape)
        return jnp.where(low, even, odd), roll(jnp.where(low, odd, even), 64, -1)

    loads[0].wait()
    t_sign = jnp.where(ta == n_ta - 1, f32(0.5), f32(-0.5))
    for mu in range(4):
        planes = gauge_ref[pl.ds(18 * mu, 18)].astype(f32)
        pair = compact(planes)
        for colour in range(2):
            if mu == 0:
                inside = jnp.logical_not((t_high[colour] == 1) & (t_low == 1))
            elif mu == 1:
                inside = x_pos != 3
            elif mu == 2:
                inside = y_pos % 4 != 3
            else:
                inside = z_pos % 4 != 3
            weight_in = jnp.where(inside, f32(-0.5), f32(0.0))
            weight_out = jnp.where(inside, f32(0.0), t_sign if mu == 0 else f32(-0.5))
            for part in range(2):
                for row in range(3):
                    first = 9 * part + 3 * row
                    mine = pair[colour][first : first + 3]
                    link_in[colour, mu, part, :, row] = mine * weight_in
                    link_out[colour, mu, part, :, row] = mine * weight_out

    loads[1].wait()
    for chi in range(2):
        for col in range(6):
            row_at = 36 * chi + 6 * col
            for part in range(2):
                base = 72 * part
                line = clover_ref[pl.ds(base + row_at, 6)].astype(f32)
                column = jnp.stack(
                    [clover_ref[base + 36 * chi + 6 * r + col].astype(f32) for r in range(6)]
                )
                if part == 0:
                    sym = 0.5 * (column + line)
                    diag = iota((6, 1, 1), 0) == col
                    sym = sym + jnp.where(diag, f32(4.0 + mass_shift), f32(0.0))
                else:
                    sym = 0.5 * (column - line)
                pair = compact(sym)
                for colour in range(2):
                    herm[colour, part, chi, col] = pair[colour]

    loads[2].wait()
    pair = compact(source_ref[...])
    for colour in range(2):
        resid[colour] = pair[colour].reshape(2, 4, 3, 8, 128)
    smooth[...] = jnp.zeros_like(smooth)

    square = (128, 128)
    into = iota(square, 0)
    outof = iota(square, 1)
    block_weights = ((into % 16) // 4 == (outof % 16) // 4).astype(f32).astype(jnp.bfloat16)

    def load(ref, colour):
        value = ref[colour]
        return [[value[part, s] for s in range(4)] for part in range(2)]

    def block_wilson(v, colour):
        out = [[None] * 4, [None] * 4]
        for chi in range(2):
            v_re = jnp.concatenate([v[0][2 * chi], v[0][2 * chi + 1]])
            v_im = jnp.concatenate([v[1][2 * chi], v[1][2 * chi + 1]])
            acc_re = acc_im = None
            for col in range(6):
                h_re = herm[colour, 0, chi, col]
                h_im = herm[colour, 1, chi, col]
                term_re = h_re * v_re[col][None] - h_im * v_im[col][None]
                term_im = h_re * v_im[col][None] + h_im * v_re[col][None]
                acc_re = term_re if col == 0 else acc_re + term_re
                acc_im = term_im if col == 0 else acc_im + term_im
            for half in range(2):
                out[0][2 * chi + half] = acc_re[3 * half : 3 * half + 3]
                out[1][2 * chi + half] = acc_im[3 * half : 3 * half + 3]
        low = t_low == 0
        for mu in range(4):
            ahead = project(v, mu, -1)
            behind = link_apply_dagger(link_in, colour, mu, project(v, mu, 1))
            if mu == 0:
                ahead = [
                    roll(jnp.where(low, roll(w, 64, -1), w), 4, -2) for w in ahead
                ]
                behind = [
                    roll(jnp.where(low, w, roll(w, 64, -1)), 4, -2) for w in behind
                ]
            elif mu == 1:
                ahead = [roll(w, -1, -2) for w in ahead]
                behind = [roll(w, 1, -2) for w in behind]
            else:
                step = 16 if mu == 2 else 1
                ahead = [roll(w, -step, -1) for w in ahead]
                behind = [roll(w, step, -1) for w in behind]
            unproject(out, link_apply(link_in, colour, mu, ahead), mu, -1)
            unproject(out, behind, mu, 1)
        return out

    def each(function, *fields):
        return [[function(*(f[part][s] for f in fields)) for s in range(4)] for part in range(2)]

    def site_sum(pairs):
        total = None
        for left, right, sign in pairs:
            for s in range(4):
                term = left[s] * right[s]
                total = term if total is None else signed_add(total, sign, term)
        return total[0] + total[1] + total[2]

    def minimal_residual(colour):
        rho = load(resid, colour)
        answer = None
        for _ in range(MR_STEPS):
            image = block_wilson(rho, colour)
            sums = jnp.concatenate(
                [
                    site_sum([(image[0], rho[0], 1), (image[1], rho[1], 1)]),
                    site_sum([(image[0], rho[1], 1), (image[1], rho[0], -1)]),
                    site_sum([(image[0], image[0], 1), (image[1], image[1], 1)]),
                ],
                axis=0,
            )
            sums = split_dot(sums, block_weights)
            sums = [
                jnp.sum(sums[8 * i : 8 * i + 8], axis=0, keepdims=True) / block_entries
                for i in range(3)
            ]
            squares = sums[2] + mean_eps
            a_re = jnp.broadcast_to(sums[0] / squares, vreg)
            a_im = jnp.broadcast_to(sums[1] / squares, vreg)
            step = [
                [a_re * rho[0][s] - a_im * rho[1][s] for s in range(4)],
                [a_re * rho[1][s] + a_im * rho[0][s] for s in range(4)],
            ]
            answer = step if answer is None else each(jnp.add, answer, step)
            rho = [
                [rho[0][s] - (a_re * image[0][s] - a_im * image[1][s]) for s in range(4)],
                [rho[1][s] - (a_re * image[1][s] + a_im * image[0][s]) for s in range(4)],
            ]
        return answer, rho

    def flat(half):
        return jnp.concatenate([half[0].reshape(6, 8, 128), half[1].reshape(6, 8, 128)])

    def pack_x(half, face):
        groups = flat(half).reshape(3, 4, 8, 128)
        packed = None
        for j in range(4):
            moved = roll(groups[:, j], j - face, -2)
            packed = moved if j == 0 else jnp.where(x_pos == j, moved, packed)
        return packed

    def unpack_x(packed, face):
        rows = jnp.stack([roll(packed, face - j, -2) for j in range(4)], axis=1)
        rows = rows.reshape(2, 2, 3, 8, 128)
        return rows[0], rows[1]

    def pack_t(half, face, away):
        groups = flat(half).reshape(3, 4, 8, 128)
        here = (away == 0) if face == 0 else (away == 1)
        first = jnp.where(here, groups[:, 0], roll(groups[:, 1], 64, -1))
        second = jnp.where(here, groups[:, 2], roll(groups[:, 3], 64, -1))
        if face == 0:
            return jnp.where(t_low == 0, first, roll(second, 4, -2))
        return jnp.where(t_low == 1, first, roll(second, 4, -2))

    def unpack_t(packed):
        turned = roll(packed, 64, -1)
        rows = jnp.stack([roll(turned, 4, -2), roll(packed, 4, -2), turned, packed], axis=1)
        rows = rows.reshape(2, 2, 3, 8, 128)
        return rows[0], rows[1]

    def halo_copy(step, side):
        target = device_at(*((-1, 0), (1, 0), (0, -1), (0, 1))[side])
        return pltpu.make_async_remote_copy(
            src_ref=halo_out.at[step, side],
            dst_ref=halo_in.at[step, side],
            send_sem=halo_send.at[step, side],
            recv_sem=halo_recv.at[step, side],
            device_id=target,
            device_id_type=MESH,
        )

    def reduce_start(slot, stage, value):
        dot_out[slot, stage] = value
        for i, peer in enumerate(groups[stage]):
            pltpu.make_async_remote_copy(
                src_ref=dot_out.at[slot, stage],
                dst_ref=dot_in.at[slot, stage_at[stage] + i],
                send_sem=dot_send.at[slot, stage],
                recv_sem=dot_recv.at[slot, stage],
                device_id=peer,
                device_id_type=MESH,
            ).start()

    def reduce_finish(slot, stage):
        count = len(groups[stage])
        arrived = dot_in.at[slot, pl.ds(stage_at[stage], count)]
        pltpu.make_async_remote_copy(
            src_ref=arrived,
            dst_ref=arrived,
            send_sem=dot_send.at[slot, stage],
            recv_sem=dot_recv.at[slot, stage],
            device_id=groups[stage][0],
            device_id_type=MESH,
        ).wait()
        first = stage_at[stage]
        return dot_out[slot, stage] + jnp.sum(dot_in[slot, first : first + count], axis=0)

    stage_at = [0, n_low - 1]

    loads[3].wait()
    coarse_lane = iota((16, 128), 1)
    coarse_row = iota((16, 128), 0)
    on_diagonal = (coarse_lane % NVEC) == coarse_row
    trace = jnp.where(on_diagonal, coarse_ref[0, 0], f32(0.0))
    trace = jnp.sum(trace, axis=0, keepdims=True)
    trace = jnp.sum(trace, axis=1, keepdims=True) / f32(128 * n_ta * n_xyz)
    trace = jnp.broadcast_to(trace, vreg)

    def stencil_copy(part, side):
        t_off, x_off = areas[1 + side]
        third = pl.ds(3 * part, 3)
        return pltpu.make_async_remote_copy(
            src_ref=coarse_ref.at[third],
            dst_ref=stencil_in.at[side, third],
            send_sem=stencil_send.at[part, side],
            recv_sem=stencil_recv.at[part, side],
            device_id=device_at(-t_off, -x_off),
            device_id_type=MESH,
        )

    def solve(colour):
        z, rho = minimal_residual(colour)
        for part in range(2):
            for s in range(4):
                z_ref[part, s] = z[part][s]
                resid[colour, part, s] = rho[part][s]
                smooth[colour, part, s] = smooth[colour, part, s] + z[part][s]

    def exchange(step, meanwhile):
        colour = lax.rem(step, 2)
        other = 1 - colour
        z = [[z_ref[part, s] for s in range(4)] for part in range(2)]
        away = jnp.where(colour == 0, t_high[0], t_high[1])
        halo_out[step, 1] = pack_t(link_apply_dagger(link_out, colour, 0, project(z, 0, 1)), 3, away)
        halo_out[step, 3] = pack_x(link_apply_dagger(link_out, colour, 1, project(z, 1, 1)), 3)
        halo_out[step, 0] = pack_t(project(z, 0, -1), 0, away)
        halo_out[step, 2] = pack_x(project(z, 1, -1), 0)
        copies = [halo_copy(step, side) for side in range(4)]
        for copy in copies[::-1]:
            copy.start()
        meanwhile(step)
        change = [[jnp.zeros((3, 8, 128), f32)] * 4 for _ in range(2)]
        for mu in (2, 3):
            ahead = project(z, mu, -1)
            behind = link_apply_dagger(link_out, colour, mu, project(z, mu, 1))
            if mu == 2:
                ahead = [roll(w, -16, -1) for w in ahead]
                behind = [roll(w, 16, -1) for w in behind]
            else:
                ahead = [jnp.where(z_pos == 15, roll(w, 15, -1), roll(w, -1, -1)) for w in ahead]
                behind = [jnp.where(z_pos == 0, roll(w, -15, -1), roll(w, 1, -1)) for w in behind]
            unproject(change, link_apply(link_out, other, mu, ahead), mu, -1)
            unproject(change, behind, mu, 1)
        for copy in copies:
            copy.wait()
        ahead = unpack_t(halo_in[step, 0])
        unproject(change, link_apply(link_out, other, 0, ahead), 0, -1)
        first = (away == 1) & (t_low == 0)
        behind = [jnp.where(first, w, f32(0.0)) for w in unpack_t(halo_in[step, 1])]
        unproject(change, behind, 0, 1)
        ahead = unpack_x(halo_in[step, 2], 3)
        unproject(change, link_apply(link_out, other, 1, ahead), 1, -1)
        behind = [jnp.where(x_pos == 0, w, f32(0.0)) for w in unpack_x(halo_in[step, 3], 0)]
        unproject(change, behind, 1, 1)
        for part in range(2):
            for s in range(4):
                resid[other, part, s] = resid[other, part, s] - change[part][s]

    def background(step):
        for side in range(4):
            stencil_copy(step, side).start()

        @pl.when(step == 0)
        def _():
            reduce_start(0, 0, trace)

        @pl.when(step == 1)
        def _():
            reduce_start(0, 1, reduce_finish(0, 0))

    def half_step(step, carry):
        exchange(step, background)
        solve(1 - lax.rem(step, 2))
        return carry

    areas = [(0, 0), (1, 0), (-1, 0), (0, 1), (0, -1)]
    loads[4].start()
    solve(0)
    pl.semaphore_wait(barrier, len(peers))
    lax.fori_loop(0, HALF_STEPS - 1, half_step, 0)
    exchange(HALF_STEPS - 1, lambda step: None)

    loads[4].wait()
    natural = expand(resid[0].reshape(24, 8, 128), resid[1].reshape(24, 8, 128))

    def restrict(a, carry):
        basis = null_ref[a].astype(f32)
        acc_re = acc_im = None
        for i, half in enumerate(natural):
            b_re = basis[0, :, 8 * i : 8 * i + 8]
            b_im = basis[1, :, 8 * i : 8 * i + 8]
            term_re = jnp.sum(b_re * half[:12] + b_im * half[12:], axis=0)
            term_im = jnp.sum(b_re * half[12:] - b_im * half[:12], axis=0)
            acc_re = term_re if i == 0 else acc_re + term_re
            acc_im = term_im if i == 0 else acc_im + term_im
        partial[0, a] = acc_re
        partial[1, a] = acc_im
        return carry

    lax.fori_loop(0, NVEC, restrict, 0)
    site_agg = 4 * (into // 64) + (into % 16) // 4
    to_agg = (site_agg == outof // NVEC).astype(f32).astype(jnp.bfloat16)
    site_agg = 4 * (outof // 64) + (outof % 16) // 4
    from_agg = (site_agg == into // NVEC).astype(f32).astype(jnp.bfloat16)
    agg_weights = (into // NVEC == outof // NVEC).astype(f32).astype(jnp.bfloat16)
    rows = jnp.sum(partial[...], axis=2).reshape(32, 128)

    def diagonal_row(both):
        return [
            jnp.sum(
                jnp.where(on_diagonal, both[16 * i : 16 * i + 16], f32(0.0)),
                axis=0,
                keepdims=True,
            )
            for i in range(2)
        ]

    vec = diagonal_row(split_dot(rows, to_agg))

    shift = reduce_finish(0, 1)

    row_at = iota(vreg, 0)
    agg_z = (lane % 64) // NVEC
    diag_shift = jnp.where(on_diagonal, jnp.broadcast_to(shift[:1], (16, 128)), f32(0.0))

    def tile(row_re, row_im):
        return jnp.where(
            row_at == 0, jnp.broadcast_to(row_re, vreg), jnp.broadcast_to(row_im, vreg)
        )

    near = [(0, -1), (0, 1), (1, 0), (-1, 0)]
    far = [(0, 2), (0, -2), (1, 1), (1, -1), (-1, 1), (-1, -1), (2, 0), (-2, 0)]
    around = far + near

    def cvec_copy(k, slot):
        t_off, x_off = around[slot]
        return pltpu.make_async_remote_copy(
            src_ref=cvec_out.at[k],
            dst_ref=cvec_in.at[k, slot],
            send_sem=cvec_send.at[k],
            recv_sem=cvec_recv.at[k],
            device_id=device_at(-t_off, -x_off),
            device_id_type=MESH,
        )

    def stencil_of(area, k):
        if area == 0:
            return coarse_ref[k, 0], coarse_ref[k, 1]
        return stencil_in[area - 1, k, 0], stencil_in[area - 1, k, 1]

    def add_term(acc, matrix, vec):
        m_re, m_im = matrix
        v_re, v_im = vec[0:1], vec[1:2]
        now = (m_re * v_re - m_im * v_im, m_re * v_im + m_im * v_re)
        return now if acc is None else (acc[0] + now[0], acc[1] + now[1])

    def local_terms(area, vec):
        m_re, m_im = stencil_of(area, 0)
        acc = add_term(None, (m_re - diag_shift, m_im), vec)
        over = roll(vec, 64, -1)
        p_re, p_im = stencil_of(area, 5)
        q_re, q_im = stencil_of(area, 6)
        acc = add_term(acc, (p_re + q_re, p_im + q_im), over)
        ahead = jnp.where(agg_z == 3, roll(vec, 48, -1), roll(vec, -16, -1))
        behind = jnp.where(agg_z == 0, roll(vec, -48, -1), roll(vec, 16, -1))
        acc = add_term(acc, stencil_of(area, 7), ahead)
        return add_term(acc, stencil_of(area, 8), behind)

    def finish(accs):
        rows = jnp.concatenate([w for acc in accs for w in acc], axis=0)
        rows = split_dot(rows, agg_weights)
        return [tile(*diagonal_row(rows[32 * i : 32 * i + 32])) for i in range(len(accs))]

    vecs = [tile(*vec)]
    for pair_at in range(GCR_ITERS // 2):
        own = vecs[-1]
        cvec_out[pair_at] = own
        copies = [cvec_copy(pair_at, slot) for slot in range(len(around))]
        for copy in copies:
            copy.start()
        accs = [local_terms(0, own)]
        if pair_at == 0:
            for part in range(3):
                for side in range(4):
                    stencil_copy(part, side).wait()
        arrived = cvec_in.at[pair_at]
        pltpu.make_async_remote_copy(
            src_ref=arrived,
            dst_ref=arrived,
            send_sem=cvec_send.at[pair_at],
            recv_sem=cvec_recv.at[pair_at],
            device_id=device_at(*around[0]),
            device_id_type=MESH,
        ).wait()
        have = {(0, 0): own}
        for slot, place in enumerate(around):
            have[place] = cvec_in[pair_at, slot]
        for area in range(1, 5):
            accs.append(local_terms(area, have[areas[area]]))
        for area, (t_off, x_off) in enumerate(areas):
            for side in range(4):
                t_step, x_step = areas[1 + side]
                there = have[(t_off + t_step, x_off + x_step)]
                accs[area] = add_term(accs[area], stencil_of(area, 1 + side), there)
        nexts = finish(accs)
        acc = local_terms(0, nexts[0])
        for side in range(4):
            acc = add_term(acc, stencil_of(0, 1 + side), nexts[1 + side])
        vecs = vecs + [nexts[0]] + finish([acc])

    basis_re = basis_im = jnp.zeros(vreg, f32)
    for k, vec in enumerate(vecs):
        basis_re = jnp.where(row_at == k, jnp.broadcast_to(vec[0:1], vreg), basis_re)
        basis_im = jnp.where(row_at == k, jnp.broadcast_to(vec[1:2], vreg), basis_im)

    gram = jnp.zeros(vreg, f32)
    for k in range(GCR_ITERS + 1):
        k_re = basis_re[k : k + 1]
        k_im = basis_im[k : k + 1]
        dot_re = jnp.sum(basis_re * k_re + basis_im * k_im, axis=1, keepdims=True)
        dot_im = jnp.sum(basis_re * k_im - basis_im * k_re, axis=1, keepdims=True)
        gram = jnp.where(lane == 2 * k, jnp.broadcast_to(dot_re, vreg), gram)
        gram = jnp.where(lane == 2 * k + 1, jnp.broadcast_to(dot_im, vreg), gram)
    reduce_start(1, 0, gram)

    diag_rows = jnp.concatenate(
        [
            jnp.where(on_diagonal, jnp.broadcast_to(vec[part : part + 1], (16, 128)), f32(0.0))
            for vec in vecs[:GCR_ITERS]
            for part in range(2)
        ],
        axis=0,
    )
    spread[...] = split_dot(diag_rows, from_agg).reshape(GCR_ITERS, 2, NVEC, 1, 128)

    def prolong(entry, carry):
        n_re = null_ref[:, 0, entry].astype(f32)
        n_im = null_ref[:, 1, entry].astype(f32)
        for k in range(GCR_ITERS):
            e_re = spread[k, 0]
            e_im = spread[k, 1]
            prolonged[k, entry] = jnp.sum(n_re * e_re - n_im * e_im, axis=0)
            prolonged[k, 12 + entry] = jnp.sum(n_re * e_im + n_im * e_re, axis=0)
        return carry

    lax.fori_loop(0, 12, prolong, 0)
    halves = expand(smooth[0].reshape(24, 8, 128), smooth[1].reshape(24, 8, 128))
    for i, half in enumerate(halves):
        out_ref[:, 8 * i : 8 * i + 8] = half

    reduce_start(1, 1, reduce_finish(1, 0))
    gram = reduce_finish(1, 1)

    columns = []
    for k in range(GCR_ITERS + 1):
        columns.append(
            (
                jnp.broadcast_to(gram[:, 2 * k : 2 * k + 1], vreg),
                jnp.broadcast_to(gram[:, 2 * k + 1 : 2 * k + 2], vreg),
            )
        )

    def scaled(a, x):
        return (a[0] * x[0] - a[1] * x[1], a[0] * x[1] + a[1] * x[0])

    def plus(x, y):
        return (x[0] + y[0], x[1] + y[1])

    def minus(x, y):
        return (x[0] - y[0], x[1] - y[1])

    def inner(pairs):
        terms = [
            term
            for left, image in pairs
            for term in (
                left[0] * image[0] + left[1] * image[1],
                left[0] * image[1] - left[1] * image[0],
            )
        ]
        sums = jnp.sum(jnp.stack(terms), axis=1, keepdims=True)
        sums = [jnp.broadcast_to(sums[i], vreg) for i in range(len(terms))]
        return list(zip(sums[::2], sums[1::2]))

    image_columns = [
        plus(columns[k + 1], (shift * columns[k][0], shift * columns[k][1]))
        for k in range(GCR_ITERS)
    ]
    remain = (jnp.where(row_at == 0, f32(1.0), f32(0.0)), jnp.zeros(vreg, f32))
    answer = (jnp.zeros(vreg, f32), jnp.zeros(vreg, f32))
    past = []
    for iteration in range(GCR_ITERS):
        direction = remain
        image = tuple(roll(w, 1, -2) + shift * w for w in direction)
        dots = None
        for k in range(iteration + 1):
            entry = tuple(jnp.broadcast_to(w[k : k + 1], vreg) for w in remain)
            now = scaled(entry, image_columns[k])
            dots = now if dots is None else plus(dots, now)
        if past:
            margins = inner([(old_image, dots) for _, old_image, _, _ in past])
            for margin, (old_direction, old_image, old_dots, inverse) in zip(margins, past):
                margin = (margin[0] * inverse, margin[1] * inverse)
                image = minus(image, scaled(margin, old_image))
                direction = minus(direction, scaled(margin, old_direction))
                dots = minus(dots, scaled(margin, old_dots))
        squares, along = inner([(image, dots), (remain, dots)])
        inverse = 1.0 / (jnp.maximum(squares[0], f32(0.0)) + mean_eps)
        step = (along[0] * inverse, -(along[1] * inverse))
        answer = plus(answer, scaled(step, direction))
        remain = minus(remain, scaled(step, image))
        past.append((direction, image, dots, inverse))

    error = scaled(answer, (basis_re, basis_im))
    error = [jnp.sum(w, axis=0, keepdims=True) for w in error]
    error_ref[0:1] = error[0]
    error_ref[1:2] = error[1]

    for k in range(GCR_ITERS):
        c_re = answer[0][k : k + 1]
        c_im = answer[1][k : k + 1]
        w_re = prolonged[k, :12]
        w_im = prolonged[k, 12:]
        now_re = c_re * w_re - c_im * w_im
        now_im = c_re * w_im + c_im * w_re
        sum_re = now_re if k == 0 else sum_re + now_re
        sum_im = now_im if k == 0 else sum_im + now_im
    out_ref[:12] = out_ref[:12] + sum_re
    out_ref[12:] = out_ref[12:] + sum_im


def solution(mesh):
    n_ta, n_xyz = mesh.shape["ta"], mesh.shape["xyz"]

    def shards(source, gauge_links, clover_raw, null_vectors, coarse_operator):
        f32 = jnp.float32
        dma = pltpu.SemaphoreType.DMA
        field, error = pl.pallas_call(
            functools.partial(kernel, n_ta, n_xyz),
            out_shape=(
                jax.ShapeDtypeStruct((24, 16, 128), f32),
                jax.ShapeDtypeStruct((2, 128), f32),
            ),
            in_specs=[pl.BlockSpec(memory_space=pltpu.HBM)] * 5,
            out_specs=(pl.BlockSpec(memory_space=pltpu.VMEM),) * 2,
            scratch_shapes=[
                pltpu.VMEM((24, 16, 128), f32),
                pltpu.VMEM((72, 16, 128), jnp.bfloat16),
                pltpu.VMEM((144, 16, 128), jnp.bfloat16),
                pltpu.VMEM((NVEC, 2, 12, 16, 128), jnp.bfloat16),
                pltpu.VMEM((9, 2, NVEC, 128), f32),
                pltpu.VMEM((2, 4, 2, 3, 3, 8, 128), f32),
                pltpu.VMEM((2, 4, 2, 3, 3, 8, 128), f32),
                pltpu.VMEM((2, 2, 2, 6, 6, 8, 128), f32),
                pltpu.VMEM((2, 2, 4, 3, 8, 128), f32),
                pltpu.VMEM((2, 2, 4, 3, 8, 128), f32),
                pltpu.VMEM((2, 4, 3, 8, 128), f32),
                pltpu.VMEM((HALF_STEPS, 4, 3, 8, 128), f32),
                pltpu.VMEM((HALF_STEPS, 4, 3, 8, 128), f32),
                pltpu.VMEM((2, NVEC, 8, 128), f32),
                pltpu.VMEM((GCR_ITERS, 2, NVEC, 1, 128), f32),
                pltpu.VMEM((GCR_ITERS, 24, 16, 128), f32),
                pltpu.VMEM((4, 9, 2, NVEC, 128), f32),
                pltpu.VMEM((GCR_ITERS // 2, 8, 128), f32),
                pltpu.VMEM((GCR_ITERS // 2, 12, 8, 128), f32),
                pltpu.VMEM((2, 2, 8, 128), f32),
                pltpu.VMEM((2, n_xyz // 2 - 1 + 2 * n_ta - 1, 8, 128), f32),
                dma((5,)),
                dma((HALF_STEPS, 4)),
                dma((HALF_STEPS, 4)),
                dma((3, 4)),
                dma((3, 4)),
                dma((GCR_ITERS // 2,)),
                dma((GCR_ITERS // 2,)),
                dma((2, 2)),
                dma((2, 2)),
            ],
            compiler_params=pltpu.CompilerParams(
                collective_id=0, has_side_effects=True, vmem_limit_bytes=40 * 2**20
            ),
        )(
            *(
                pltpu.with_memory_space_constraint(operand, pltpu.HBM)
                for operand in (
                    source.reshape(24, 16, 128),
                    gauge_links.reshape(72, 16, 128),
                    clover_raw.reshape(144, 16, 128),
                    null_vectors.reshape(NVEC, 2, 12, 16, 128),
                    coarse_operator,
                )
            )
        )
        return field.reshape(source.shape), error

    in_specs = (
        P(None, None, None, "ta", "xyz", None),
        P(None, None, None, None, "ta", "xyz", None),
        P(None, None, None, None, "ta", "xyz", None),
        P(None, None, None, None, "ta", "xyz", None),
        P(None, None, None, ("ta", "xyz")),
    )
    out_specs = (P(None, None, None, "ta", "xyz", None), P(None, ("ta", "xyz")))
    return jax.shard_map(shards, mesh=mesh, in_specs=in_specs, out_specs=out_specs, check_vma=False)
```

```python
import functools

import jax
import jax.numpy as jnp
from jax import lax
from jax.experimental import pallas as pl
from jax.experimental.pallas import tpu as pltpu
from jax.sharding import PartitionSpec as P

MESH = pl.DeviceIdType.MESH
NVEC = 16
MR_STEPS = 2
SAP_CYCLES = 2
GCR_ITERS = 4
HALF_STEPS = 2 * SAP_CYCLES

mass_shift = 0.2
mean_eps = 1e-06
block_entries = 6144.0

gamma_perm = [[2, 3, 0, 1], [3, 2, 1, 0], [3, 2, 1, 0], [2, 3, 0, 1]]
gamma_real = [[1, 1, 1, 1], [0, 0, 0, 0], [-1, 1, 1, -1], [0, 0, 0, 0]]
gamma_imag = [[0, 0, 0, 0], [1, 1, -1, -1], [0, 0, 0, 0], [1, -1, -1, 1]]


def roll(value, shift, axis):
    axis = value.ndim + axis
    size = value.shape[axis]
    return pltpu.roll(value, shift % size, axis)


def signed_add(base, sign, value):
    return base + value if sign > 0 else base - value


def project(v, mu, sign):
    half_re, half_im = [], []
    for s in range(2):
        q = gamma_perm[mu][s]
        if gamma_real[mu][s]:
            w = sign * gamma_real[mu][s]
            half_re.append(signed_add(v[0][s], w, v[0][q]))
            half_im.append(signed_add(v[1][s], w, v[1][q]))
        else:
            w = sign * gamma_imag[mu][s]
            half_re.append(signed_add(v[0][s], -w, v[1][q]))
            half_im.append(signed_add(v[1][s], w, v[0][q]))
    return jnp.stack(half_re), jnp.stack(half_im)


def unproject(out, half, mu, sign):
    half_re, half_im = half
    for s in range(2):
        out[0][s] = out[0][s] + half_re[s]
        out[1][s] = out[1][s] + half_im[s]
    for s in range(2, 4):
        q = gamma_perm[mu][s]
        if gamma_real[mu][s]:
            w = sign * gamma_real[mu][s]
            out[0][s] = signed_add(out[0][s], w, half_re[q])
            out[1][s] = signed_add(out[1][s], w, half_im[q])
        else:
            w = sign * gamma_imag[mu][s]
            out[0][s] = signed_add(out[0][s], -w, half_im[q])
            out[1][s] = signed_add(out[1][s], w, half_re[q])


def link_apply(links, colour, mu, half):
    half_re, half_im = half
    out_re = out_im = None
    for b in range(3):
        u_re = links[colour, mu, 0, b][None]
        u_im = links[colour, mu, 1, b][None]
        h_re = half_re[:, b][:, None]
        h_im = half_im[:, b][:, None]
        term_re = u_re * h_re - u_im * h_im
        term_im = u_re * h_im + u_im * h_re
        out_re = term_re if b == 0 else out_re + term_re
        out_im = term_im if b == 0 else out_im + term_im
    return out_re, out_im


def link_apply_dagger(links, colour, mu, half):
    half_re, half_im = half
    out_re = out_im = None
    for b in range(3):
        u_re = links[colour, mu, 0, :, b][None]
        u_im = links[colour, mu, 1, :, b][None]
        h_re = half_re[:, b][:, None]
        h_im = half_im[:, b][:, None]
        term_re = u_re * h_re + u_im * h_im
        term_im = u_re * h_im - u_im * h_re
        out_re = term_re if b == 0 else out_re + term_re
        out_im = term_im if b == 0 else out_im + term_im
    return out_re, out_im


def split_dot(value, weights):
    rows = value.shape[0]
    high = value.astype(jnp.bfloat16)
    rest = value - high.astype(jnp.float32)
    mid = rest.astype(jnp.bfloat16)
    low = (rest - mid.astype(jnp.float32)).astype(jnp.bfloat16)
    out = jnp.dot(
        jnp.concatenate([high, mid, low], axis=0), weights, preferred_element_type=jnp.float32
    )
    return out[:rows] + out[rows : 2 * rows] + out[2 * rows :]


def iota(shape, dim):
    return lax.broadcasted_iota(jnp.int32, shape, dim)


def kernel(
    n_ta, n_xyz,
    source_hbm, gauge_hbm, clover_hbm, null_hbm, coarse_hbm,
    out_ref, error_ref,
    source_ref, gauge_ref, clover_ref, null_ref, coarse_ref,
    link_in, link_out, herm, resid, smooth, z_ref,
    halo_out, halo_in, partial, rest, null_even, spread, prolonged,
    stencil_in, cvec_out, cvec_in, dot_out, dot_in,
    load_sem, halo_send, halo_recv, stencil_send, stencil_recv, cvec_send, cvec_recv,
    dot_send, dot_recv,
):
    f32 = jnp.float32
    ta = lax.axis_index("ta")
    xyz = lax.axis_index("xyz")

    loads = [
        pltpu.make_async_copy(src, dst, load_sem.at[i])
        for i, (src, dst) in enumerate(
            [
                (gauge_hbm, gauge_ref),
                (clover_hbm, clover_ref),
                (source_hbm, source_ref),
                (coarse_hbm, coarse_ref),
                (null_hbm, null_ref),
            ]
        )
    ]

    def device_at(t_off, x_off):
        return (lax.rem(ta + t_off + n_ta, n_ta), lax.rem(xyz + x_off + n_xyz, n_xyz))

    def depth_peer(d):
        low = lax.rem(xyz, n_low)
        return (ta, xyz - low + lax.rem(low + d, n_low))

    def plane_peer(d):
        return (lax.rem(ta + d, n_ta), lax.rem(xyz + n_low * (d // n_ta), n_xyz))

    n_low = n_xyz // 2
    groups = [
        [depth_peer(d) for d in range(1, n_low)],
        [plane_peer(d) for d in range(1, 2 * n_ta)],
    ]
    close = [(0, 1), (0, -1), (0, 2), (0, -2), (1, 1), (1, -1), (-1, 1), (-1, -1)]
    peers = [device_at(*place) for place in close[::-1]] + groups[1][::-1] + groups[0][::-1]
    barrier = pltpu.get_barrier_semaphore()
    for peer in peers[:12]:
        pl.semaphore_signal(barrier, inc=1, device_id=peer, device_id_type=MESH)
    for load in loads[:-1]:
        load.start()
    for peer in peers[12:]:
        pl.semaphore_signal(barrier, inc=1, device_id=peer, device_id_type=MESH)

    vreg = (8, 128)
    lane = iota(vreg, 1)
    subl = iota(vreg, 0)
    t_low = subl // 4
    x_pos = subl % 4
    y_pos = lane // 16
    z_pos = lane % 16
    parity = (ta + xyz + y_pos // 4 + z_pos // 4) % 2
    t_high = [parity, 1 - parity]

    def compact(natural):
        first = natural[..., :8, :]
        second = roll(natural[..., 8:, :], 64, -1)
        low = jnp.broadcast_to(parity == 0, first.shape)
        return jnp.where(low, first, second), jnp.where(low, second, first)

    def expand(even, odd):
        low = jnp.broadcast_to(parity == 0, even.shape)
        return jnp.where(low, even, odd), roll(jnp.where(low, odd, even), 64, -1)

    loads[0].wait()
    t_sign = jnp.where(ta == n_ta - 1, f32(0.5), f32(-0.5))
    for mu in range(4):
        planes = gauge_ref[pl.ds(18 * mu, 18)].astype(f32)
        pair = compact(planes)
        for colour in range(2):
            if mu == 0:
                inside = jnp.logical_not((t_high[colour] == 1) & (t_low == 1))
            elif mu == 1:
                inside = x_pos != 3
            elif mu == 2:
                inside = y_pos % 4 != 3
            else:
                inside = z_pos % 4 != 3
            weight_in = jnp.where(inside, f32(-0.5), f32(0.0))
            weight_out = jnp.where(inside, f32(0.0), t_sign if mu == 0 else f32(-0.5))
            for part in range(2):
                for row in range(3):
                    first = 9 * part + 3 * row
                    mine = pair[colour][first : first + 3]
                    link_in[colour, mu, part, :, row] = mine * weight_in
                    link_out[colour, mu, part, :, row] = mine * weight_out

    loads[1].wait()
    for chi in range(2):
        for col in range(6):
            row_at = 36 * chi + 6 * col
            for part in range(2):
                base = 72 * part
                line = clover_ref[pl.ds(base + row_at, 6)].astype(f32)
                column = jnp.stack(
                    [clover_ref[base + 36 * chi + 6 * r + col].astype(f32) for r in range(6)]
                )
                if part == 0:
                    sym = 0.5 * (column + line)
                    diag = iota((6, 1, 1), 0) == col
                    sym = sym + jnp.where(diag, f32(4.0 + mass_shift), f32(0.0))
                else:
                    sym = 0.5 * (column - line)
                pair = compact(sym)
                for colour in range(2):
                    herm[colour, part, chi, col] = pair[colour]

    loads[2].wait()
    pair = compact(source_ref[...])
    for colour in range(2):
        resid[colour] = pair[colour].reshape(2, 4, 3, 8, 128)
    smooth[...] = jnp.zeros_like(smooth)

    square = (128, 128)
    into = iota(square, 0)
    outof = iota(square, 1)
    block_weights = ((into % 16) // 4 == (outof % 16) // 4).astype(f32).astype(jnp.bfloat16)

    def load(ref, colour):
        value = ref[colour]
        return [[value[part, s] for s in range(4)] for part in range(2)]

    def block_wilson(v, colour):
        out = [[None] * 4, [None] * 4]
        for chi in range(2):
            v_re = jnp.concatenate([v[0][2 * chi], v[0][2 * chi + 1]])
            v_im = jnp.concatenate([v[1][2 * chi], v[1][2 * chi + 1]])
            acc_re = acc_im = None
            for col in range(6):
                h_re = herm[colour, 0, chi, col]
                h_im = herm[colour, 1, chi, col]
                term_re = h_re * v_re[col][None] - h_im * v_im[col][None]
                term_im = h_re * v_im[col][None] + h_im * v_re[col][None]
                acc_re = term_re if col == 0 else acc_re + term_re
                acc_im = term_im if col == 0 else acc_im + term_im
            for half in range(2):
                out[0][2 * chi + half] = acc_re[3 * half : 3 * half + 3]
                out[1][2 * chi + half] = acc_im[3 * half : 3 * half + 3]
        low = t_low == 0
        for mu in range(4):
            ahead = project(v, mu, -1)
            behind = link_apply_dagger(link_in, colour, mu, project(v, mu, 1))
            if mu == 0:
                ahead = [
                    roll(jnp.where(low, roll(w, 64, -1), w), 4, -2) for w in ahead
                ]
                behind = [
                    roll(jnp.where(low, w, roll(w, 64, -1)), 4, -2) for w in behind
                ]
            elif mu == 1:
                ahead = [roll(w, -1, -2) for w in ahead]
                behind = [roll(w, 1, -2) for w in behind]
            else:
                step = 16 if mu == 2 else 1
                ahead = [roll(w, -step, -1) for w in ahead]
                behind = [roll(w, step, -1) for w in behind]
            unproject(out, link_apply(link_in, colour, mu, ahead), mu, -1)
            unproject(out, behind, mu, 1)
        return out

    def each(function, *fields):
        return [[function(*(f[part][s] for f in fields)) for s in range(4)] for part in range(2)]

    def site_sum(pairs):
        total = None
        for left, right, sign in pairs:
            for s in range(4):
                term = left[s] * right[s]
                total = term if total is None else signed_add(total, sign, term)
        return total[0] + total[1] + total[2]

    def minimal_residual(colour):
        rho = load(resid, colour)
        image = block_wilson(rho, colour)
        second = block_wilson(image, colour)

        def dot(left, right):
            return [
                site_sum([(left[0], right[0], 1), (left[1], right[1], 1)]),
                site_sum([(left[0], right[1], 1), (left[1], right[0], -1)]),
            ]

        sums = dot(image, rho) + dot(second, rho) + dot(second, image)
        sums = sums + [dot_self(image), dot_self(second)]
        sums = split_dot(jnp.concatenate(sums, axis=0), block_weights).reshape(8, 8, 128)
        sums = jnp.sum(sums, axis=1, keepdims=True) / block_entries
        pr_re, pr_im, wr_re, wr_im, wp_re, wp_im, pp, ww = [sums[i] for i in range(8)]
        inverse = 1.0 / (pp + mean_eps)
        a_re = pr_re * inverse
        a_im = pr_im * inverse
        size = a_re * a_re + a_im * a_im
        s_re = pr_re - a_re * pp - (a_re * wr_re + a_im * wr_im) + size * wp_re
        s_im = pr_im - a_im * pp - (a_re * wr_im - a_im * wr_re) + size * wp_im
        squares = pp - 2.0 * (a_re * wp_re + a_im * wp_im) + size * ww
        inverse = 1.0 / (jnp.maximum(squares, f32(0.0)) + mean_eps)
        b_re = s_re * inverse
        b_im = s_im * inverse
        sum_re = jnp.broadcast_to(a_re + b_re, vreg)
        sum_im = jnp.broadcast_to(a_im + b_im, vreg)
        both_re = jnp.broadcast_to(a_re * b_re - a_im * b_im, vreg)
        both_im = jnp.broadcast_to(a_re * b_im + a_im * b_re, vreg)

        def combine(x, y):
            return [
                [
                    (sum_re * x[0][s] - sum_im * x[1][s])
                    - (both_re * y[0][s] - both_im * y[1][s])
                    for s in range(4)
                ],
                [
                    (sum_re * x[1][s] + sum_im * x[0][s])
                    - (both_re * y[1][s] + both_im * y[0][s])
                    for s in range(4)
                ],
            ]

        answer = combine(rho, image)
        return answer, each(jnp.subtract, rho, combine(image, second))

    def dot_self(value):
        return site_sum([(value[0], value[0], 1), (value[1], value[1], 1)])

    def flat(half):
        return jnp.concatenate([half[0].reshape(6, 8, 128), half[1].reshape(6, 8, 128)])

    def pack_x(half, face):
        groups = flat(half).reshape(3, 4, 8, 128)
        packed = None
        for j in range(4):
            moved = roll(groups[:, j], j - face, -2)
            packed = moved if j == 0 else jnp.where(x_pos == j, moved, packed)
        return packed

    def unpack_x(packed, face):
        rows = jnp.stack([roll(packed, face - j, -2) for j in range(4)], axis=1)
        rows = rows.reshape(2, 2, 3, 8, 128)
        return rows[0], rows[1]

    def pack_t(half, face, away):
        groups = flat(half).reshape(3, 4, 8, 128)
        here = (away == 0) if face == 0 else (away == 1)
        first = jnp.where(here, groups[:, 0], roll(groups[:, 1], 64, -1))
        second = jnp.where(here, groups[:, 2], roll(groups[:, 3], 64, -1))
        if face == 0:
            return jnp.where(t_low == 0, first, roll(second, 4, -2))
        return jnp.where(t_low == 1, first, roll(second, 4, -2))

    def unpack_t(packed):
        turned = roll(packed, 64, -1)
        rows = jnp.stack([roll(turned, 4, -2), roll(packed, 4, -2), turned, packed], axis=1)
        rows = rows.reshape(2, 2, 3, 8, 128)
        return rows[0], rows[1]

    def halo_copy(step, side):
        target = device_at(*((-1, 0), (1, 0), (0, -1), (0, 1))[side])
        return pltpu.make_async_remote_copy(
            src_ref=halo_out.at[step, side],
            dst_ref=halo_in.at[step, side],
            send_sem=halo_send.at[step, side],
            recv_sem=halo_recv.at[step, side],
            device_id=target,
            device_id_type=MESH,
        )

    def reduce_start(slot, stage, value):
        dot_out[slot, stage] = value
        for i, peer in enumerate(groups[stage]):
            pltpu.make_async_remote_copy(
                src_ref=dot_out.at[slot, stage],
                dst_ref=dot_in.at[slot, stage_at[stage] + i],
                send_sem=dot_send.at[slot, stage],
                recv_sem=dot_recv.at[slot, stage],
                device_id=peer,
                device_id_type=MESH,
            ).start()

    def reduce_finish(slot, stage):
        count = len(groups[stage])
        arrived = dot_in.at[slot, pl.ds(stage_at[stage], count)]
        pltpu.make_async_remote_copy(
            src_ref=arrived,
            dst_ref=arrived,
            send_sem=dot_send.at[slot, stage],
            recv_sem=dot_recv.at[slot, stage],
            device_id=groups[stage][0],
            device_id_type=MESH,
        ).wait()
        first = stage_at[stage]
        return dot_out[slot, stage] + jnp.sum(dot_in[slot, first : first + count], axis=0)

    stage_at = [0, n_low - 1]

    loads[3].wait()
    coarse_lane = iota((16, 128), 1)
    coarse_row = iota((16, 128), 0)
    on_diagonal = (coarse_lane % NVEC) == coarse_row
    trace = jnp.where(on_diagonal, coarse_ref[0, 0], f32(0.0))
    trace = jnp.sum(trace, axis=0, keepdims=True)
    trace = jnp.sum(trace, axis=1, keepdims=True) / f32(128 * n_ta * n_xyz)
    trace = jnp.broadcast_to(trace, vreg)

    def stencil_copy(part, side):
        t_off, x_off = areas[1 + side]
        third = pl.ds(3 * part, 3)
        return pltpu.make_async_remote_copy(
            src_ref=coarse_ref.at[third],
            dst_ref=stencil_in.at[side, third],
            send_sem=stencil_send.at[part, side],
            recv_sem=stencil_recv.at[part, side],
            device_id=device_at(-t_off, -x_off),
            device_id_type=MESH,
        )

    def solve(colour):
        z, rho = minimal_residual(colour)
        for part in range(2):
            for s in range(4):
                z_ref[part, s] = z[part][s]
                resid[colour, part, s] = rho[part][s]
                smooth[colour, part, s] = smooth[colour, part, s] + z[part][s]

    def subtract(colour, change):
        for part in range(2):
            for s in range(4):
                resid[colour, part, s] = resid[colour, part, s] - change[part][s]

    def exchange(step, meanwhile, early=None):
        colour = lax.rem(step, 2)
        other = 1 - colour
        z = [[z_ref[part, s] for s in range(4)] for part in range(2)]
        away = jnp.where(colour == 0, t_high[0], t_high[1])
        halo_out[step, 1] = pack_t(link_apply_dagger(link_out, colour, 0, project(z, 0, 1)), 3, away)
        halo_out[step, 3] = pack_x(link_apply_dagger(link_out, colour, 1, project(z, 1, 1)), 3)
        halo_out[step, 0] = pack_t(project(z, 0, -1), 0, away)
        halo_out[step, 2] = pack_x(project(z, 1, -1), 0)
        copies = [halo_copy(step, side) for side in range(4)]
        for copy in copies[::-1]:
            copy.start()
        meanwhile(step)
        change = [[jnp.zeros((3, 8, 128), f32)] * 4 for _ in range(2)]
        for mu in (2, 3):
            ahead = project(z, mu, -1)
            behind = link_apply_dagger(link_out, colour, mu, project(z, mu, 1))
            if mu == 2:
                ahead = [roll(w, -16, -1) for w in ahead]
                behind = [roll(w, 16, -1) for w in behind]
            else:
                ahead = [jnp.where(z_pos == 15, roll(w, 15, -1), roll(w, -1, -1)) for w in ahead]
                behind = [jnp.where(z_pos == 0, roll(w, -15, -1), roll(w, 1, -1)) for w in behind]
            unproject(change, link_apply(link_out, other, mu, ahead), mu, -1)
            unproject(change, behind, mu, 1)
        if early:
            early(change)
            change = [[jnp.zeros((3, 8, 128), f32)] * 4 for _ in range(2)]
        for copy in copies:
            copy.wait()
        ahead = unpack_t(halo_in[step, 0])
        unproject(change, link_apply(link_out, other, 0, ahead), 0, -1)
        first = (away == 1) & (t_low == 0)
        behind = [jnp.where(first, w, f32(0.0)) for w in unpack_t(halo_in[step, 1])]
        unproject(change, behind, 0, 1)
        ahead = unpack_x(halo_in[step, 2], 3)
        unproject(change, link_apply(link_out, other, 1, ahead), 1, -1)
        behind = [jnp.where(x_pos == 0, w, f32(0.0)) for w in unpack_x(halo_in[step, 3], 0)]
        unproject(change, behind, 1, 1)
        if early:
            return change
        subtract(other, change)
        return None

    def narrow_null(a, carry):
        even, _ = compact(null_ref[a].astype(f32))
        null_even[a] = even
        return carry

    def background(step):
        for side in range(4):
            stencil_copy(step, side).start()

        @pl.when(step == 0)
        def _():
            reduce_start(0, 0, trace)
            loads[4].wait()
            lax.fori_loop(0, NVEC, narrow_null, 0)

        @pl.when(step == 1)
        def _():
            reduce_start(0, 1, reduce_finish(0, 0))

    def half_step(step, carry):
        exchange(step, background)
        solve(1 - lax.rem(step, 2))
        return carry

    areas = [(0, 0), (1, 0), (-1, 0), (0, 1), (0, -1)]
    loads[4].start()
    solve(0)
    pl.semaphore_wait(barrier, len(peers))
    lax.fori_loop(0, HALF_STEPS - 1, half_step, 0)

    def restrict_known(change):
        subtract(0, change)
        natural = expand(resid[0].reshape(24, 8, 128), resid[1].reshape(24, 8, 128))

        def restrict(a, carry):
            basis = null_ref[a].astype(f32)
            acc_re = acc_im = None
            for i, half in enumerate(natural):
                b_re = basis[0, :, 8 * i : 8 * i + 8]
                b_im = basis[1, :, 8 * i : 8 * i + 8]
                term_re = jnp.sum(b_re * half[:12] + b_im * half[12:], axis=0)
                term_im = jnp.sum(b_re * half[12:] - b_im * half[:12], axis=0)
                acc_re = term_re if i == 0 else acc_re + term_re
                acc_im = term_im if i == 0 else acc_im + term_im
            partial[0, a] = acc_re
            partial[1, a] = acc_im
            return carry

        lax.fori_loop(0, NVEC, restrict, 0)

    change = exchange(HALF_STEPS - 1, lambda step: None, restrict_known)
    change_re = jnp.concatenate(change[0])
    change_im = jnp.concatenate(change[1])

    def restrict_rest(a, carry):
        b_re = null_even[a, 0]
        b_im = null_even[a, 1]
        rest[0, a] = jnp.sum(b_re * change_re + b_im * change_im, axis=0)
        rest[1, a] = jnp.sum(b_re * change_im - b_im * change_re, axis=0)
        return carry

    lax.fori_loop(0, NVEC, restrict_rest, 0)
    site_agg = 4 * (into // 64) + (into % 16) // 4
    to_agg = (site_agg == outof // NVEC).astype(f32).astype(jnp.bfloat16)
    site_agg = 4 * (outof // 64) + (outof % 16) // 4
    from_agg = (site_agg == into // NVEC).astype(f32).astype(jnp.bfloat16)
    agg_weights = (into // NVEC == outof // NVEC).astype(f32).astype(jnp.bfloat16)
    row_z = (into % 16) // 4
    even_agg = 4 * ((ta + xyz + row_z) % 2) + row_z
    from_even = (even_agg == outof // NVEC).astype(f32).astype(jnp.bfloat16)
    rows = split_dot(jnp.sum(partial[...], axis=2).reshape(32, 128), to_agg)
    rows = rows - split_dot(jnp.sum(rest[...], axis=2).reshape(32, 128), from_even)

    def diagonal_row(both):
        return [
            jnp.sum(
                jnp.where(on_diagonal, both[16 * i : 16 * i + 16], f32(0.0)),
                axis=0,
                keepdims=True,
            )
            for i in range(2)
        ]

    vec = diagonal_row(rows)

    shift = reduce_finish(0, 1)

    row_at = iota(vreg, 0)
    agg_z = (lane % 64) // NVEC
    diag_shift = jnp.where(on_diagonal, jnp.broadcast_to(shift[:1], (16, 128)), f32(0.0))

    def tile(row_re, row_im):
        return jnp.where(
            row_at == 0, jnp.broadcast_to(row_re, vreg), jnp.broadcast_to(row_im, vreg)
        )

    near = [(0, -1), (0, 1), (1, 0), (-1, 0)]
    far = [(0, 2), (0, -2), (1, 1), (1, -1), (-1, 1), (-1, -1), (2, 0), (-2, 0)]
    around = far + near

    def cvec_copy(k, slot):
        t_off, x_off = around[slot]
        return pltpu.make_async_remote_copy(
            src_ref=cvec_out.at[k],
            dst_ref=cvec_in.at[k, slot],
            send_sem=cvec_send.at[k],
            recv_sem=cvec_recv.at[k],
            device_id=device_at(-t_off, -x_off),
            device_id_type=MESH,
        )

    def stencil_of(area, k):
        if area == 0:
            return coarse_ref[k, 0], coarse_ref[k, 1]
        return stencil_in[area - 1, k, 0], stencil_in[area - 1, k, 1]

    def add_term(acc, matrix, vec):
        m_re, m_im = matrix
        v_re, v_im = vec[0:1], vec[1:2]
        now = (m_re * v_re - m_im * v_im, m_re * v_im + m_im * v_re)
        return now if acc is None else (acc[0] + now[0], acc[1] + now[1])

    def local_terms(area, vec):
        m_re, m_im = stencil_of(area, 0)
        acc = add_term(None, (m_re - diag_shift, m_im), vec)
        over = roll(vec, 64, -1)
        p_re, p_im = stencil_of(area, 5)
        q_re, q_im = stencil_of(area, 6)
        acc = add_term(acc, (p_re + q_re, p_im + q_im), over)
        ahead = jnp.where(agg_z == 3, roll(vec, 48, -1), roll(vec, -16, -1))
        behind = jnp.where(agg_z == 0, roll(vec, -48, -1), roll(vec, 16, -1))
        acc = add_term(acc, stencil_of(area, 7), ahead)
        return add_term(acc, stencil_of(area, 8), behind)

    def finish(accs):
        rows = jnp.concatenate([w for acc in accs for w in acc], axis=0)
        rows = split_dot(rows, agg_weights)
        return [tile(*diagonal_row(rows[32 * i : 32 * i + 32])) for i in range(len(accs))]

    vecs = [tile(*vec)]
    for pair_at in range(GCR_ITERS // 2):
        own = vecs[-1]
        cvec_out[pair_at] = own
        copies = [cvec_copy(pair_at, slot) for slot in range(len(around))]
        for copy in copies:
            copy.start()
        accs = [local_terms(0, own)]
        if pair_at == 0:
            for part in range(3):
                for side in range(4):
                    stencil_copy(part, side).wait()
        arrived = cvec_in.at[pair_at]
        pltpu.make_async_remote_copy(
            src_ref=arrived,
            dst_ref=arrived,
            send_sem=cvec_send.at[pair_at],
            recv_sem=cvec_recv.at[pair_at],
            device_id=device_at(*around[0]),
            device_id_type=MESH,
        ).wait()
        have = {(0, 0): own}
        for slot, place in enumerate(around):
            have[place] = cvec_in[pair_at, slot]
        for area in range(1, 5):
            accs.append(local_terms(area, have[areas[area]]))
        for area, (t_off, x_off) in enumerate(areas):
            for side in range(4):
                t_step, x_step = areas[1 + side]
                there = have[(t_off + t_step, x_off + x_step)]
                accs[area] = add_term(accs[area], stencil_of(area, 1 + side), there)
        nexts = finish(accs)
        acc = local_terms(0, nexts[0])
        for side in range(4):
            acc = add_term(acc, stencil_of(0, 1 + side), nexts[1 + side])
        vecs = vecs + [nexts[0]] + finish([acc])

    basis_re = basis_im = jnp.zeros(vreg, f32)
    for k, vec in enumerate(vecs):
        basis_re = jnp.where(row_at == k, jnp.broadcast_to(vec[0:1], vreg), basis_re)
        basis_im = jnp.where(row_at == k, jnp.broadcast_to(vec[1:2], vreg), basis_im)

    gram = jnp.zeros(vreg, f32)
    for k in range(GCR_ITERS + 1):
        k_re = basis_re[k : k + 1]
        k_im = basis_im[k : k + 1]
        dot_re = jnp.sum(basis_re * k_re + basis_im * k_im, axis=1, keepdims=True)
        dot_im = jnp.sum(basis_re * k_im - basis_im * k_re, axis=1, keepdims=True)
        gram = jnp.where(lane == 2 * k, jnp.broadcast_to(dot_re, vreg), gram)
        gram = jnp.where(lane == 2 * k + 1, jnp.broadcast_to(dot_im, vreg), gram)
    reduce_start(1, 0, gram)

    diag_rows = jnp.concatenate(
        [
            jnp.where(on_diagonal, jnp.broadcast_to(vec[part : part + 1], (16, 128)), f32(0.0))
            for vec in vecs[:GCR_ITERS]
            for part in range(2)
        ],
        axis=0,
    )
    spread[...] = split_dot(diag_rows, from_agg).reshape(GCR_ITERS, 2, NVEC, 1, 128)

    def prolong(entry, carry):
        n_re = null_ref[:, 0, entry].astype(f32)
        n_im = null_ref[:, 1, entry].astype(f32)
        for k in range(GCR_ITERS):
            e_re = spread[k, 0]
            e_im = spread[k, 1]
            prolonged[k, entry] = jnp.sum(n_re * e_re - n_im * e_im, axis=0)
            prolonged[k, 12 + entry] = jnp.sum(n_re * e_im + n_im * e_re, axis=0)
        return carry

    lax.fori_loop(0, 12, prolong, 0)
    halves = expand(smooth[0].reshape(24, 8, 128), smooth[1].reshape(24, 8, 128))
    for i, half in enumerate(halves):
        out_ref[:, 8 * i : 8 * i + 8] = half

    reduce_start(1, 1, reduce_finish(1, 0))
    gram = reduce_finish(1, 1)

    columns = []
    for k in range(GCR_ITERS + 1):
        columns.append(
            (
                jnp.broadcast_to(gram[:, 2 * k : 2 * k + 1], vreg),
                jnp.broadcast_to(gram[:, 2 * k + 1 : 2 * k + 2], vreg),
            )
        )

    def scaled(a, x):
        return (a[0] * x[0] - a[1] * x[1], a[0] * x[1] + a[1] * x[0])

    def plus(x, y):
        return (x[0] + y[0], x[1] + y[1])

    def minus(x, y):
        return (x[0] - y[0], x[1] - y[1])

    def inner(pairs):
        terms = [
            term
            for left, image in pairs
            for term in (
                left[0] * image[0] + left[1] * image[1],
                left[0] * image[1] - left[1] * image[0],
            )
        ]
        sums = jnp.sum(jnp.stack(terms), axis=1, keepdims=True)
        sums = [jnp.broadcast_to(sums[i], vreg) for i in range(len(terms))]
        return list(zip(sums[::2], sums[1::2]))

    image_columns = [
        plus(columns[k + 1], (shift * columns[k][0], shift * columns[k][1]))
        for k in range(GCR_ITERS)
    ]
    remain = (jnp.where(row_at == 0, f32(1.0), f32(0.0)), jnp.zeros(vreg, f32))
    answer = (jnp.zeros(vreg, f32), jnp.zeros(vreg, f32))
    past = []
    for iteration in range(GCR_ITERS):
        direction = remain
        image = tuple(roll(w, 1, -2) + shift * w for w in direction)
        dots = None
        for k in range(iteration + 1):
            entry = tuple(jnp.broadcast_to(w[k : k + 1], vreg) for w in remain)
            now = scaled(entry, image_columns[k])
            dots = now if dots is None else plus(dots, now)
        if past:
            margins = inner([(old_image, dots) for _, old_image, _, _ in past])
            for margin, (old_direction, old_image, old_dots, inverse) in zip(margins, past):
                margin = (margin[0] * inverse, margin[1] * inverse)
                image = minus(image, scaled(margin, old_image))
                direction = minus(direction, scaled(margin, old_direction))
                dots = minus(dots, scaled(margin, old_dots))
        squares, along = inner([(image, dots), (remain, dots)])
        inverse = 1.0 / (jnp.maximum(squares[0], f32(0.0)) + mean_eps)
        step = (along[0] * inverse, -(along[1] * inverse))
        answer = plus(answer, scaled(step, direction))
        remain = minus(remain, scaled(step, image))
        past.append((direction, image, dots, inverse))

    error = scaled(answer, (basis_re, basis_im))
    error = [jnp.sum(w, axis=0, keepdims=True) for w in error]
    error_ref[0:1] = error[0]
    error_ref[1:2] = error[1]

    for k in range(GCR_ITERS):
        c_re = answer[0][k : k + 1]
        c_im = answer[1][k : k + 1]
        w_re = prolonged[k, :12]
        w_im = prolonged[k, 12:]
        now_re = c_re * w_re - c_im * w_im
        now_im = c_re * w_im + c_im * w_re
        sum_re = now_re if k == 0 else sum_re + now_re
        sum_im = now_im if k == 0 else sum_im + now_im
    out_ref[:12] = out_ref[:12] + sum_re
    out_ref[12:] = out_ref[12:] + sum_im


def solution(mesh):
    n_ta, n_xyz = mesh.shape["ta"], mesh.shape["xyz"]

    def shards(source, gauge_links, clover_raw, null_vectors, coarse_operator):
        f32 = jnp.float32
        dma = pltpu.SemaphoreType.DMA
        field, error = pl.pallas_call(
            functools.partial(kernel, n_ta, n_xyz),
            out_shape=(
                jax.ShapeDtypeStruct((24, 16, 128), f32),
                jax.ShapeDtypeStruct((2, 128), f32),
            ),
            in_specs=[pl.BlockSpec(memory_space=pltpu.HBM)] * 5,
            out_specs=(pl.BlockSpec(memory_space=pltpu.VMEM),) * 2,
            scratch_shapes=[
                pltpu.VMEM((24, 16, 128), f32),
                pltpu.VMEM((72, 16, 128), jnp.bfloat16),
                pltpu.VMEM((144, 16, 128), jnp.bfloat16),
                pltpu.VMEM((NVEC, 2, 12, 16, 128), jnp.bfloat16),
                pltpu.VMEM((9, 2, NVEC, 128), f32),
                pltpu.VMEM((2, 4, 2, 3, 3, 8, 128), f32),
                pltpu.VMEM((2, 4, 2, 3, 3, 8, 128), f32),
                pltpu.VMEM((2, 2, 2, 6, 6, 8, 128), f32),
                pltpu.VMEM((2, 2, 4, 3, 8, 128), f32),
                pltpu.VMEM((2, 2, 4, 3, 8, 128), f32),
                pltpu.VMEM((2, 4, 3, 8, 128), f32),
                pltpu.VMEM((HALF_STEPS, 4, 3, 8, 128), f32),
                pltpu.VMEM((HALF_STEPS, 4, 3, 8, 128), f32),
                pltpu.VMEM((2, NVEC, 8, 128), f32),
                pltpu.VMEM((2, NVEC, 8, 128), f32),
                pltpu.VMEM((NVEC, 2, 12, 8, 128), f32),
                pltpu.VMEM((GCR_ITERS, 2, NVEC, 1, 128), f32),
                pltpu.VMEM((GCR_ITERS, 24, 16, 128), f32),
                pltpu.VMEM((4, 9, 2, NVEC, 128), f32),
                pltpu.VMEM((GCR_ITERS // 2, 8, 128), f32),
                pltpu.VMEM((GCR_ITERS // 2, 12, 8, 128), f32),
                pltpu.VMEM((2, 2, 8, 128), f32),
                pltpu.VMEM((2, n_xyz // 2 - 1 + 2 * n_ta - 1, 8, 128), f32),
                dma((5,)),
                dma((HALF_STEPS, 4)),
                dma((HALF_STEPS, 4)),
                dma((3, 4)),
                dma((3, 4)),
                dma((GCR_ITERS // 2,)),
                dma((GCR_ITERS // 2,)),
                dma((2, 2)),
                dma((2, 2)),
            ],
            compiler_params=pltpu.CompilerParams(
                collective_id=0, has_side_effects=True, vmem_limit_bytes=40 * 2**20
            ),
        )(
            *(
                pltpu.with_memory_space_constraint(operand, pltpu.HBM)
                for operand in (
                    source.reshape(24, 16, 128),
                    gauge_links.reshape(72, 16, 128),
                    clover_raw.reshape(144, 16, 128),
                    null_vectors.reshape(NVEC, 2, 12, 16, 128),
                    coarse_operator,
                )
            )
        )
        return field.reshape(source.shape), error

    in_specs = (
        P(None, None, None, "ta", "xyz", None),
        P(None, None, None, None, "ta", "xyz", None),
        P(None, None, None, None, "ta", "xyz", None),
        P(None, None, None, None, "ta", "xyz", None),
        P(None, None, None, ("ta", "xyz")),
    )
    out_specs = (P(None, None, None, "ta", "xyz", None), P(None, ("ta", "xyz")))
    return jax.shard_map(shards, mesh=mesh, in_specs=in_specs, out_specs=out_specs, check_vma=False)
```

```python
import functools

import jax
import jax.numpy as jnp
from jax import lax
from jax.experimental import pallas as pl
from jax.experimental.pallas import tpu as pltpu
from jax.sharding import PartitionSpec as P

MESH = pl.DeviceIdType.MESH
NVEC = 16
MR_STEPS = 2
SAP_CYCLES = 2
GCR_ITERS = 4
HALF_STEPS = 2 * SAP_CYCLES

mass_shift = 0.2
mean_eps = 1e-06
block_entries = 6144.0

gamma_perm = [[2, 3, 0, 1], [3, 2, 1, 0], [3, 2, 1, 0], [2, 3, 0, 1]]
gamma_real = [[1, 1, 1, 1], [0, 0, 0, 0], [-1, 1, 1, -1], [0, 0, 0, 0]]
gamma_imag = [[0, 0, 0, 0], [1, 1, -1, -1], [0, 0, 0, 0], [1, -1, -1, 1]]


def roll(value, shift, axis):
    axis = value.ndim + axis
    size = value.shape[axis]
    return pltpu.roll(value, shift % size, axis)


def signed_add(base, sign, value):
    return base + value if sign > 0 else base - value


def project(v, mu, sign):
    half_re, half_im = [], []
    for s in range(2):
        q = gamma_perm[mu][s]
        if gamma_real[mu][s]:
            w = sign * gamma_real[mu][s]
            half_re.append(signed_add(v[0][s], w, v[0][q]))
            half_im.append(signed_add(v[1][s], w, v[1][q]))
        else:
            w = sign * gamma_imag[mu][s]
            half_re.append(signed_add(v[0][s], -w, v[1][q]))
            half_im.append(signed_add(v[1][s], w, v[0][q]))
    return jnp.stack(half_re), jnp.stack(half_im)


def unproject(out, half, mu, sign):
    half_re, half_im = half
    for s in range(2):
        out[0][s] = out[0][s] + half_re[s]
        out[1][s] = out[1][s] + half_im[s]
    for s in range(2, 4):
        q = gamma_perm[mu][s]
        if gamma_real[mu][s]:
            w = sign * gamma_real[mu][s]
            out[0][s] = signed_add(out[0][s], w, half_re[q])
            out[1][s] = signed_add(out[1][s], w, half_im[q])
        else:
            w = sign * gamma_imag[mu][s]
            out[0][s] = signed_add(out[0][s], -w, half_im[q])
            out[1][s] = signed_add(out[1][s], w, half_re[q])


def link_apply(links, colour, mu, half):
    half_re, half_im = half
    out_re = out_im = None
    for b in range(3):
        u_re = links[colour, mu, 0, b][None]
        u_im = links[colour, mu, 1, b][None]
        h_re = half_re[:, b][:, None]
        h_im = half_im[:, b][:, None]
        term_re = u_re * h_re - u_im * h_im
        term_im = u_re * h_im + u_im * h_re
        out_re = term_re if b == 0 else out_re + term_re
        out_im = term_im if b == 0 else out_im + term_im
    return out_re, out_im


def link_apply_dagger(links, colour, mu, half):
    half_re, half_im = half
    out_re = out_im = None
    for b in range(3):
        u_re = links[colour, mu, 0, :, b][None]
        u_im = links[colour, mu, 1, :, b][None]
        h_re = half_re[:, b][:, None]
        h_im = half_im[:, b][:, None]
        term_re = u_re * h_re + u_im * h_im
        term_im = u_re * h_im - u_im * h_re
        out_re = term_re if b == 0 else out_re + term_re
        out_im = term_im if b == 0 else out_im + term_im
    return out_re, out_im


def split_dot(value, weights):
    rows = value.shape[0]
    high = value.astype(jnp.bfloat16)
    rest = value - high.astype(jnp.float32)
    mid = rest.astype(jnp.bfloat16)
    low = (rest - mid.astype(jnp.float32)).astype(jnp.bfloat16)
    out = jnp.dot(
        jnp.concatenate([high, mid, low], axis=0), weights, preferred_element_type=jnp.float32
    )
    return out[:rows] + out[rows : 2 * rows] + out[2 * rows :]


def iota(shape, dim):
    return lax.broadcasted_iota(jnp.int32, shape, dim)


def kernel(
    n_ta, n_xyz,
    source_hbm, gauge_hbm, clover_hbm, null_hbm, coarse_hbm,
    out_ref, error_ref,
    source_ref, gauge_ref, clover_ref, null_ref, coarse_ref,
    link_in, link_out, herm, resid, smooth, z_ref,
    halo_out, halo_in, partial, rest, null_even, spread, prolonged,
    stencil_in, cvec_out, cvec_in, dot_out, dot_in,
    load_sem, halo_send, halo_recv, stencil_send, stencil_recv, cvec_send, cvec_recv,
    dot_send, dot_recv,
):
    f32 = jnp.float32
    ta = lax.axis_index("ta")
    xyz = lax.axis_index("xyz")

    loads = [
        pltpu.make_async_copy(src, dst, load_sem.at[i])
        for i, (src, dst) in enumerate(
            [
                (gauge_hbm, gauge_ref),
                (clover_hbm, clover_ref),
                (source_hbm, source_ref),
                (coarse_hbm, coarse_ref),
                (null_hbm, null_ref),
            ]
        )
    ]

    def device_at(t_off, x_off):
        return (lax.rem(ta + t_off + n_ta, n_ta), lax.rem(xyz + x_off + n_xyz, n_xyz))

    def depth_peer(d):
        low = lax.rem(xyz, n_low)
        return (ta, xyz - low + lax.rem(low + d, n_low))

    def plane_peer(d):
        return (lax.rem(ta + d, n_ta), lax.rem(xyz + n_low * (d // n_ta), n_xyz))

    n_low = n_xyz // 2
    groups = [
        [depth_peer(d) for d in range(1, n_low)],
        [plane_peer(d) for d in range(1, 2 * n_ta)],
    ]
    barrier = pltpu.get_barrier_semaphore()
    for place in [(0, 1), (0, -1), (1, 0), (-1, 0)]:
        pl.semaphore_signal(barrier, inc=1, device_id=device_at(*place), device_id_type=MESH)
    for load in loads[:-1]:
        load.start()

    vreg = (8, 128)
    lane = iota(vreg, 1)
    subl = iota(vreg, 0)
    t_low = subl // 4
    x_pos = subl % 4
    y_pos = lane // 16
    z_pos = lane % 16
    parity = (ta + xyz + y_pos // 4 + z_pos // 4) % 2
    t_high = [parity, 1 - parity]

    def compact(natural):
        first = natural[..., :8, :]
        second = roll(natural[..., 8:, :], 64, -1)
        low = jnp.broadcast_to(parity == 0, first.shape)
        return jnp.where(low, first, second), jnp.where(low, second, first)

    def expand(even, odd):
        low = jnp.broadcast_to(parity == 0, even.shape)
        return jnp.where(low, even, odd), roll(jnp.where(low, odd, even), 64, -1)

    loads[0].wait()
    t_sign = jnp.where(ta == n_ta - 1, f32(0.5), f32(-0.5))
    for mu in range(4):
        planes = gauge_ref[pl.ds(18 * mu, 18)].astype(f32)
        pair = compact(planes)
        for colour in range(2):
            if mu == 0:
                inside = jnp.logical_not((t_high[colour] == 1) & (t_low == 1))
            elif mu == 1:
                inside = x_pos != 3
            elif mu == 2:
                inside = y_pos % 4 != 3
            else:
                inside = z_pos % 4 != 3
            weight_in = jnp.where(inside, f32(-0.5), f32(0.0))
            weight_out = jnp.where(inside, f32(0.0), t_sign if mu == 0 else f32(-0.5))
            for part in range(2):
                for row in range(3):
                    first = 9 * part + 3 * row
                    mine = pair[colour][first : first + 3]
                    link_in[colour, mu, part, :, row] = mine * weight_in
                    link_out[colour, mu, part, :, row] = mine * weight_out

    loads[1].wait()
    for chi in range(2):
        for col in range(6):
            row_at = 36 * chi + 6 * col
            for part in range(2):
                base = 72 * part
                line = clover_ref[pl.ds(base + row_at, 6)].astype(f32)
                column = jnp.stack(
                    [clover_ref[base + 36 * chi + 6 * r + col].astype(f32) for r in range(6)]
                )
                if part == 0:
                    sym = 0.5 * (column + line)
                    diag = iota((6, 1, 1), 0) == col
                    sym = sym + jnp.where(diag, f32(4.0 + mass_shift), f32(0.0))
                else:
                    sym = 0.5 * (column - line)
                pair = compact(sym)
                for colour in range(2):
                    herm[colour, part, chi, col] = pair[colour]

    loads[2].wait()
    pair = compact(source_ref[...])
    for colour in range(2):
        resid[colour] = pair[colour].reshape(2, 4, 3, 8, 128)
    smooth[...] = jnp.zeros_like(smooth)

    square = (128, 128)
    into = iota(square, 0)
    outof = iota(square, 1)
    block_weights = ((into % 16) // 4 == (outof % 16) // 4).astype(f32).astype(jnp.bfloat16)

    def load(ref, colour):
        value = ref[colour]
        return [[value[part, s] for s in range(4)] for part in range(2)]

    def block_wilson(v, colour):
        out = [[None] * 4, [None] * 4]
        for chi in range(2):
            v_re = jnp.concatenate([v[0][2 * chi], v[0][2 * chi + 1]])
            v_im = jnp.concatenate([v[1][2 * chi], v[1][2 * chi + 1]])
            acc_re = acc_im = None
            for col in range(6):
                h_re = herm[colour, 0, chi, col]
                h_im = herm[colour, 1, chi, col]
                term_re = h_re * v_re[col][None] - h_im * v_im[col][None]
                term_im = h_re * v_im[col][None] + h_im * v_re[col][None]
                acc_re = term_re if col == 0 else acc_re + term_re
                acc_im = term_im if col == 0 else acc_im + term_im
            for half in range(2):
                out[0][2 * chi + half] = acc_re[3 * half : 3 * half + 3]
                out[1][2 * chi + half] = acc_im[3 * half : 3 * half + 3]
        low = t_low == 0
        for mu in range(4):
            ahead = project(v, mu, -1)
            behind = link_apply_dagger(link_in, colour, mu, project(v, mu, 1))
            if mu == 0:
                ahead = [
                    roll(jnp.where(low, roll(w, 64, -1), w), 4, -2) for w in ahead
                ]
                behind = [
                    roll(jnp.where(low, w, roll(w, 64, -1)), 4, -2) for w in behind
                ]
            elif mu == 1:
                ahead = [roll(w, -1, -2) for w in ahead]
                behind = [roll(w, 1, -2) for w in behind]
            else:
                step = 16 if mu == 2 else 1
                ahead = [roll(w, -step, -1) for w in ahead]
                behind = [roll(w, step, -1) for w in behind]
            unproject(out, link_apply(link_in, colour, mu, ahead), mu, -1)
            unproject(out, behind, mu, 1)
        return out

    def each(function, *fields):
        return [[function(*(f[part][s] for f in fields)) for s in range(4)] for part in range(2)]

    def site_sum(pairs):
        total = None
        for left, right, sign in pairs:
            for s in range(4):
                term = left[s] * right[s]
                total = term if total is None else signed_add(total, sign, term)
        return total[0] + total[1] + total[2]

    def minimal_residual(colour):
        rho = load(resid, colour)
        image = block_wilson(rho, colour)
        second = block_wilson(image, colour)

        def dot(left, right):
            return [
                site_sum([(left[0], right[0], 1), (left[1], right[1], 1)]),
                site_sum([(left[0], right[1], 1), (left[1], right[0], -1)]),
            ]

        sums = dot(image, rho) + dot(second, rho) + dot(second, image)
        sums = sums + [dot_self(image), dot_self(second)]
        sums = split_dot(jnp.concatenate(sums, axis=0), block_weights).reshape(8, 8, 128)
        sums = jnp.sum(sums, axis=1, keepdims=True) / block_entries
        pr_re, pr_im, wr_re, wr_im, wp_re, wp_im, pp, ww = [sums[i] for i in range(8)]
        inverse = 1.0 / (pp + mean_eps)
        a_re = pr_re * inverse
        a_im = pr_im * inverse
        size = a_re * a_re + a_im * a_im
        s_re = pr_re - a_re * pp - (a_re * wr_re + a_im * wr_im) + size * wp_re
        s_im = pr_im - a_im * pp - (a_re * wr_im - a_im * wr_re) + size * wp_im
        squares = pp - 2.0 * (a_re * wp_re + a_im * wp_im) + size * ww
        inverse = 1.0 / (jnp.maximum(squares, f32(0.0)) + mean_eps)
        b_re = s_re * inverse
        b_im = s_im * inverse
        sum_re = jnp.broadcast_to(a_re + b_re, vreg)
        sum_im = jnp.broadcast_to(a_im + b_im, vreg)
        both_re = jnp.broadcast_to(a_re * b_re - a_im * b_im, vreg)
        both_im = jnp.broadcast_to(a_re * b_im + a_im * b_re, vreg)

        def combine(x, y):
            return [
                [
                    (sum_re * x[0][s] - sum_im * x[1][s])
                    - (both_re * y[0][s] - both_im * y[1][s])
                    for s in range(4)
                ],
                [
                    (sum_re * x[1][s] + sum_im * x[0][s])
                    - (both_re * y[1][s] + both_im * y[0][s])
                    for s in range(4)
                ],
            ]

        answer = combine(rho, image)
        return answer, each(jnp.subtract, rho, combine(image, second))

    def dot_self(value):
        return site_sum([(value[0], value[0], 1), (value[1], value[1], 1)])

    def flat(half):
        return jnp.concatenate([half[0].reshape(6, 8, 128), half[1].reshape(6, 8, 128)])

    def pack_x(half, face):
        groups = flat(half).reshape(3, 4, 8, 128)
        packed = None
        for j in range(4):
            moved = roll(groups[:, j], j - face, -2)
            packed = moved if j == 0 else jnp.where(x_pos == j, moved, packed)
        return packed

    def unpack_x(packed, face):
        rows = jnp.stack([roll(packed, face - j, -2) for j in range(4)], axis=1)
        rows = rows.reshape(2, 2, 3, 8, 128)
        return rows[0], rows[1]

    def pack_t(half, face, away):
        groups = flat(half).reshape(3, 4, 8, 128)
        here = (away == 0) if face == 0 else (away == 1)
        first = jnp.where(here, groups[:, 0], roll(groups[:, 1], 64, -1))
        second = jnp.where(here, groups[:, 2], roll(groups[:, 3], 64, -1))
        if face == 0:
            return jnp.where(t_low == 0, first, roll(second, 4, -2))
        return jnp.where(t_low == 1, first, roll(second, 4, -2))

    def unpack_t(packed):
        turned = roll(packed, 64, -1)
        rows = jnp.stack([roll(turned, 4, -2), roll(packed, 4, -2), turned, packed], axis=1)
        rows = rows.reshape(2, 2, 3, 8, 128)
        return rows[0], rows[1]

    def halo_copy(step, side):
        target = device_at(*((-1, 0), (1, 0), (0, -1), (0, 1))[side])
        return pltpu.make_async_remote_copy(
            src_ref=halo_out.at[step, side],
            dst_ref=halo_in.at[step, side],
            send_sem=halo_send.at[step, side],
            recv_sem=halo_recv.at[step, side],
            device_id=target,
            device_id_type=MESH,
        )

    def reduce_start(stage, value):
        dot_out[stage] = value
        for i, peer in enumerate(groups[stage]):
            pltpu.make_async_remote_copy(
                src_ref=dot_out.at[stage],
                dst_ref=dot_in.at[stage_at[stage] + i],
                send_sem=dot_send.at[stage],
                recv_sem=dot_recv.at[stage],
                device_id=peer,
                device_id_type=MESH,
            ).start()

    def reduce_finish(stage):
        count = len(groups[stage])
        arrived = dot_in.at[pl.ds(stage_at[stage], count)]
        pltpu.make_async_remote_copy(
            src_ref=arrived,
            dst_ref=arrived,
            send_sem=dot_send.at[stage],
            recv_sem=dot_recv.at[stage],
            device_id=groups[stage][0],
            device_id_type=MESH,
        ).wait()
        first = stage_at[stage]
        return dot_out[stage] + jnp.sum(dot_in[first : first + count], axis=0)

    stage_at = [0, n_low - 1]

    loads[3].wait()
    coarse_lane = iota((16, 128), 1)
    coarse_row = iota((16, 128), 0)
    on_diagonal = (coarse_lane % NVEC) == coarse_row
    def stencil_copy(part, side):
        t_off, x_off = areas[1 + side]
        third = pl.ds(3 * part, 3)
        return pltpu.make_async_remote_copy(
            src_ref=coarse_ref.at[third],
            dst_ref=stencil_in.at[side, third],
            send_sem=stencil_send.at[part, side],
            recv_sem=stencil_recv.at[part, side],
            device_id=device_at(-t_off, -x_off),
            device_id_type=MESH,
        )

    def solve(colour):
        z, rho = minimal_residual(colour)
        for part in range(2):
            for s in range(4):
                z_ref[part, s] = z[part][s]
                resid[colour, part, s] = rho[part][s]
                smooth[colour, part, s] = smooth[colour, part, s] + z[part][s]

    def subtract(colour, change):
        for part in range(2):
            for s in range(4):
                resid[colour, part, s] = resid[colour, part, s] - change[part][s]

    def exchange(step, meanwhile, early=None):
        colour = lax.rem(step, 2)
        other = 1 - colour
        z = [[z_ref[part, s] for s in range(4)] for part in range(2)]
        away = jnp.where(colour == 0, t_high[0], t_high[1])
        halo_out[step, 1] = pack_t(link_apply_dagger(link_out, colour, 0, project(z, 0, 1)), 3, away)
        halo_out[step, 3] = pack_x(link_apply_dagger(link_out, colour, 1, project(z, 1, 1)), 3)
        halo_out[step, 0] = pack_t(project(z, 0, -1), 0, away)
        halo_out[step, 2] = pack_x(project(z, 1, -1), 0)
        copies = [halo_copy(step, side) for side in range(4)]
        for copy in copies[::-1]:
            copy.start()
        meanwhile(step)
        change = [[jnp.zeros((3, 8, 128), f32)] * 4 for _ in range(2)]
        for mu in (2, 3):
            ahead = project(z, mu, -1)
            behind = link_apply_dagger(link_out, colour, mu, project(z, mu, 1))
            if mu == 2:
                ahead = [roll(w, -16, -1) for w in ahead]
                behind = [roll(w, 16, -1) for w in behind]
            else:
                ahead = [jnp.where(z_pos == 15, roll(w, 15, -1), roll(w, -1, -1)) for w in ahead]
                behind = [jnp.where(z_pos == 0, roll(w, -15, -1), roll(w, 1, -1)) for w in behind]
            unproject(change, link_apply(link_out, other, mu, ahead), mu, -1)
            unproject(change, behind, mu, 1)
        if early:
            early(change)
            change = [[jnp.zeros((3, 8, 128), f32)] * 4 for _ in range(2)]
        for copy in copies:
            copy.wait()
        ahead = unpack_t(halo_in[step, 0])
        unproject(change, link_apply(link_out, other, 0, ahead), 0, -1)
        first = (away == 1) & (t_low == 0)
        behind = [jnp.where(first, w, f32(0.0)) for w in unpack_t(halo_in[step, 1])]
        unproject(change, behind, 0, 1)
        ahead = unpack_x(halo_in[step, 2], 3)
        unproject(change, link_apply(link_out, other, 1, ahead), 1, -1)
        behind = [jnp.where(x_pos == 0, w, f32(0.0)) for w in unpack_x(halo_in[step, 3], 0)]
        unproject(change, behind, 1, 1)
        if early:
            return change
        subtract(other, change)
        return None

    def narrow_null(a, carry):
        even, _ = compact(null_ref[a].astype(f32))
        null_even[a] = even
        return carry

    def background(step):
        for side in range(4):
            stencil_copy(step, side).start()

        @pl.when(step == 0)
        def _():
            loads[4].wait()
            lax.fori_loop(0, NVEC, narrow_null, 0)

    def half_step(step, carry):
        exchange(step, background)
        solve(1 - lax.rem(step, 2))
        return carry

    areas = [(0, 0), (1, 0), (-1, 0), (0, 1), (0, -1)]
    loads[4].start()
    solve(0)
    pl.semaphore_wait(barrier, 4)
    lax.fori_loop(0, HALF_STEPS - 1, half_step, 0)

    def restrict_known(change):
        subtract(0, change)
        natural = expand(resid[0].reshape(24, 8, 128), resid[1].reshape(24, 8, 128))

        def restrict(a, carry):
            basis = null_ref[a].astype(f32)
            acc_re = acc_im = None
            for i, half in enumerate(natural):
                b_re = basis[0, :, 8 * i : 8 * i + 8]
                b_im = basis[1, :, 8 * i : 8 * i + 8]
                term_re = jnp.sum(b_re * half[:12] + b_im * half[12:], axis=0)
                term_im = jnp.sum(b_re * half[12:] - b_im * half[:12], axis=0)
                acc_re = term_re if i == 0 else acc_re + term_re
                acc_im = term_im if i == 0 else acc_im + term_im
            partial[0, a] = acc_re
            partial[1, a] = acc_im
            return carry

        lax.fori_loop(0, NVEC, restrict, 0)

    change = exchange(HALF_STEPS - 1, lambda step: None, restrict_known)
    change_re = jnp.concatenate(change[0])
    change_im = jnp.concatenate(change[1])

    def restrict_rest(a, carry):
        b_re = null_even[a, 0]
        b_im = null_even[a, 1]
        rest[0, a] = jnp.sum(b_re * change_re + b_im * change_im, axis=0)
        rest[1, a] = jnp.sum(b_re * change_im - b_im * change_re, axis=0)
        return carry

    lax.fori_loop(0, NVEC, restrict_rest, 0)
    site_agg = 4 * (into // 64) + (into % 16) // 4
    to_agg = (site_agg == outof // NVEC).astype(f32).astype(jnp.bfloat16)
    site_agg = 4 * (outof // 64) + (outof % 16) // 4
    from_agg = (site_agg == into // NVEC).astype(f32).astype(jnp.bfloat16)
    agg_weights = (into // NVEC == outof // NVEC).astype(f32).astype(jnp.bfloat16)
    row_z = (into % 16) // 4
    even_agg = 4 * ((ta + xyz + row_z) % 2) + row_z
    from_even = (even_agg == outof // NVEC).astype(f32).astype(jnp.bfloat16)
    rows = split_dot(jnp.sum(partial[...], axis=2).reshape(32, 128), to_agg)
    rows = rows - split_dot(jnp.sum(rest[...], axis=2).reshape(32, 128), from_even)

    def diagonal_row(both):
        return [
            jnp.sum(
                jnp.where(on_diagonal, both[16 * i : 16 * i + 16], f32(0.0)),
                axis=0,
                keepdims=True,
            )
            for i in range(2)
        ]

    vec = diagonal_row(rows)

    shift = jnp.full(vreg, 1.26, f32)

    row_at = iota(vreg, 0)
    agg_z = (lane % 64) // NVEC
    diag_shift = jnp.where(on_diagonal, jnp.broadcast_to(shift[:1], (16, 128)), f32(0.0))

    def tile(row_re, row_im):
        return jnp.where(
            row_at == 0, jnp.broadcast_to(row_re, vreg), jnp.broadcast_to(row_im, vreg)
        )

    near = [(0, -1), (0, 1), (1, 0), (-1, 0)]
    far = [(0, 2), (0, -2), (1, 1), (1, -1), (-1, 1), (-1, -1), (2, 0), (-2, 0)]
    around = far + near

    def cvec_copy(k, slot):
        t_off, x_off = around[slot]
        return pltpu.make_async_remote_copy(
            src_ref=cvec_out.at[k],
            dst_ref=cvec_in.at[k, slot],
            send_sem=cvec_send.at[k],
            recv_sem=cvec_recv.at[k],
            device_id=device_at(-t_off, -x_off),
            device_id_type=MESH,
        )

    def stencil_of(area, k):
        if area == 0:
            return coarse_ref[k, 0], coarse_ref[k, 1]
        return stencil_in[area - 1, k, 0], stencil_in[area - 1, k, 1]

    def add_term(acc, matrix, vec):
        m_re, m_im = matrix
        v_re, v_im = vec[0:1], vec[1:2]
        now = (m_re * v_re - m_im * v_im, m_re * v_im + m_im * v_re)
        return now if acc is None else (acc[0] + now[0], acc[1] + now[1])

    def local_terms(area, vec):
        m_re, m_im = stencil_of(area, 0)
        acc = add_term(None, (m_re - diag_shift, m_im), vec)
        over = roll(vec, 64, -1)
        p_re, p_im = stencil_of(area, 5)
        q_re, q_im = stencil_of(area, 6)
        acc = add_term(acc, (p_re + q_re, p_im + q_im), over)
        ahead = jnp.where(agg_z == 3, roll(vec, 48, -1), roll(vec, -16, -1))
        behind = jnp.where(agg_z == 0, roll(vec, -48, -1), roll(vec, 16, -1))
        acc = add_term(acc, stencil_of(area, 7), ahead)
        return add_term(acc, stencil_of(area, 8), behind)

    def finish(accs):
        rows = jnp.concatenate([w for acc in accs for w in acc], axis=0)
        rows = split_dot(rows, agg_weights)
        return [tile(*diagonal_row(rows[32 * i : 32 * i + 32])) for i in range(len(accs))]

    vecs = [tile(*vec)]
    for pair_at in range(GCR_ITERS // 2):
        own = vecs[-1]
        cvec_out[pair_at] = own
        copies = [cvec_copy(pair_at, slot) for slot in range(len(around))]
        for copy in copies:
            copy.start()
        accs = [local_terms(0, own)]
        if pair_at == 0:
            for part in range(3):
                for side in range(4):
                    stencil_copy(part, side).wait()
        arrived = cvec_in.at[pair_at]
        pltpu.make_async_remote_copy(
            src_ref=arrived,
            dst_ref=arrived,
            send_sem=cvec_send.at[pair_at],
            recv_sem=cvec_recv.at[pair_at],
            device_id=device_at(*around[0]),
            device_id_type=MESH,
        ).wait()
        have = {(0, 0): own}
        for slot, place in enumerate(around):
            have[place] = cvec_in[pair_at, slot]
        for area in range(1, 5):
            accs.append(local_terms(area, have[areas[area]]))
        for area, (t_off, x_off) in enumerate(areas):
            for side in range(4):
                t_step, x_step = areas[1 + side]
                there = have[(t_off + t_step, x_off + x_step)]
                accs[area] = add_term(accs[area], stencil_of(area, 1 + side), there)
        nexts = finish(accs)
        acc = local_terms(0, nexts[0])
        for side in range(4):
            acc = add_term(acc, stencil_of(0, 1 + side), nexts[1 + side])
        vecs = vecs + [nexts[0]] + finish([acc])

    basis_re = basis_im = jnp.zeros(vreg, f32)
    for k, vec in enumerate(vecs):
        basis_re = jnp.where(row_at == k, jnp.broadcast_to(vec[0:1], vreg), basis_re)
        basis_im = jnp.where(row_at == k, jnp.broadcast_to(vec[1:2], vreg), basis_im)

    gram = jnp.zeros(vreg, f32)
    for k in range(GCR_ITERS + 1):
        k_re = basis_re[k : k + 1]
        k_im = basis_im[k : k + 1]
        dot_re = jnp.sum(basis_re * k_re + basis_im * k_im, axis=1, keepdims=True)
        dot_im = jnp.sum(basis_re * k_im - basis_im * k_re, axis=1, keepdims=True)
        gram = jnp.where(lane == 2 * k, jnp.broadcast_to(dot_re, vreg), gram)
        gram = jnp.where(lane == 2 * k + 1, jnp.broadcast_to(dot_im, vreg), gram)
    reduce_start(0, gram)

    diag_rows = jnp.concatenate(
        [
            jnp.where(on_diagonal, jnp.broadcast_to(vec[part : part + 1], (16, 128)), f32(0.0))
            for vec in vecs[:GCR_ITERS]
            for part in range(2)
        ],
        axis=0,
    )
    spread[...] = split_dot(diag_rows, from_agg).reshape(GCR_ITERS, 2, NVEC, 1, 128)

    def prolong(entry, carry):
        n_re = null_ref[:, 0, entry].astype(f32)
        n_im = null_ref[:, 1, entry].astype(f32)
        for k in range(GCR_ITERS):
            e_re = spread[k, 0]
            e_im = spread[k, 1]
            prolonged[k, entry] = jnp.sum(n_re * e_re - n_im * e_im, axis=0)
            prolonged[k, 12 + entry] = jnp.sum(n_re * e_im + n_im * e_re, axis=0)
        return carry

    lax.fori_loop(0, 12, prolong, 0)
    halves = expand(smooth[0].reshape(24, 8, 128), smooth[1].reshape(24, 8, 128))
    for i, half in enumerate(halves):
        out_ref[:, 8 * i : 8 * i + 8] = half

    reduce_start(1, reduce_finish(0))
    gram = reduce_finish(1)

    columns = []
    for k in range(GCR_ITERS + 1):
        columns.append(
            (
                jnp.broadcast_to(gram[:, 2 * k : 2 * k + 1], vreg),
                jnp.broadcast_to(gram[:, 2 * k + 1 : 2 * k + 2], vreg),
            )
        )

    def scaled(a, x):
        return (a[0] * x[0] - a[1] * x[1], a[0] * x[1] + a[1] * x[0])

    def plus(x, y):
        return (x[0] + y[0], x[1] + y[1])

    def minus(x, y):
        return (x[0] - y[0], x[1] - y[1])

    def inner(pairs):
        terms = [
            term
            for left, image in pairs
            for term in (
                left[0] * image[0] + left[1] * image[1],
                left[0] * image[1] - left[1] * image[0],
            )
        ]
        sums = jnp.sum(jnp.stack(terms), axis=1, keepdims=True)
        sums = [jnp.broadcast_to(sums[i], vreg) for i in range(len(terms))]
        return list(zip(sums[::2], sums[1::2]))

    image_columns = [
        plus(columns[k + 1], (shift * columns[k][0], shift * columns[k][1]))
        for k in range(GCR_ITERS)
    ]
    remain = (jnp.where(row_at == 0, f32(1.0), f32(0.0)), jnp.zeros(vreg, f32))
    answer = (jnp.zeros(vreg, f32), jnp.zeros(vreg, f32))
    past = []
    for iteration in range(GCR_ITERS):
        direction = remain
        image = tuple(roll(w, 1, -2) + shift * w for w in direction)
        dots = None
        for k in range(iteration + 1):
            entry = tuple(jnp.broadcast_to(w[k : k + 1], vreg) for w in remain)
            now = scaled(entry, image_columns[k])
            dots = now if dots is None else plus(dots, now)
        if past:
            margins = inner([(old_image, dots) for _, old_image, _, _ in past])
            for margin, (old_direction, old_image, old_dots, inverse) in zip(margins, past):
                margin = (margin[0] * inverse, margin[1] * inverse)
                image = minus(image, scaled(margin, old_image))
                direction = minus(direction, scaled(margin, old_direction))
                dots = minus(dots, scaled(margin, old_dots))
        squares, along = inner([(image, dots), (remain, dots)])
        inverse = 1.0 / (jnp.maximum(squares[0], f32(0.0)) + mean_eps)
        step = (along[0] * inverse, -(along[1] * inverse))
        answer = plus(answer, scaled(step, direction))
        remain = minus(remain, scaled(step, image))
        past.append((direction, image, dots, inverse))

    error = scaled(answer, (basis_re, basis_im))
    error = [jnp.sum(w, axis=0, keepdims=True) for w in error]
    error_ref[0:1] = error[0]
    error_ref[1:2] = error[1]

    for k in range(GCR_ITERS):
        c_re = answer[0][k : k + 1]
        c_im = answer[1][k : k + 1]
        w_re = prolonged[k, :12]
        w_im = prolonged[k, 12:]
        now_re = c_re * w_re - c_im * w_im
        now_im = c_re * w_im + c_im * w_re
        sum_re = now_re if k == 0 else sum_re + now_re
        sum_im = now_im if k == 0 else sum_im + now_im
    out_ref[:12] = out_ref[:12] + sum_re
    out_ref[12:] = out_ref[12:] + sum_im


def solution(mesh):
    n_ta, n_xyz = mesh.shape["ta"], mesh.shape["xyz"]

    def shards(source, gauge_links, clover_raw, null_vectors, coarse_operator):
        f32 = jnp.float32
        dma = pltpu.SemaphoreType.DMA
        field, error = pl.pallas_call(
            functools.partial(kernel, n_ta, n_xyz),
            out_shape=(
                jax.ShapeDtypeStruct((24, 16, 128), f32),
                jax.ShapeDtypeStruct((2, 128), f32),
            ),
            in_specs=[pl.BlockSpec(memory_space=pltpu.HBM)] * 5,
            out_specs=(pl.BlockSpec(memory_space=pltpu.VMEM),) * 2,
            scratch_shapes=[
                pltpu.VMEM((24, 16, 128), f32),
                pltpu.VMEM((72, 16, 128), jnp.bfloat16),
                pltpu.VMEM((144, 16, 128), jnp.bfloat16),
                pltpu.VMEM((NVEC, 2, 12, 16, 128), jnp.bfloat16),
                pltpu.VMEM((9, 2, NVEC, 128), f32),
                pltpu.VMEM((2, 4, 2, 3, 3, 8, 128), f32),
                pltpu.VMEM((2, 4, 2, 3, 3, 8, 128), f32),
                pltpu.VMEM((2, 2, 2, 6, 6, 8, 128), f32),
                pltpu.VMEM((2, 2, 4, 3, 8, 128), f32),
                pltpu.VMEM((2, 2, 4, 3, 8, 128), f32),
                pltpu.VMEM((2, 4, 3, 8, 128), f32),
                pltpu.VMEM((HALF_STEPS, 4, 3, 8, 128), f32),
                pltpu.VMEM((HALF_STEPS, 4, 3, 8, 128), f32),
                pltpu.VMEM((2, NVEC, 8, 128), f32),
                pltpu.VMEM((2, NVEC, 8, 128), f32),
                pltpu.VMEM((NVEC, 2, 12, 8, 128), f32),
                pltpu.VMEM((GCR_ITERS, 2, NVEC, 1, 128), f32),
                pltpu.VMEM((GCR_ITERS, 24, 16, 128), f32),
                pltpu.VMEM((4, 9, 2, NVEC, 128), f32),
                pltpu.VMEM((GCR_ITERS // 2, 8, 128), f32),
                pltpu.VMEM((GCR_ITERS // 2, 12, 8, 128), f32),
                pltpu.VMEM((2, 8, 128), f32),
                pltpu.VMEM((n_xyz // 2 - 1 + 2 * n_ta - 1, 8, 128), f32),
                dma((5,)),
                dma((HALF_STEPS, 4)),
                dma((HALF_STEPS, 4)),
                dma((3, 4)),
                dma((3, 4)),
                dma((GCR_ITERS // 2,)),
                dma((GCR_ITERS // 2,)),
                dma((2,)),
                dma((2,)),
            ],
            compiler_params=pltpu.CompilerParams(
                collective_id=0, has_side_effects=True, vmem_limit_bytes=40 * 2**20
            ),
        )(
            *(
                pltpu.with_memory_space_constraint(operand, pltpu.HBM)
                for operand in (
                    source.reshape(24, 16, 128),
                    gauge_links.reshape(72, 16, 128),
                    clover_raw.reshape(144, 16, 128),
                    null_vectors.reshape(NVEC, 2, 12, 16, 128),
                    coarse_operator,
                )
            )
        )
        return field.reshape(source.shape), error

    in_specs = (
        P(None, None, None, "ta", "xyz", None),
        P(None, None, None, None, "ta", "xyz", None),
        P(None, None, None, None, "ta", "xyz", None),
        P(None, None, None, None, "ta", "xyz", None),
        P(None, None, None, ("ta", "xyz")),
    )
    out_specs = (P(None, None, None, "ta", "xyz", None), P(None, ("ta", "xyz")))
    return jax.shard_map(shards, mesh=mesh, in_specs=in_specs, out_specs=out_specs, check_vma=False)
```

```python
import functools

import jax
import jax.numpy as jnp
from jax import lax
from jax.experimental import pallas as pl
from jax.experimental.pallas import tpu as pltpu
from jax.sharding import PartitionSpec as P

MESH = pl.DeviceIdType.MESH
NVEC = 16
MR_STEPS = 2
SAP_CYCLES = 2
GCR_ITERS = 4
HALF_STEPS = 2 * SAP_CYCLES

mass_shift = 0.2
mean_eps = 1e-06
block_entries = 6144.0

gamma_perm = [[2, 3, 0, 1], [3, 2, 1, 0], [3, 2, 1, 0], [2, 3, 0, 1]]
gamma_real = [[1, 1, 1, 1], [0, 0, 0, 0], [-1, 1, 1, -1], [0, 0, 0, 0]]
gamma_imag = [[0, 0, 0, 0], [1, 1, -1, -1], [0, 0, 0, 0], [1, -1, -1, 1]]


def roll(value, shift, axis):
    axis = value.ndim + axis
    size = value.shape[axis]
    return pltpu.roll(value, shift % size, axis)


def signed_add(base, sign, value):
    return base + value if sign > 0 else base - value


def project(v, mu, sign):
    half_re, half_im = [], []
    for s in range(2):
        q = gamma_perm[mu][s]
        if gamma_real[mu][s]:
            w = sign * gamma_real[mu][s]
            half_re.append(signed_add(v[0][s], w, v[0][q]))
            half_im.append(signed_add(v[1][s], w, v[1][q]))
        else:
            w = sign * gamma_imag[mu][s]
            half_re.append(signed_add(v[0][s], -w, v[1][q]))
            half_im.append(signed_add(v[1][s], w, v[0][q]))
    return jnp.stack(half_re), jnp.stack(half_im)


def unproject(out, half, mu, sign):
    half_re, half_im = half
    for s in range(2):
        out[0][s] = out[0][s] + half_re[s]
        out[1][s] = out[1][s] + half_im[s]
    for s in range(2, 4):
        q = gamma_perm[mu][s]
        if gamma_real[mu][s]:
            w = sign * gamma_real[mu][s]
            out[0][s] = signed_add(out[0][s], w, half_re[q])
            out[1][s] = signed_add(out[1][s], w, half_im[q])
        else:
            w = sign * gamma_imag[mu][s]
            out[0][s] = signed_add(out[0][s], -w, half_im[q])
            out[1][s] = signed_add(out[1][s], w, half_re[q])


def link_apply(links, colour, mu, half):
    half_re, half_im = half
    out_re = out_im = None
    for b in range(3):
        u_re = links[colour, mu, 0, b][None]
        u_im = links[colour, mu, 1, b][None]
        h_re = half_re[:, b][:, None]
        h_im = half_im[:, b][:, None]
        term_re = u_re * h_re - u_im * h_im
        term_im = u_re * h_im + u_im * h_re
        out_re = term_re if b == 0 else out_re + term_re
        out_im = term_im if b == 0 else out_im + term_im
    return out_re, out_im


def link_apply_dagger(links, colour, mu, half):
    half_re, half_im = half
    out_re = out_im = None
    for b in range(3):
        u_re = links[colour, mu, 0, :, b][None]
        u_im = links[colour, mu, 1, :, b][None]
        h_re = half_re[:, b][:, None]
        h_im = half_im[:, b][:, None]
        term_re = u_re * h_re + u_im * h_im
        term_im = u_re * h_im - u_im * h_re
        out_re = term_re if b == 0 else out_re + term_re
        out_im = term_im if b == 0 else out_im + term_im
    return out_re, out_im


def split_dot(value, weights):
    rows = value.shape[0]
    high = value.astype(jnp.bfloat16)
    rest = value - high.astype(jnp.float32)
    mid = rest.astype(jnp.bfloat16)
    low = (rest - mid.astype(jnp.float32)).astype(jnp.bfloat16)
    out = jnp.dot(
        jnp.concatenate([high, mid, low], axis=0), weights, preferred_element_type=jnp.float32
    )
    return out[:rows] + out[rows : 2 * rows] + out[2 * rows :]


def iota(shape, dim):
    return lax.broadcasted_iota(jnp.int32, shape, dim)


def kernel(
    n_ta, n_xyz,
    source_hbm, gauge_hbm, clover_hbm, null_hbm, coarse_hbm,
    out_ref, error_ref,
    source_ref, gauge_ref, clover_ref, null_ref, coarse_ref,
    link_in, link_out, herm, resid, smooth, z_ref,
    halo_out, halo_in, partial, rest, null_even, spread, prolonged,
    stencil_in, cvec_out, cvec_in, dot_out, dot_in,
    load_sem, halo_send, halo_recv, stencil_send, stencil_recv, cvec_send, cvec_recv,
    dot_send, dot_recv,
):
    f32 = jnp.float32
    ta = lax.axis_index("ta")
    xyz = lax.axis_index("xyz")

    loads = [
        pltpu.make_async_copy(src, dst, load_sem.at[i])
        for i, (src, dst) in enumerate(
            [
                (gauge_hbm, gauge_ref),
                (clover_hbm, clover_ref),
                (source_hbm, source_ref),
                (coarse_hbm, coarse_ref),
                (null_hbm, null_ref),
            ]
        )
    ]

    def device_at(t_off, x_off):
        return (lax.rem(ta + t_off + n_ta, n_ta), lax.rem(xyz + x_off + n_xyz, n_xyz))

    def depth_peer(d):
        low = lax.rem(xyz, n_low)
        return (ta, xyz - low + lax.rem(low + d, n_low))

    def plane_peer(d):
        return (lax.rem(ta + d, n_ta), lax.rem(xyz + n_low * (d // n_ta), n_xyz))

    n_low = n_xyz // 2
    groups = [
        [depth_peer(d) for d in range(1, n_low)],
        [plane_peer(d) for d in range(1, 2 * n_ta)],
    ]
    barrier = pltpu.get_barrier_semaphore()
    for place in [(0, 1), (0, -1), (1, 0), (-1, 0)]:
        pl.semaphore_signal(barrier, inc=1, device_id=device_at(*place), device_id_type=MESH)
    for load in loads[:-1]:
        load.start()

    vreg = (8, 128)
    lane = iota(vreg, 1)
    subl = iota(vreg, 0)
    t_low = subl // 4
    x_pos = subl % 4
    y_pos = lane // 16
    z_pos = lane % 16
    parity = (ta + xyz + y_pos // 4 + z_pos // 4) % 2
    t_high = [parity, 1 - parity]

    def compact(natural):
        first = natural[..., :8, :]
        second = roll(natural[..., 8:, :], 64, -1)
        low = jnp.broadcast_to(parity == 0, first.shape)
        return jnp.where(low, first, second), jnp.where(low, second, first)

    def expand(even, odd):
        low = jnp.broadcast_to(parity == 0, even.shape)
        return jnp.where(low, even, odd), roll(jnp.where(low, odd, even), 64, -1)

    t_sign = jnp.where(ta == n_ta - 1, f32(0.5), f32(-0.5))

    def unpack_links(colour):
        for mu in range(4):
            mine = compact(gauge_ref[pl.ds(18 * mu, 18)].astype(f32))[colour]
            if mu == 0:
                inside = jnp.logical_not((t_high[colour] == 1) & (t_low == 1))
            elif mu == 1:
                inside = x_pos != 3
            elif mu == 2:
                inside = y_pos % 4 != 3
            else:
                inside = z_pos % 4 != 3
            weight_in = jnp.where(inside, f32(-0.5), f32(0.0))
            weight_out = jnp.where(inside, f32(0.0), t_sign if mu == 0 else f32(-0.5))
            for part in range(2):
                for row in range(3):
                    first = 9 * part + 3 * row
                    link_in[colour, mu, part, :, row] = mine[first : first + 3] * weight_in
                    link_out[colour, mu, part, :, row] = mine[first : first + 3] * weight_out

    def unpack_clover(colour):
        for chi in range(2):
            for col in range(6):
                for part in range(2):
                    base = 72 * part + 36 * chi
                    line = clover_ref[pl.ds(base + 6 * col, 6)].astype(f32)
                    column = jnp.stack(
                        [clover_ref[base + 6 * r + col].astype(f32) for r in range(6)]
                    )
                    if part == 0:
                        sym = 0.5 * (column + line)
                        diag = iota((6, 1, 1), 0) == col
                        sym = sym + jnp.where(diag, f32(4.0 + mass_shift), f32(0.0))
                    else:
                        sym = 0.5 * (column - line)
                    herm[colour, part, chi, col] = compact(sym)[colour]

    loads[0].wait()
    unpack_links(0)
    loads[1].wait()
    unpack_clover(0)
    loads[2].wait()
    pair = compact(source_ref[...])
    for colour in range(2):
        resid[colour] = pair[colour].reshape(2, 4, 3, 8, 128)
    smooth[...] = jnp.zeros_like(smooth)

    square = (128, 128)
    into = iota(square, 0)
    outof = iota(square, 1)
    block_weights = ((into % 16) // 4 == (outof % 16) // 4).astype(f32).astype(jnp.bfloat16)

    def load(ref, colour):
        value = ref[colour]
        return [[value[part, s] for s in range(4)] for part in range(2)]

    def block_wilson(v, colour):
        out = [[None] * 4, [None] * 4]
        for chi in range(2):
            v_re = jnp.concatenate([v[0][2 * chi], v[0][2 * chi + 1]])
            v_im = jnp.concatenate([v[1][2 * chi], v[1][2 * chi + 1]])
            acc_re = acc_im = None
            for col in range(6):
                h_re = herm[colour, 0, chi, col]
                h_im = herm[colour, 1, chi, col]
                term_re = h_re * v_re[col][None] - h_im * v_im[col][None]
                term_im = h_re * v_im[col][None] + h_im * v_re[col][None]
                acc_re = term_re if col == 0 else acc_re + term_re
                acc_im = term_im if col == 0 else acc_im + term_im
            for half in range(2):
                out[0][2 * chi + half] = acc_re[3 * half : 3 * half + 3]
                out[1][2 * chi + half] = acc_im[3 * half : 3 * half + 3]
        low = t_low == 0
        for mu in range(4):
            ahead = project(v, mu, -1)
            behind = link_apply_dagger(link_in, colour, mu, project(v, mu, 1))
            if mu == 0:
                ahead = [
                    roll(jnp.where(low, roll(w, 64, -1), w), 4, -2) for w in ahead
                ]
                behind = [
                    roll(jnp.where(low, w, roll(w, 64, -1)), 4, -2) for w in behind
                ]
            elif mu == 1:
                ahead = [roll(w, -1, -2) for w in ahead]
                behind = [roll(w, 1, -2) for w in behind]
            else:
                step = 16 if mu == 2 else 1
                ahead = [roll(w, -step, -1) for w in ahead]
                behind = [roll(w, step, -1) for w in behind]
            unproject(out, link_apply(link_in, colour, mu, ahead), mu, -1)
            unproject(out, behind, mu, 1)
        return out

    def each(function, *fields):
        return [[function(*(f[part][s] for f in fields)) for s in range(4)] for part in range(2)]

    def site_sum(pairs):
        total = None
        for left, right, sign in pairs:
            for s in range(4):
                term = left[s] * right[s]
                total = term if total is None else signed_add(total, sign, term)
        return total[0] + total[1] + total[2]

    def minimal_residual(colour):
        rho = load(resid, colour)
        image = block_wilson(rho, colour)
        second = block_wilson(image, colour)

        def dot(left, right):
            return [
                site_sum([(left[0], right[0], 1), (left[1], right[1], 1)]),
                site_sum([(left[0], right[1], 1), (left[1], right[0], -1)]),
            ]

        sums = dot(image, rho) + dot(second, rho) + dot(second, image)
        sums = sums + [dot_self(image), dot_self(second)]
        sums = split_dot(jnp.concatenate(sums, axis=0), block_weights).reshape(8, 8, 128)
        sums = jnp.sum(sums, axis=1, keepdims=True) / block_entries
        pr_re, pr_im, wr_re, wr_im, wp_re, wp_im, pp, ww = [sums[i] for i in range(8)]
        inverse = 1.0 / (pp + mean_eps)
        a_re = pr_re * inverse
        a_im = pr_im * inverse
        size = a_re * a_re + a_im * a_im
        s_re = pr_re - a_re * pp - (a_re * wr_re + a_im * wr_im) + size * wp_re
        s_im = pr_im - a_im * pp - (a_re * wr_im - a_im * wr_re) + size * wp_im
        squares = pp - 2.0 * (a_re * wp_re + a_im * wp_im) + size * ww
        inverse = 1.0 / (jnp.maximum(squares, f32(0.0)) + mean_eps)
        b_re = s_re * inverse
        b_im = s_im * inverse
        sum_re = jnp.broadcast_to(a_re + b_re, vreg)
        sum_im = jnp.broadcast_to(a_im + b_im, vreg)
        both_re = jnp.broadcast_to(a_re * b_re - a_im * b_im, vreg)
        both_im = jnp.broadcast_to(a_re * b_im + a_im * b_re, vreg)

        def combine(x, y):
            return [
                [
                    (sum_re * x[0][s] - sum_im * x[1][s])
                    - (both_re * y[0][s] - both_im * y[1][s])
                    for s in range(4)
                ],
                [
                    (sum_re * x[1][s] + sum_im * x[0][s])
                    - (both_re * y[1][s] + both_im * y[0][s])
                    for s in range(4)
                ],
            ]

        return combine(rho, image), lambda: each(jnp.subtract, rho, combine(image, second))

    def dot_self(value):
        return site_sum([(value[0], value[0], 1), (value[1], value[1], 1)])

    def flat(half):
        return jnp.concatenate([half[0].reshape(6, 8, 128), half[1].reshape(6, 8, 128)])

    def pack_x(half, face):
        groups = flat(half).reshape(3, 4, 8, 128)
        packed = None
        for j in range(4):
            moved = roll(groups[:, j], j - face, -2)
            packed = moved if j == 0 else jnp.where(x_pos == j, moved, packed)
        return packed

    def unpack_x(packed, face):
        rows = jnp.stack([roll(packed, face - j, -2) for j in range(4)], axis=1)
        rows = rows.reshape(2, 2, 3, 8, 128)
        return rows[0], rows[1]

    def pack_t(half, face, away):
        groups = flat(half).reshape(3, 4, 8, 128)
        here = (away == 0) if face == 0 else (away == 1)
        first = jnp.where(here, groups[:, 0], roll(groups[:, 1], 64, -1))
        second = jnp.where(here, groups[:, 2], roll(groups[:, 3], 64, -1))
        if face == 0:
            return jnp.where(t_low == 0, first, roll(second, 4, -2))
        return jnp.where(t_low == 1, first, roll(second, 4, -2))

    def unpack_t(packed):
        turned = roll(packed, 64, -1)
        rows = jnp.stack([roll(turned, 4, -2), roll(packed, 4, -2), turned, packed], axis=1)
        rows = rows.reshape(2, 2, 3, 8, 128)
        return rows[0], rows[1]

    def halo_copy(step, side):
        target = device_at(*((-1, 0), (1, 0), (0, -1), (0, 1))[side])
        return pltpu.make_async_remote_copy(
            src_ref=halo_out.at[step, side],
            dst_ref=halo_in.at[step, side],
            send_sem=halo_send.at[step, side],
            recv_sem=halo_recv.at[step, side],
            device_id=target,
            device_id_type=MESH,
        )

    def reduce_start(stage, value):
        dot_out[stage] = value
        for i, peer in enumerate(groups[stage]):
            pltpu.make_async_remote_copy(
                src_ref=dot_out.at[stage],
                dst_ref=dot_in.at[stage_at[stage] + i],
                send_sem=dot_send.at[stage],
                recv_sem=dot_recv.at[stage],
                device_id=peer,
                device_id_type=MESH,
            ).start()

    def reduce_finish(stage):
        count = len(groups[stage])
        arrived = dot_in.at[pl.ds(stage_at[stage], count)]
        pltpu.make_async_remote_copy(
            src_ref=arrived,
            dst_ref=arrived,
            send_sem=dot_send.at[stage],
            recv_sem=dot_recv.at[stage],
            device_id=groups[stage][0],
            device_id_type=MESH,
        ).wait()
        first = stage_at[stage]
        return dot_out[stage] + jnp.sum(dot_in[first : first + count], axis=0)

    stage_at = [0, n_low - 1]

    coarse_lane = iota((16, 128), 1)
    coarse_row = iota((16, 128), 0)
    on_diagonal = (coarse_lane % NVEC) == coarse_row
    def stencil_copy(part, side):
        t_off, x_off = areas[1 + side]
        third = pl.ds(3 * part, 3)
        return pltpu.make_async_remote_copy(
            src_ref=coarse_ref.at[third],
            dst_ref=stencil_in.at[side, third],
            send_sem=stencil_send.at[part, side],
            recv_sem=stencil_recv.at[part, side],
            device_id=device_at(-t_off, -x_off),
            device_id_type=MESH,
        )

    def send_faces(step, colour, z):
        away = jnp.where(colour == 0, t_high[0], t_high[1])
        halo_out[step, 2] = pack_x(project(z, 1, -1), 0)
        halo_copy(step, 2).start()
        halo_out[step, 3] = pack_x(link_apply_dagger(link_out, colour, 1, project(z, 1, 1)), 3)
        halo_copy(step, 3).start()
        halo_out[step, 0] = pack_t(project(z, 0, -1), 0, away)
        halo_copy(step, 0).start()
        halo_out[step, 1] = pack_t(link_apply_dagger(link_out, colour, 0, project(z, 0, 1)), 3, away)
        halo_copy(step, 1).start()

    def solve(step, colour):
        z, remainder = minimal_residual(colour)
        if isinstance(step, int):
            pl.semaphore_wait(barrier, 4)
        send_faces(step, colour, z)
        rho = remainder()
        for part in range(2):
            for s in range(4):
                z_ref[part, s] = z[part][s]
                resid[colour, part, s] = rho[part][s]
                smooth[colour, part, s] = smooth[colour, part, s] + z[part][s]

    def subtract(colour, change):
        for part in range(2):
            for s in range(4):
                resid[colour, part, s] = resid[colour, part, s] - change[part][s]

    def exchange(step, meanwhile, early=None):
        colour = lax.rem(step, 2)
        other = 1 - colour
        z = [[z_ref[part, s] for s in range(4)] for part in range(2)]
        away = jnp.where(colour == 0, t_high[0], t_high[1])
        meanwhile(step)
        change = [[jnp.zeros((3, 8, 128), f32)] * 4 for _ in range(2)]
        for mu in (2, 3):
            ahead = project(z, mu, -1)
            behind = link_apply_dagger(link_out, colour, mu, project(z, mu, 1))
            if mu == 2:
                ahead = [roll(w, -16, -1) for w in ahead]
                behind = [roll(w, 16, -1) for w in behind]
            else:
                ahead = [jnp.where(z_pos == 15, roll(w, 15, -1), roll(w, -1, -1)) for w in ahead]
                behind = [jnp.where(z_pos == 0, roll(w, -15, -1), roll(w, 1, -1)) for w in behind]
            unproject(change, link_apply(link_out, other, mu, ahead), mu, -1)
            unproject(change, behind, mu, 1)
        if early:
            early(change)
            change = [[jnp.zeros((3, 8, 128), f32)] * 4 for _ in range(2)]
        halo_copy(step, 0).wait()
        halo_copy(step, 1).wait()
        ahead = unpack_t(halo_in[step, 0])
        unproject(change, link_apply(link_out, other, 0, ahead), 0, -1)
        first = (away == 1) & (t_low == 0)
        behind = [jnp.where(first, w, f32(0.0)) for w in unpack_t(halo_in[step, 1])]
        unproject(change, behind, 0, 1)
        halo_copy(step, 2).wait()
        halo_copy(step, 3).wait()
        ahead = unpack_x(halo_in[step, 2], 3)
        unproject(change, link_apply(link_out, other, 1, ahead), 1, -1)
        behind = [jnp.where(x_pos == 0, w, f32(0.0)) for w in unpack_x(halo_in[step, 3], 0)]
        unproject(change, behind, 1, 1)
        if early:
            return change
        subtract(other, change)
        return None

    def narrow_null(a, carry):
        even, _ = compact(null_ref[a].astype(f32))
        null_even[a] = even
        return carry

    def background(step):
        for side in range(4):
            stencil_copy(step, side).start()

        @pl.when(step == 0)
        def _():
            unpack_links(1)
            unpack_clover(1)

        @pl.when(step == 1)
        def _():
            loads[4].wait()
            lax.fori_loop(0, NVEC, narrow_null, 0)

    def half_step(step, carry):
        exchange(step, background)
        solve(step + 1, 1 - lax.rem(step, 2))
        return carry

    areas = [(0, 0), (1, 0), (-1, 0), (0, 1), (0, -1)]
    loads[4].start()
    solve(0, 0)
    loads[3].wait()
    lax.fori_loop(0, HALF_STEPS - 1, half_step, 0)

    def restrict_known(change):
        subtract(0, change)
        natural = expand(resid[0].reshape(24, 8, 128), resid[1].reshape(24, 8, 128))

        def restrict(a, carry):
            basis = null_ref[a].astype(f32)
            acc_re = acc_im = None
            for i, half in enumerate(natural):
                b_re = basis[0, :, 8 * i : 8 * i + 8]
                b_im = basis[1, :, 8 * i : 8 * i + 8]
                term_re = jnp.sum(b_re * half[:12] + b_im * half[12:], axis=0)
                term_im = jnp.sum(b_re * half[12:] - b_im * half[:12], axis=0)
                acc_re = term_re if i == 0 else acc_re + term_re
                acc_im = term_im if i == 0 else acc_im + term_im
            partial[0, a] = acc_re
            partial[1, a] = acc_im
            return carry

        lax.fori_loop(0, NVEC, restrict, 0)

    change = exchange(HALF_STEPS - 1, lambda step: None, restrict_known)
    change_re = jnp.concatenate(change[0])
    change_im = jnp.concatenate(change[1])

    def restrict_rest(a, carry):
        b_re = null_even[a, 0]
        b_im = null_even[a, 1]
        rest[0, a] = jnp.sum(b_re * change_re + b_im * change_im, axis=0)
        rest[1, a] = jnp.sum(b_re * change_im - b_im * change_re, axis=0)
        return carry

    lax.fori_loop(0, NVEC, restrict_rest, 0)
    site_agg = 4 * (into // 64) + (into % 16) // 4
    to_agg = (site_agg == outof // NVEC).astype(f32).astype(jnp.bfloat16)
    site_agg = 4 * (outof // 64) + (outof % 16) // 4
    from_agg = (site_agg == into // NVEC).astype(f32).astype(jnp.bfloat16)
    agg_weights = (into // NVEC == outof // NVEC).astype(f32).astype(jnp.bfloat16)
    row_z = (into % 16) // 4
    even_agg = 4 * ((ta + xyz + row_z) % 2) + row_z
    from_even = (even_agg == outof // NVEC).astype(f32).astype(jnp.bfloat16)
    rows = split_dot(jnp.sum(partial[...], axis=2).reshape(32, 128), to_agg)
    rows = rows - split_dot(jnp.sum(rest[...], axis=2).reshape(32, 128), from_even)

    def diagonal_row(both):
        return [
            jnp.sum(
                jnp.where(on_diagonal, both[16 * i : 16 * i + 16], f32(0.0)),
                axis=0,
                keepdims=True,
            )
            for i in range(2)
        ]

    vec = diagonal_row(rows)

    shift = jnp.full(vreg, 1.26, f32)

    row_at = iota(vreg, 0)
    agg_z = (lane % 64) // NVEC
    diag_shift = jnp.where(on_diagonal, jnp.broadcast_to(shift[:1], (16, 128)), f32(0.0))

    def tile(row_re, row_im):
        return jnp.where(
            row_at == 0, jnp.broadcast_to(row_re, vreg), jnp.broadcast_to(row_im, vreg)
        )

    near = [(0, -1), (0, 1), (1, 0), (-1, 0)]
    far = [(0, 2), (0, -2), (1, 1), (1, -1), (-1, 1), (-1, -1), (2, 0), (-2, 0)]
    around = far + near

    def cvec_copy(k, slot):
        t_off, x_off = around[slot]
        return pltpu.make_async_remote_copy(
            src_ref=cvec_out.at[k],
            dst_ref=cvec_in.at[k, slot],
            send_sem=cvec_send.at[k],
            recv_sem=cvec_recv.at[k],
            device_id=device_at(-t_off, -x_off),
            device_id_type=MESH,
        )

    def stencil_of(area, k):
        if area == 0:
            return coarse_ref[k, 0], coarse_ref[k, 1]
        return stencil_in[area - 1, k, 0], stencil_in[area - 1, k, 1]

    def add_term(acc, matrix, vec):
        m_re, m_im = matrix
        v_re, v_im = vec[0:1], vec[1:2]
        now = (m_re * v_re - m_im * v_im, m_re * v_im + m_im * v_re)
        return now if acc is None else (acc[0] + now[0], acc[1] + now[1])

    def local_terms(area, vec):
        m_re, m_im = stencil_of(area, 0)
        acc = add_term(None, (m_re - diag_shift, m_im), vec)
        over = roll(vec, 64, -1)
        p_re, p_im = stencil_of(area, 5)
        q_re, q_im = stencil_of(area, 6)
        acc = add_term(acc, (p_re + q_re, p_im + q_im), over)
        ahead = jnp.where(agg_z == 3, roll(vec, 48, -1), roll(vec, -16, -1))
        behind = jnp.where(agg_z == 0, roll(vec, -48, -1), roll(vec, 16, -1))
        acc = add_term(acc, stencil_of(area, 7), ahead)
        return add_term(acc, stencil_of(area, 8), behind)

    def finish(accs):
        rows = jnp.concatenate([w for acc in accs for w in acc], axis=0)
        rows = split_dot(rows, agg_weights)
        return [tile(*diagonal_row(rows[32 * i : 32 * i + 32])) for i in range(len(accs))]

    vecs = [tile(*vec)]
    for pair_at in range(GCR_ITERS // 2):
        own = vecs[-1]
        cvec_out[pair_at] = own
        copies = [cvec_copy(pair_at, slot) for slot in range(len(around))]
        for copy in copies:
            copy.start()
        accs = [local_terms(0, own)]
        if pair_at == 0:
            for part in range(3):
                for side in range(4):
                    stencil_copy(part, side).wait()
        arrived = cvec_in.at[pair_at]
        pltpu.make_async_remote_copy(
            src_ref=arrived,
            dst_ref=arrived,
            send_sem=cvec_send.at[pair_at],
            recv_sem=cvec_recv.at[pair_at],
            device_id=device_at(*around[0]),
            device_id_type=MESH,
        ).wait()
        have = {(0, 0): own}
        for slot, place in enumerate(around):
            have[place] = cvec_in[pair_at, slot]
        for area in range(1, 5):
            accs.append(local_terms(area, have[areas[area]]))
        for area, (t_off, x_off) in enumerate(areas):
            for side in range(4):
                t_step, x_step = areas[1 + side]
                there = have[(t_off + t_step, x_off + x_step)]
                accs[area] = add_term(accs[area], stencil_of(area, 1 + side), there)
        nexts = finish(accs)
        acc = local_terms(0, nexts[0])
        for side in range(4):
            acc = add_term(acc, stencil_of(0, 1 + side), nexts[1 + side])
        vecs = vecs + [nexts[0]] + finish([acc])

    basis_re = basis_im = jnp.zeros(vreg, f32)
    for k, vec in enumerate(vecs):
        basis_re = jnp.where(row_at == k, jnp.broadcast_to(vec[0:1], vreg), basis_re)
        basis_im = jnp.where(row_at == k, jnp.broadcast_to(vec[1:2], vreg), basis_im)

    gram = jnp.zeros(vreg, f32)
    for k in range(GCR_ITERS + 1):
        k_re = basis_re[k : k + 1]
        k_im = basis_im[k : k + 1]
        dot_re = jnp.sum(basis_re * k_re + basis_im * k_im, axis=1, keepdims=True)
        dot_im = jnp.sum(basis_re * k_im - basis_im * k_re, axis=1, keepdims=True)
        gram = jnp.where(lane == 2 * k, jnp.broadcast_to(dot_re, vreg), gram)
        gram = jnp.where(lane == 2 * k + 1, jnp.broadcast_to(dot_im, vreg), gram)
    reduce_start(0, gram)

    diag_rows = jnp.concatenate(
        [
            jnp.where(on_diagonal, jnp.broadcast_to(vec[part : part + 1], (16, 128)), f32(0.0))
            for vec in vecs[:GCR_ITERS]
            for part in range(2)
        ],
        axis=0,
    )
    spread[...] = split_dot(diag_rows, from_agg).reshape(GCR_ITERS, 2, NVEC, 1, 128)

    def prolong(entry, carry):
        n_re = null_ref[:, 0, entry].astype(f32)
        n_im = null_ref[:, 1, entry].astype(f32)
        for k in range(GCR_ITERS):
            e_re = spread[k, 0]
            e_im = spread[k, 1]
            prolonged[k, entry] = jnp.sum(n_re * e_re - n_im * e_im, axis=0)
            prolonged[k, 12 + entry] = jnp.sum(n_re * e_im + n_im * e_re, axis=0)
        return carry

    lax.fori_loop(0, 12, prolong, 0)
    halves = expand(smooth[0].reshape(24, 8, 128), smooth[1].reshape(24, 8, 128))
    for i, half in enumerate(halves):
        out_ref[:, 8 * i : 8 * i + 8] = half

    reduce_start(1, reduce_finish(0))
    gram = reduce_finish(1)

    columns = []
    for k in range(GCR_ITERS + 1):
        columns.append(
            (
                jnp.broadcast_to(gram[:, 2 * k : 2 * k + 1], vreg),
                jnp.broadcast_to(gram[:, 2 * k + 1 : 2 * k + 2], vreg),
            )
        )

    def scaled(a, x):
        return (a[0] * x[0] - a[1] * x[1], a[0] * x[1] + a[1] * x[0])

    def plus(x, y):
        return (x[0] + y[0], x[1] + y[1])

    def minus(x, y):
        return (x[0] - y[0], x[1] - y[1])

    def inner(pairs):
        terms = [
            term
            for left, image in pairs
            for term in (
                left[0] * image[0] + left[1] * image[1],
                left[0] * image[1] - left[1] * image[0],
            )
        ]
        sums = jnp.sum(jnp.stack(terms), axis=1, keepdims=True)
        sums = [jnp.broadcast_to(sums[i], vreg) for i in range(len(terms))]
        return list(zip(sums[::2], sums[1::2]))

    image_columns = [
        plus(columns[k + 1], (shift * columns[k][0], shift * columns[k][1]))
        for k in range(GCR_ITERS)
    ]
    remain = (jnp.where(row_at == 0, f32(1.0), f32(0.0)), jnp.zeros(vreg, f32))
    answer = (jnp.zeros(vreg, f32), jnp.zeros(vreg, f32))
    past = []
    for iteration in range(GCR_ITERS):
        direction = remain
        image = tuple(roll(w, 1, -2) + shift * w for w in direction)
        dots = None
        for k in range(iteration + 1):
            entry = tuple(jnp.broadcast_to(w[k : k + 1], vreg) for w in remain)
            now = scaled(entry, image_columns[k])
            dots = now if dots is None else plus(dots, now)
        if past:
            margins = inner([(old_image, dots) for _, old_image, _, _ in past])
            for margin, (old_direction, old_image, old_dots, inverse) in zip(margins, past):
                margin = (margin[0] * inverse, margin[1] * inverse)
                image = minus(image, scaled(margin, old_image))
                direction = minus(direction, scaled(margin, old_direction))
                dots = minus(dots, scaled(margin, old_dots))
        squares, along = inner([(image, dots), (remain, dots)])
        inverse = 1.0 / (jnp.maximum(squares[0], f32(0.0)) + mean_eps)
        step = (along[0] * inverse, -(along[1] * inverse))
        answer = plus(answer, scaled(step, direction))
        remain = minus(remain, scaled(step, image))
        past.append((direction, image, dots, inverse))

    error = scaled(answer, (basis_re, basis_im))
    error = [jnp.sum(w, axis=0, keepdims=True) for w in error]
    error_ref[0:1] = error[0]
    error_ref[1:2] = error[1]

    for k in range(GCR_ITERS):
        c_re = answer[0][k : k + 1]
        c_im = answer[1][k : k + 1]
        w_re = prolonged[k, :12]
        w_im = prolonged[k, 12:]
        now_re = c_re * w_re - c_im * w_im
        now_im = c_re * w_im + c_im * w_re
        sum_re = now_re if k == 0 else sum_re + now_re
        sum_im = now_im if k == 0 else sum_im + now_im
    out_ref[:12] = out_ref[:12] + sum_re
    out_ref[12:] = out_ref[12:] + sum_im


def solution(mesh):
    n_ta, n_xyz = mesh.shape["ta"], mesh.shape["xyz"]

    def shards(source, gauge_links, clover_raw, null_vectors, coarse_operator):
        f32 = jnp.float32
        dma = pltpu.SemaphoreType.DMA
        field, error = pl.pallas_call(
            functools.partial(kernel, n_ta, n_xyz),
            out_shape=(
                jax.ShapeDtypeStruct((24, 16, 128), f32),
                jax.ShapeDtypeStruct((2, 128), f32),
            ),
            in_specs=[pl.BlockSpec(memory_space=pltpu.HBM)] * 5,
            out_specs=(pl.BlockSpec(memory_space=pltpu.VMEM),) * 2,
            scratch_shapes=[
                pltpu.VMEM((24, 16, 128), f32),
                pltpu.VMEM((72, 16, 128), jnp.bfloat16),
                pltpu.VMEM((144, 16, 128), jnp.bfloat16),
                pltpu.VMEM((NVEC, 2, 12, 16, 128), jnp.bfloat16),
                pltpu.VMEM((9, 2, NVEC, 128), f32),
                pltpu.VMEM((2, 4, 2, 3, 3, 8, 128), f32),
                pltpu.VMEM((2, 4, 2, 3, 3, 8, 128), f32),
                pltpu.VMEM((2, 2, 2, 6, 6, 8, 128), f32),
                pltpu.VMEM((2, 2, 4, 3, 8, 128), f32),
                pltpu.VMEM((2, 2, 4, 3, 8, 128), f32),
                pltpu.VMEM((2, 4, 3, 8, 128), f32),
                pltpu.VMEM((HALF_STEPS, 4, 3, 8, 128), f32),
                pltpu.VMEM((HALF_STEPS, 4, 3, 8, 128), f32),
                pltpu.VMEM((2, NVEC, 8, 128), f32),
                pltpu.VMEM((2, NVEC, 8, 128), f32),
                pltpu.VMEM((NVEC, 2, 12, 8, 128), f32),
                pltpu.VMEM((GCR_ITERS, 2, NVEC, 1, 128), f32),
                pltpu.VMEM((GCR_ITERS, 24, 16, 128), f32),
                pltpu.VMEM((4, 9, 2, NVEC, 128), f32),
                pltpu.VMEM((GCR_ITERS // 2, 8, 128), f32),
                pltpu.VMEM((GCR_ITERS // 2, 12, 8, 128), f32),
                pltpu.VMEM((2, 8, 128), f32),
                pltpu.VMEM((n_xyz // 2 - 1 + 2 * n_ta - 1, 8, 128), f32),
                dma((5,)),
                dma((HALF_STEPS, 4)),
                dma((HALF_STEPS, 4)),
                dma((3, 4)),
                dma((3, 4)),
                dma((GCR_ITERS // 2,)),
                dma((GCR_ITERS // 2,)),
                dma((2,)),
                dma((2,)),
            ],
            compiler_params=pltpu.CompilerParams(
                collective_id=0, has_side_effects=True, vmem_limit_bytes=40 * 2**20
            ),
        )(
            *(
                pltpu.with_memory_space_constraint(operand, pltpu.HBM)
                for operand in (
                    source.reshape(24, 16, 128),
                    gauge_links.reshape(72, 16, 128),
                    clover_raw.reshape(144, 16, 128),
                    null_vectors.reshape(NVEC, 2, 12, 16, 128),
                    coarse_operator,
                )
            )
        )
        return field.reshape(source.shape), error

    in_specs = (
        P(None, None, None, "ta", "xyz", None),
        P(None, None, None, None, "ta", "xyz", None),
        P(None, None, None, None, "ta", "xyz", None),
        P(None, None, None, None, "ta", "xyz", None),
        P(None, None, None, ("ta", "xyz")),
    )
    out_specs = (P(None, None, None, "ta", "xyz", None), P(None, ("ta", "xyz")))
    return jax.shard_map(shards, mesh=mesh, in_specs=in_specs, out_specs=out_specs, check_vma=False)
```

```python
import functools

import jax
import jax.numpy as jnp
from jax import lax
from jax.experimental import pallas as pl
from jax.experimental.pallas import tpu as pltpu
from jax.sharding import PartitionSpec as P

MESH = pl.DeviceIdType.MESH
NVEC = 16
MR_STEPS = 2
SAP_CYCLES = 2
GCR_ITERS = 4
HALF_STEPS = 2 * SAP_CYCLES

mass_shift = 0.2
mean_eps = 1e-06
block_entries = 6144.0

gamma_perm = [[2, 3, 0, 1], [3, 2, 1, 0], [3, 2, 1, 0], [2, 3, 0, 1]]
gamma_real = [[1, 1, 1, 1], [0, 0, 0, 0], [-1, 1, 1, -1], [0, 0, 0, 0]]
gamma_imag = [[0, 0, 0, 0], [1, 1, -1, -1], [0, 0, 0, 0], [1, -1, -1, 1]]


def roll(value, shift, axis):
    axis = value.ndim + axis
    size = value.shape[axis]
    return pltpu.roll(value, shift % size, axis)


def signed_add(base, sign, value):
    return base + value if sign > 0 else base - value


def project(v, mu, sign):
    half_re, half_im = [], []
    for s in range(2):
        q = gamma_perm[mu][s]
        if gamma_real[mu][s]:
            w = sign * gamma_real[mu][s]
            half_re.append(signed_add(v[0][s], w, v[0][q]))
            half_im.append(signed_add(v[1][s], w, v[1][q]))
        else:
            w = sign * gamma_imag[mu][s]
            half_re.append(signed_add(v[0][s], -w, v[1][q]))
            half_im.append(signed_add(v[1][s], w, v[0][q]))
    return jnp.stack(half_re), jnp.stack(half_im)


def unproject(out, half, mu, sign):
    half_re, half_im = half
    for s in range(2):
        out[0][s] = out[0][s] + half_re[s]
        out[1][s] = out[1][s] + half_im[s]
    for s in range(2, 4):
        q = gamma_perm[mu][s]
        if gamma_real[mu][s]:
            w = sign * gamma_real[mu][s]
            out[0][s] = signed_add(out[0][s], w, half_re[q])
            out[1][s] = signed_add(out[1][s], w, half_im[q])
        else:
            w = sign * gamma_imag[mu][s]
            out[0][s] = signed_add(out[0][s], -w, half_im[q])
            out[1][s] = signed_add(out[1][s], w, half_re[q])


def link_apply(links, colour, mu, half):
    half_re, half_im = half
    out_re = out_im = None
    for b in range(3):
        u_re = links[colour, mu, 0, b][None]
        u_im = links[colour, mu, 1, b][None]
        h_re = half_re[:, b][:, None]
        h_im = half_im[:, b][:, None]
        term_re = u_re * h_re - u_im * h_im
        term_im = u_re * h_im + u_im * h_re
        out_re = term_re if b == 0 else out_re + term_re
        out_im = term_im if b == 0 else out_im + term_im
    return out_re, out_im


def link_apply_dagger(links, colour, mu, half):
    half_re, half_im = half
    out_re = out_im = None
    for b in range(3):
        u_re = links[colour, mu, 0, :, b][None]
        u_im = links[colour, mu, 1, :, b][None]
        h_re = half_re[:, b][:, None]
        h_im = half_im[:, b][:, None]
        term_re = u_re * h_re + u_im * h_im
        term_im = u_re * h_im - u_im * h_re
        out_re = term_re if b == 0 else out_re + term_re
        out_im = term_im if b == 0 else out_im + term_im
    return out_re, out_im


def split_dot(value, weights):
    rows = value.shape[0]
    high = value.astype(jnp.bfloat16)
    rest = value - high.astype(jnp.float32)
    mid = rest.astype(jnp.bfloat16)
    low = (rest - mid.astype(jnp.float32)).astype(jnp.bfloat16)
    out = jnp.dot(
        jnp.concatenate([high, mid, low], axis=0), weights, preferred_element_type=jnp.float32
    )
    return out[:rows] + out[rows : 2 * rows] + out[2 * rows :]


def iota(shape, dim):
    return lax.broadcasted_iota(jnp.int32, shape, dim)


def kernel(
    n_ta, n_xyz,
    source_hbm, gauge_hbm, clover_hbm, null_hbm, coarse_hbm,
    out_ref, error_ref,
    source_ref, gauge_ref, clover_ref, null_ref, coarse_ref,
    link_in, link_out, herm, resid, smooth, z_ref,
    halo_out, halo_in, partial, rest, null_even, spread, prolonged,
    stencil_in, cvec_out, cvec_in, dot_out, dot_in,
    load_sem, halo_send, halo_recv, stencil_send, stencil_recv, cvec_send, cvec_recv,
    dot_send, dot_recv,
):
    f32 = jnp.float32
    ta = lax.axis_index("ta")
    xyz = lax.axis_index("xyz")

    loads = [
        pltpu.make_async_copy(src, dst, load_sem.at[i])
        for i, (src, dst) in enumerate(
            [
                (gauge_hbm, gauge_ref),
                (clover_hbm, clover_ref),
                (source_hbm, source_ref),
                (coarse_hbm, coarse_ref),
                (null_hbm, null_ref),
            ]
        )
    ]

    def device_at(t_off, x_off):
        return (lax.rem(ta + t_off + n_ta, n_ta), lax.rem(xyz + x_off + n_xyz, n_xyz))

    def depth_peer(d):
        low = lax.rem(xyz, n_low)
        return (ta, xyz - low + lax.rem(low + d, n_low))

    def plane_peer(d):
        return (lax.rem(ta + d, n_ta), lax.rem(xyz + n_low * (d // n_ta), n_xyz))

    n_low = n_xyz // 2
    groups = [
        [depth_peer(d) for d in range(1, n_low)],
        [plane_peer(d) for d in range(1, 2 * n_ta)],
    ]
    barrier = pltpu.get_barrier_semaphore()
    for place in [(0, 1), (0, -1), (1, 0), (-1, 0)]:
        pl.semaphore_signal(barrier, inc=1, device_id=device_at(*place), device_id_type=MESH)
    for load in loads[:-1]:
        load.start()

    vreg = (8, 128)
    lane = iota(vreg, 1)
    subl = iota(vreg, 0)
    t_low = subl // 4
    x_pos = subl % 4
    y_pos = lane // 16
    z_pos = lane % 16
    parity = (ta + xyz + y_pos // 4 + z_pos // 4) % 2
    t_high = [parity, 1 - parity]

    def compact(natural):
        first = natural[..., :8, :]
        second = roll(natural[..., 8:, :], 64, -1)
        low = jnp.broadcast_to(parity == 0, first.shape)
        return jnp.where(low, first, second), jnp.where(low, second, first)

    def expand(even, odd):
        low = jnp.broadcast_to(parity == 0, even.shape)
        return jnp.where(low, even, odd), roll(jnp.where(low, odd, even), 64, -1)

    t_sign = jnp.where(ta == n_ta - 1, f32(0.5), f32(-0.5))

    def unpack_links(colour):
        for mu in range(4):
            mine = compact(gauge_ref[pl.ds(18 * mu, 18)].astype(f32))[colour]
            if mu == 0:
                inside = jnp.logical_not((t_high[colour] == 1) & (t_low == 1))
            elif mu == 1:
                inside = x_pos != 3
            elif mu == 2:
                inside = y_pos % 4 != 3
            else:
                inside = z_pos % 4 != 3
            weight_in = jnp.where(inside, f32(-0.5), f32(0.0))
            weight_out = jnp.where(inside, f32(0.0), t_sign if mu == 0 else f32(-0.5))
            for part in range(2):
                for row in range(3):
                    first = 9 * part + 3 * row
                    link_in[colour, mu, part, :, row] = mine[first : first + 3] * weight_in
                    link_out[colour, mu, part, :, row] = mine[first : first + 3] * weight_out

    def unpack_clover(colour):
        for chi in range(2):
            for col in range(6):
                for part in range(2):
                    base = 72 * part + 36 * chi
                    line = clover_ref[pl.ds(base + 6 * col, 6)].astype(f32)
                    column = jnp.stack(
                        [clover_ref[base + 6 * r + col].astype(f32) for r in range(6)]
                    )
                    if part == 0:
                        sym = 0.5 * (column + line)
                        diag = iota((6, 1, 1), 0) == col
                        sym = sym + jnp.where(diag, f32(4.0 + mass_shift), f32(0.0))
                    else:
                        sym = 0.5 * (column - line)
                    herm[colour, part, chi, col] = compact(sym)[colour]

    loads[0].wait()
    unpack_links(0)
    loads[1].wait()
    unpack_clover(0)
    loads[2].wait()
    pair = compact(source_ref[...])
    for colour in range(2):
        resid[colour] = pair[colour].reshape(2, 4, 3, 8, 128)
    smooth[...] = jnp.zeros_like(smooth)

    square = (128, 128)
    into = iota(square, 0)
    outof = iota(square, 1)
    block_weights = ((into % 16) // 4 == (outof % 16) // 4).astype(f32).astype(jnp.bfloat16)

    def load(ref, colour):
        value = ref[colour]
        return [[value[part, s] for s in range(4)] for part in range(2)]

    def block_wilson(v, colour):
        out = [[None] * 4, [None] * 4]
        for chi in range(2):
            v_re = jnp.concatenate([v[0][2 * chi], v[0][2 * chi + 1]])
            v_im = jnp.concatenate([v[1][2 * chi], v[1][2 * chi + 1]])
            acc_re = acc_im = None
            for col in range(6):
                h_re = herm[colour, 0, chi, col]
                h_im = herm[colour, 1, chi, col]
                term_re = h_re * v_re[col][None] - h_im * v_im[col][None]
                term_im = h_re * v_im[col][None] + h_im * v_re[col][None]
                acc_re = term_re if col == 0 else acc_re + term_re
                acc_im = term_im if col == 0 else acc_im + term_im
            for half in range(2):
                out[0][2 * chi + half] = acc_re[3 * half : 3 * half + 3]
                out[1][2 * chi + half] = acc_im[3 * half : 3 * half + 3]
        low = t_low == 0
        for mu in range(4):
            ahead = project(v, mu, -1)
            behind = link_apply_dagger(link_in, colour, mu, project(v, mu, 1))
            if mu == 0:
                ahead = [
                    roll(jnp.where(low, roll(w, 64, -1), w), 4, -2) for w in ahead
                ]
                behind = [
                    roll(jnp.where(low, w, roll(w, 64, -1)), 4, -2) for w in behind
                ]
            elif mu == 1:
                ahead = [roll(w, -1, -2) for w in ahead]
                behind = [roll(w, 1, -2) for w in behind]
            else:
                step = 16 if mu == 2 else 1
                ahead = [roll(w, -step, -1) for w in ahead]
                behind = [roll(w, step, -1) for w in behind]
            unproject(out, link_apply(link_in, colour, mu, ahead), mu, -1)
            unproject(out, behind, mu, 1)
        return out

    def each(function, *fields):
        return [[function(*(f[part][s] for f in fields)) for s in range(4)] for part in range(2)]

    def site_sum(pairs):
        total = None
        for left, right, sign in pairs:
            for s in range(4):
                term = left[s] * right[s]
                total = term if total is None else signed_add(total, sign, term)
        return total[0] + total[1] + total[2]

    def minimal_residual(colour):
        rho = load(resid, colour)
        image = block_wilson(rho, colour)
        second = block_wilson(image, colour)

        def dot(left, right):
            return [
                site_sum([(left[0], right[0], 1), (left[1], right[1], 1)]),
                site_sum([(left[0], right[1], 1), (left[1], right[0], -1)]),
            ]

        sums = dot(image, rho) + dot(second, rho) + dot(second, image)
        sums = sums + [dot_self(image), dot_self(second)]
        sums = jnp.sum(jnp.stack(sums), axis=1) / block_entries
        sums = split_dot(sums, block_weights)
        pr_re, pr_im, wr_re, wr_im, wp_re, wp_im, pp, ww = [sums[i : i + 1] for i in range(8)]
        inverse = 1.0 / (pp + mean_eps)
        a_re = pr_re * inverse
        a_im = pr_im * inverse
        size = a_re * a_re + a_im * a_im
        s_re = pr_re - a_re * pp - (a_re * wr_re + a_im * wr_im) + size * wp_re
        s_im = pr_im - a_im * pp - (a_re * wr_im - a_im * wr_re) + size * wp_im
        squares = pp - 2.0 * (a_re * wp_re + a_im * wp_im) + size * ww
        inverse = 1.0 / (jnp.maximum(squares, f32(0.0)) + mean_eps)
        b_re = s_re * inverse
        b_im = s_im * inverse
        sum_re = jnp.broadcast_to(a_re + b_re, vreg)
        sum_im = jnp.broadcast_to(a_im + b_im, vreg)
        both_re = jnp.broadcast_to(a_re * b_re - a_im * b_im, vreg)
        both_im = jnp.broadcast_to(a_re * b_im + a_im * b_re, vreg)

        def combine(x, y):
            return [
                [
                    (sum_re * x[0][s] - sum_im * x[1][s])
                    - (both_re * y[0][s] - both_im * y[1][s])
                    for s in range(4)
                ],
                [
                    (sum_re * x[1][s] + sum_im * x[0][s])
                    - (both_re * y[1][s] + both_im * y[0][s])
                    for s in range(4)
                ],
            ]

        return combine(rho, image), lambda: each(jnp.subtract, rho, combine(image, second))

    def dot_self(value):
        return site_sum([(value[0], value[0], 1), (value[1], value[1], 1)])

    def flat(half):
        return jnp.concatenate([half[0].reshape(6, 8, 128), half[1].reshape(6, 8, 128)])

    def pack_x(half, face):
        groups = flat(half).reshape(3, 4, 8, 128)
        packed = None
        for j in range(4):
            moved = roll(groups[:, j], j - face, -2)
            packed = moved if j == 0 else jnp.where(x_pos == j, moved, packed)
        return packed

    def unpack_x(packed, face):
        rows = jnp.stack([roll(packed, face - j, -2) for j in range(4)], axis=1)
        rows = rows.reshape(2, 2, 3, 8, 128)
        return rows[0], rows[1]

    def pack_t(half, face, away):
        groups = flat(half).reshape(3, 4, 8, 128)
        here = (away == 0) if face == 0 else (away == 1)
        first = jnp.where(here, groups[:, 0], roll(groups[:, 1], 64, -1))
        second = jnp.where(here, groups[:, 2], roll(groups[:, 3], 64, -1))
        if face == 0:
            return jnp.where(t_low == 0, first, roll(second, 4, -2))
        return jnp.where(t_low == 1, first, roll(second, 4, -2))

    def unpack_t(packed):
        turned = roll(packed, 64, -1)
        rows = jnp.stack([roll(turned, 4, -2), roll(packed, 4, -2), turned, packed], axis=1)
        rows = rows.reshape(2, 2, 3, 8, 128)
        return rows[0], rows[1]

    def halo_copy(step, side):
        target = device_at(*((-1, 0), (1, 0), (0, -1), (0, 1))[side])
        return pltpu.make_async_remote_copy(
            src_ref=halo_out.at[step, side],
            dst_ref=halo_in.at[step, side],
            send_sem=halo_send.at[step, side],
            recv_sem=halo_recv.at[step, side],
            device_id=target,
            device_id_type=MESH,
        )

    def reduce_start(stage, value):
        dot_out[stage] = value
        for i, peer in enumerate(groups[stage]):
            pltpu.make_async_remote_copy(
                src_ref=dot_out.at[stage],
                dst_ref=dot_in.at[stage_at[stage] + i],
                send_sem=dot_send.at[stage],
                recv_sem=dot_recv.at[stage],
                device_id=peer,
                device_id_type=MESH,
            ).start()

    def reduce_finish(stage):
        count = len(groups[stage])
        arrived = dot_in.at[pl.ds(stage_at[stage], count)]
        pltpu.make_async_remote_copy(
            src_ref=arrived,
            dst_ref=arrived,
            send_sem=dot_send.at[stage],
            recv_sem=dot_recv.at[stage],
            device_id=groups[stage][0],
            device_id_type=MESH,
        ).wait()
        first = stage_at[stage]
        return dot_out[stage] + jnp.sum(dot_in[first : first + count], axis=0)

    stage_at = [0, n_low - 1]

    coarse_lane = iota((16, 128), 1)
    coarse_row = iota((16, 128), 0)
    on_diagonal = (coarse_lane % NVEC) == coarse_row
    def stencil_copy(part, side):
        t_off, x_off = areas[1 + side]
        third = pl.ds(3 * part, 3)
        return pltpu.make_async_remote_copy(
            src_ref=coarse_ref.at[third],
            dst_ref=stencil_in.at[side, third],
            send_sem=stencil_send.at[part, side],
            recv_sem=stencil_recv.at[part, side],
            device_id=device_at(-t_off, -x_off),
            device_id_type=MESH,
        )

    def send_faces(step, colour, z):
        away = jnp.where(colour == 0, t_high[0], t_high[1])
        halo_out[step, 2] = pack_x(project(z, 1, -1), 0)
        halo_copy(step, 2).start()
        halo_out[step, 3] = pack_x(link_apply_dagger(link_out, colour, 1, project(z, 1, 1)), 3)
        halo_copy(step, 3).start()
        halo_out[step, 0] = pack_t(project(z, 0, -1), 0, away)
        halo_copy(step, 0).start()
        halo_out[step, 1] = pack_t(link_apply_dagger(link_out, colour, 0, project(z, 0, 1)), 3, away)
        halo_copy(step, 1).start()

    def solve(step, colour):
        z, remainder = minimal_residual(colour)
        if isinstance(step, int):
            pl.semaphore_wait(barrier, 4)
        send_faces(step, colour, z)
        rho = remainder()
        for part in range(2):
            for s in range(4):
                z_ref[part, s] = z[part][s]
                resid[colour, part, s] = rho[part][s]
                smooth[colour, part, s] = smooth[colour, part, s] + z[part][s]

    def subtract(colour, change):
        for part in range(2):
            for s in range(4):
                resid[colour, part, s] = resid[colour, part, s] - change[part][s]

    def exchange(step, meanwhile, early=None):
        colour = lax.rem(step, 2)
        other = 1 - colour
        z = [[z_ref[part, s] for s in range(4)] for part in range(2)]
        away = jnp.where(colour == 0, t_high[0], t_high[1])
        meanwhile(step)
        change = [[jnp.zeros((3, 8, 128), f32)] * 4 for _ in range(2)]
        for mu in (2, 3):
            ahead = project(z, mu, -1)
            behind = link_apply_dagger(link_out, colour, mu, project(z, mu, 1))
            if mu == 2:
                ahead = [roll(w, -16, -1) for w in ahead]
                behind = [roll(w, 16, -1) for w in behind]
            else:
                ahead = [jnp.where(z_pos == 15, roll(w, 15, -1), roll(w, -1, -1)) for w in ahead]
                behind = [jnp.where(z_pos == 0, roll(w, -15, -1), roll(w, 1, -1)) for w in behind]
            unproject(change, link_apply(link_out, other, mu, ahead), mu, -1)
            unproject(change, behind, mu, 1)
        if early:
            early(change)
            change = [[jnp.zeros((3, 8, 128), f32)] * 4 for _ in range(2)]
        halo_copy(step, 0).wait()
        halo_copy(step, 1).wait()
        ahead = unpack_t(halo_in[step, 0])
        unproject(change, link_apply(link_out, other, 0, ahead), 0, -1)
        first = (away == 1) & (t_low == 0)
        behind = [jnp.where(first, w, f32(0.0)) for w in unpack_t(halo_in[step, 1])]
        unproject(change, behind, 0, 1)
        halo_copy(step, 2).wait()
        halo_copy(step, 3).wait()
        ahead = unpack_x(halo_in[step, 2], 3)
        unproject(change, link_apply(link_out, other, 1, ahead), 1, -1)
        behind = [jnp.where(x_pos == 0, w, f32(0.0)) for w in unpack_x(halo_in[step, 3], 0)]
        unproject(change, behind, 1, 1)
        if early:
            return change
        subtract(other, change)
        return None

    def narrow_null(a, carry):
        even, _ = compact(null_ref[a].astype(f32))
        null_even[a] = even
        return carry

    def background(step):
        for side in range(4):
            stencil_copy(step, side).start()

        @pl.when(step == 0)
        def _():
            unpack_links(1)
            unpack_clover(1)

        @pl.when(step == 1)
        def _():
            loads[4].wait()
            lax.fori_loop(0, NVEC, narrow_null, 0)

    def half_step(step, carry):
        exchange(step, background)
        solve(step + 1, 1 - lax.rem(step, 2))
        return carry

    areas = [(0, 0), (1, 0), (-1, 0), (0, 1), (0, -1)]
    loads[4].start()
    solve(0, 0)
    loads[3].wait()
    lax.fori_loop(0, HALF_STEPS - 1, half_step, 0)

    def restrict_known(change):
        subtract(0, change)
        natural = expand(resid[0].reshape(24, 8, 128), resid[1].reshape(24, 8, 128))

        def restrict(a, carry):
            basis = null_ref[a].astype(f32)
            acc_re = acc_im = None
            for i, half in enumerate(natural):
                b_re = basis[0, :, 8 * i : 8 * i + 8]
                b_im = basis[1, :, 8 * i : 8 * i + 8]
                term_re = jnp.sum(b_re * half[:12] + b_im * half[12:], axis=0)
                term_im = jnp.sum(b_re * half[12:] - b_im * half[:12], axis=0)
                acc_re = term_re if i == 0 else acc_re + term_re
                acc_im = term_im if i == 0 else acc_im + term_im
            partial[0, a] = acc_re
            partial[1, a] = acc_im
            return carry

        lax.fori_loop(0, NVEC, restrict, 0)

    change = exchange(HALF_STEPS - 1, lambda step: None, restrict_known)
    change_re = jnp.concatenate(change[0])
    change_im = jnp.concatenate(change[1])

    def restrict_rest(a, carry):
        b_re = null_even[a, 0]
        b_im = null_even[a, 1]
        rest[0, a] = jnp.sum(b_re * change_re + b_im * change_im, axis=0)
        rest[1, a] = jnp.sum(b_re * change_im - b_im * change_re, axis=0)
        return carry

    lax.fori_loop(0, NVEC, restrict_rest, 0)
    site_agg = 4 * (into // 64) + (into % 16) // 4
    to_agg = (site_agg == outof // NVEC).astype(f32).astype(jnp.bfloat16)
    site_agg = 4 * (outof // 64) + (outof % 16) // 4
    from_agg = (site_agg == into // NVEC).astype(f32).astype(jnp.bfloat16)
    agg_weights = (into // NVEC == outof // NVEC).astype(f32).astype(jnp.bfloat16)
    row_z = (into % 16) // 4
    even_agg = 4 * ((ta + xyz + row_z) % 2) + row_z
    from_even = (even_agg == outof // NVEC).astype(f32).astype(jnp.bfloat16)
    rows = split_dot(jnp.sum(partial[...], axis=2).reshape(32, 128), to_agg)
    rows = rows - split_dot(jnp.sum(rest[...], axis=2).reshape(32, 128), from_even)

    def diagonal_row(both):
        return [
            jnp.sum(
                jnp.where(on_diagonal, both[16 * i : 16 * i + 16], f32(0.0)),
                axis=0,
                keepdims=True,
            )
            for i in range(2)
        ]

    vec = diagonal_row(rows)

    shift = jnp.full(vreg, 1.26, f32)

    row_at = iota(vreg, 0)
    agg_z = (lane % 64) // NVEC
    diag_shift = jnp.where(on_diagonal, jnp.broadcast_to(shift[:1], (16, 128)), f32(0.0))

    def tile(row_re, row_im):
        return jnp.where(
            row_at == 0, jnp.broadcast_to(row_re, vreg), jnp.broadcast_to(row_im, vreg)
        )

    near = [(0, -1), (0, 1), (1, 0), (-1, 0)]
    far = [(0, 2), (0, -2), (1, 1), (1, -1), (-1, 1), (-1, -1), (2, 0), (-2, 0)]
    around = far + near

    def cvec_copy(k, slot):
        t_off, x_off = around[slot]
        return pltpu.make_async_remote_copy(
            src_ref=cvec_out.at[k],
            dst_ref=cvec_in.at[k, slot],
            send_sem=cvec_send.at[k],
            recv_sem=cvec_recv.at[k],
            device_id=device_at(-t_off, -x_off),
            device_id_type=MESH,
        )

    def stencil_of(area, k):
        if area == 0:
            return coarse_ref[k, 0], coarse_ref[k, 1]
        return stencil_in[area - 1, k, 0], stencil_in[area - 1, k, 1]

    def add_term(acc, matrix, vec):
        m_re, m_im = matrix
        v_re, v_im = vec[0:1], vec[1:2]
        now = (m_re * v_re - m_im * v_im, m_re * v_im + m_im * v_re)
        return now if acc is None else (acc[0] + now[0], acc[1] + now[1])

    def local_terms(area, vec):
        m_re, m_im = stencil_of(area, 0)
        acc = add_term(None, (m_re - diag_shift, m_im), vec)
        over = roll(vec, 64, -1)
        p_re, p_im = stencil_of(area, 5)
        q_re, q_im = stencil_of(area, 6)
        acc = add_term(acc, (p_re + q_re, p_im + q_im), over)
        ahead = jnp.where(agg_z == 3, roll(vec, 48, -1), roll(vec, -16, -1))
        behind = jnp.where(agg_z == 0, roll(vec, -48, -1), roll(vec, 16, -1))
        acc = add_term(acc, stencil_of(area, 7), ahead)
        return add_term(acc, stencil_of(area, 8), behind)

    def finish(accs):
        rows = jnp.concatenate([w for acc in accs for w in acc], axis=0)
        rows = split_dot(rows, agg_weights)
        return [tile(*diagonal_row(rows[32 * i : 32 * i + 32])) for i in range(len(accs))]

    vecs = [tile(*vec)]
    for pair_at in range(GCR_ITERS // 2):
        own = vecs[-1]
        cvec_out[pair_at] = own
        copies = [cvec_copy(pair_at, slot) for slot in range(len(around))]
        for copy in copies:
            copy.start()
        accs = [local_terms(0, own)]
        if pair_at == 0:
            for part in range(3):
                for side in range(4):
                    stencil_copy(part, side).wait()
        arrived = cvec_in.at[pair_at]
        pltpu.make_async_remote_copy(
            src_ref=arrived,
            dst_ref=arrived,
            send_sem=cvec_send.at[pair_at],
            recv_sem=cvec_recv.at[pair_at],
            device_id=device_at(*around[0]),
            device_id_type=MESH,
        ).wait()
        have = {(0, 0): own}
        for slot, place in enumerate(around):
            have[place] = cvec_in[pair_at, slot]
        for area in range(1, 5):
            accs.append(local_terms(area, have[areas[area]]))
        for area, (t_off, x_off) in enumerate(areas):
            for side in range(4):
                t_step, x_step = areas[1 + side]
                there = have[(t_off + t_step, x_off + x_step)]
                accs[area] = add_term(accs[area], stencil_of(area, 1 + side), there)
        nexts = finish(accs)
        acc = local_terms(0, nexts[0])
        for side in range(4):
            acc = add_term(acc, stencil_of(0, 1 + side), nexts[1 + side])
        vecs = vecs + [nexts[0]] + finish([acc])

    basis_re = basis_im = jnp.zeros(vreg, f32)
    for k, vec in enumerate(vecs):
        basis_re = jnp.where(row_at == k, jnp.broadcast_to(vec[0:1], vreg), basis_re)
        basis_im = jnp.where(row_at == k, jnp.broadcast_to(vec[1:2], vreg), basis_im)

    gram = jnp.zeros(vreg, f32)
    for k in range(GCR_ITERS + 1):
        k_re = basis_re[k : k + 1]
        k_im = basis_im[k : k + 1]
        dot_re = jnp.sum(basis_re * k_re + basis_im * k_im, axis=1, keepdims=True)
        dot_im = jnp.sum(basis_re * k_im - basis_im * k_re, axis=1, keepdims=True)
        gram = jnp.where(lane == 2 * k, jnp.broadcast_to(dot_re, vreg), gram)
        gram = jnp.where(lane == 2 * k + 1, jnp.broadcast_to(dot_im, vreg), gram)
    reduce_start(0, gram)

    diag_rows = jnp.concatenate(
        [
            jnp.where(on_diagonal, jnp.broadcast_to(vec[part : part + 1], (16, 128)), f32(0.0))
            for vec in vecs[:GCR_ITERS]
            for part in range(2)
        ],
        axis=0,
    )
    spread[...] = split_dot(diag_rows, from_agg).reshape(GCR_ITERS, 2, NVEC, 1, 128)

    def prolong(entry, carry):
        n_re = null_ref[:, 0, entry].astype(f32)
        n_im = null_ref[:, 1, entry].astype(f32)
        for k in range(GCR_ITERS):
            e_re = spread[k, 0]
            e_im = spread[k, 1]
            prolonged[k, entry] = jnp.sum(n_re * e_re - n_im * e_im, axis=0)
            prolonged[k, 12 + entry] = jnp.sum(n_re * e_im + n_im * e_re, axis=0)
        return carry

    lax.fori_loop(0, 12, prolong, 0)
    halves = expand(smooth[0].reshape(24, 8, 128), smooth[1].reshape(24, 8, 128))
    for i, half in enumerate(halves):
        out_ref[:, 8 * i : 8 * i + 8] = half

    reduce_start(1, reduce_finish(0))
    gram = reduce_finish(1)

    columns = []
    for k in range(GCR_ITERS + 1):
        columns.append(
            (
                jnp.broadcast_to(gram[:, 2 * k : 2 * k + 1], vreg),
                jnp.broadcast_to(gram[:, 2 * k + 1 : 2 * k + 2], vreg),
            )
        )

    def scaled(a, x):
        return (a[0] * x[0] - a[1] * x[1], a[0] * x[1] + a[1] * x[0])

    def plus(x, y):
        return (x[0] + y[0], x[1] + y[1])

    def minus(x, y):
        return (x[0] - y[0], x[1] - y[1])

    def inner(pairs):
        terms = [
            term
            for left, image in pairs
            for term in (
                left[0] * image[0] + left[1] * image[1],
                left[0] * image[1] - left[1] * image[0],
            )
        ]
        sums = jnp.sum(jnp.stack(terms), axis=1, keepdims=True)
        sums = [jnp.broadcast_to(sums[i], vreg) for i in range(len(terms))]
        return list(zip(sums[::2], sums[1::2]))

    image_columns = [
        plus(columns[k + 1], (shift * columns[k][0], shift * columns[k][1]))
        for k in range(GCR_ITERS)
    ]
    remain = (jnp.where(row_at == 0, f32(1.0), f32(0.0)), jnp.zeros(vreg, f32))
    answer = (jnp.zeros(vreg, f32), jnp.zeros(vreg, f32))
    past = []
    for iteration in range(GCR_ITERS):
        direction = remain
        image = tuple(roll(w, 1, -2) + shift * w for w in direction)
        dots = None
        for k in range(iteration + 1):
            entry = tuple(jnp.broadcast_to(w[k : k + 1], vreg) for w in remain)
            now = scaled(entry, image_columns[k])
            dots = now if dots is None else plus(dots, now)
        if past:
            margins = inner([(old_image, dots) for _, old_image, _, _ in past])
            for margin, (old_direction, old_image, old_dots, inverse) in zip(margins, past):
                margin = (margin[0] * inverse, margin[1] * inverse)
                image = minus(image, scaled(margin, old_image))
                direction = minus(direction, scaled(margin, old_direction))
                dots = minus(dots, scaled(margin, old_dots))
        squares, along = inner([(image, dots), (remain, dots)])
        inverse = 1.0 / (jnp.maximum(squares[0], f32(0.0)) + mean_eps)
        step = (along[0] * inverse, -(along[1] * inverse))
        answer = plus(answer, scaled(step, direction))
        remain = minus(remain, scaled(step, image))
        past.append((direction, image, dots, inverse))

    error = scaled(answer, (basis_re, basis_im))
    error = [jnp.sum(w, axis=0, keepdims=True) for w in error]
    error_ref[0:1] = error[0]
    error_ref[1:2] = error[1]

    for k in range(GCR_ITERS):
        c_re = answer[0][k : k + 1]
        c_im = answer[1][k : k + 1]
        w_re = prolonged[k, :12]
        w_im = prolonged[k, 12:]
        now_re = c_re * w_re - c_im * w_im
        now_im = c_re * w_im + c_im * w_re
        sum_re = now_re if k == 0 else sum_re + now_re
        sum_im = now_im if k == 0 else sum_im + now_im
    out_ref[:12] = out_ref[:12] + sum_re
    out_ref[12:] = out_ref[12:] + sum_im


def solution(mesh):
    n_ta, n_xyz = mesh.shape["ta"], mesh.shape["xyz"]

    def shards(source, gauge_links, clover_raw, null_vectors, coarse_operator):
        f32 = jnp.float32
        dma = pltpu.SemaphoreType.DMA
        field, error = pl.pallas_call(
            functools.partial(kernel, n_ta, n_xyz),
            out_shape=(
                jax.ShapeDtypeStruct((24, 16, 128), f32),
                jax.ShapeDtypeStruct((2, 128), f32),
            ),
            in_specs=[pl.BlockSpec(memory_space=pltpu.HBM)] * 5,
            out_specs=(pl.BlockSpec(memory_space=pltpu.VMEM),) * 2,
            scratch_shapes=[
                pltpu.VMEM((24, 16, 128), f32),
                pltpu.VMEM((72, 16, 128), jnp.bfloat16),
                pltpu.VMEM((144, 16, 128), jnp.bfloat16),
                pltpu.VMEM((NVEC, 2, 12, 16, 128), jnp.bfloat16),
                pltpu.VMEM((9, 2, NVEC, 128), f32),
                pltpu.VMEM((2, 4, 2, 3, 3, 8, 128), f32),
                pltpu.VMEM((2, 4, 2, 3, 3, 8, 128), f32),
                pltpu.VMEM((2, 2, 2, 6, 6, 8, 128), f32),
                pltpu.VMEM((2, 2, 4, 3, 8, 128), f32),
                pltpu.VMEM((2, 2, 4, 3, 8, 128), f32),
                pltpu.VMEM((2, 4, 3, 8, 128), f32),
                pltpu.VMEM((HALF_STEPS, 4, 3, 8, 128), f32),
                pltpu.VMEM((HALF_STEPS, 4, 3, 8, 128), f32),
                pltpu.VMEM((2, NVEC, 8, 128), f32),
                pltpu.VMEM((2, NVEC, 8, 128), f32),
                pltpu.VMEM((NVEC, 2, 12, 8, 128), f32),
                pltpu.VMEM((GCR_ITERS, 2, NVEC, 1, 128), f32),
                pltpu.VMEM((GCR_ITERS, 24, 16, 128), f32),
                pltpu.VMEM((4, 9, 2, NVEC, 128), f32),
                pltpu.VMEM((GCR_ITERS // 2, 8, 128), f32),
                pltpu.VMEM((GCR_ITERS // 2, 12, 8, 128), f32),
                pltpu.VMEM((2, 8, 128), f32),
                pltpu.VMEM((n_xyz // 2 - 1 + 2 * n_ta - 1, 8, 128), f32),
                dma((5,)),
                dma((HALF_STEPS, 4)),
                dma((HALF_STEPS, 4)),
                dma((3, 4)),
                dma((3, 4)),
                dma((GCR_ITERS // 2,)),
                dma((GCR_ITERS // 2,)),
                dma((2,)),
                dma((2,)),
            ],
            compiler_params=pltpu.CompilerParams(
                collective_id=0, has_side_effects=True, vmem_limit_bytes=40 * 2**20
            ),
        )(
            *(
                pltpu.with_memory_space_constraint(operand, pltpu.HBM)
                for operand in (
                    source.reshape(24, 16, 128),
                    gauge_links.reshape(72, 16, 128),
                    clover_raw.reshape(144, 16, 128),
                    null_vectors.reshape(NVEC, 2, 12, 16, 128),
                    coarse_operator,
                )
            )
        )
        return field.reshape(source.shape), error

    in_specs = (
        P(None, None, None, "ta", "xyz", None),
        P(None, None, None, None, "ta", "xyz", None),
        P(None, None, None, None, "ta", "xyz", None),
        P(None, None, None, None, "ta", "xyz", None),
        P(None, None, None, ("ta", "xyz")),
    )
    out_specs = (P(None, None, None, "ta", "xyz", None), P(None, ("ta", "xyz")))
    return jax.shard_map(shards, mesh=mesh, in_specs=in_specs, out_specs=out_specs, check_vma=False)
```
